256 devices in a mesh: tile: 64 (over y, z, core), view: 4 (over x).
Axes of the slice: x: 4, y: 4, z: 8, core: 2. Of those that a mesh axis runs over, the one named last changes fastest.
Arguments:
- volumes: float32 [64, 4, 4, 512, 512], P('tile', 'view'), may hold values from -6 to 6
- initial_affine: float32 [64, 12], P('tile'), may hold values from -0.5 to 0.5
- slab_start: int32 [64], P('tile'), may hold values from 0 to 448
- margin_rows: int32 [64], P('tile'), may hold values from 16 to 64, as said below
- view_gain: float32 [64, 4], P('tile', 'view'), may hold values from 0.5 to 4
Outputs:
- joined: float32 [64, 4, 512, 512], P('tile', 'view')
- refined: float32 [64, 12], P('tile')
The draws below stay inside these ranges and needn't reach their ends.
Inputs may be any that keep to these rules, and one draw needn't show every extreme that they name: `margin_rows`: some tile has exactly 64 rows.
All inputs are finite; a program needn't handle non-finite values.
Results may differ from the reference program's by a relative error of at most 0.0003.
Values sent between devices are 32-bit elements; how exact they have to be, the bound alone decides.
A program may use at most 64 MiB of HBM per device.

```python
import math
import jax
import jax.numpy as jnp
from jax import lax

PX = 512
PY = 512
PZ = 4
SLAB = 64
ROUNDS = 2
TILES = 64
VIEWS = 4


def draw_margin_rows(key, part):
    key = jax.random.fold_in(key, 11)
    rows = jax.random.randint(key, (TILES,), SLAB // 4, SLAB + 1)
    return rows.at[0].set(SLAB)


def touch_ends(values, stream_key, smallest, high):
    dims = values.shape
    spot = [jax.random.randint(jax.random.fold_in(stream_key, axis), (), 0, dims[axis]) for axis in range(len(dims))]
    values = values.at[tuple(spot)].set(smallest)
    longest = dims.index(max(dims))
    spot[longest] = (spot[longest] + 1) % dims[longest]
    return values.at[tuple(spot)].set(high)


def block_scale(own_key, shape, pieces, least, top_value):
    factor_of, own = 1.0, jax.random.fold_in(own_key, 6)
    for dim, blocks in pieces:
        heights = jnp.exp(jax.random.uniform(jax.random.fold_in(own, dim), (blocks,), jnp.float32, least / len(pieces), top_value / len(pieces)))
        factor_of = factor_of * jnp.repeat(heights, shape[dim] // blocks).reshape([-1 if axis == dim else 1 for axis in range(len(shape))])
    return factor_of


def centred(own_key, dims, scale, most, cuts=(), kind=jnp.bfloat16):
    drawn = scale * jax.random.normal(own_key, dims, jnp.float32)
    if cuts:
        drawn = drawn * block_scale(own_key, dims, cuts, -0.22, 0.18)
    return jnp.clip(drawn, -most, most).astype(kind)


def setup_inputs(seed: int = 0) -> dict:
    streams_of = jax.random.split(jax.random.key(seed), 6)
    volumes = centred(streams_of[0], (TILES, VIEWS, PZ, PY, PX), 1.0, 6.0, ((0, 64), (1, 4)), jnp.float32)
    initial_affine = centred(streams_of[1], (TILES, 12), 0.1, 0.5, ((0, 64),), jnp.float32)
    slab_start = touch_ends(jax.random.randint(streams_of[2], (TILES,), 0, PY - SLAB + 1), jax.random.fold_in(streams_of[2], 1), 0, PY - SLAB).astype(jnp.int32)
    margin_rows = draw_margin_rows(jax.random.fold_in(streams_of[5], 71), 0)
    view_gain = jnp.clip(jnp.exp(math.log(4.0) - 2.0794415 * jax.random.uniform(streams_of[4], (TILES, VIEWS), jnp.float32) ** block_scale(streams_of[4], (TILES, VIEWS), ((0, 64), (1, 4)), -0.2, 0.2)), 0.5, 4.0)
    return dict(volumes=volumes, initial_affine=initial_affine, slab_start=slab_start, margin_rows=margin_rows, view_gain=view_gain)


stiffness_factor = 0.25

def coordinate(count):
    return (jnp.arange(count, dtype=jnp.float32) + 0.5) / count * 2.0 - 1.0

def axis_gradient(array, axis):
    length = array.shape[axis]
    upper = lax.slice_in_dim(array, 2, length, axis=axis)
    lower = lax.slice_in_dim(array, 0, length - 2, axis=axis)
    inner = (upper - lower) * 0.5
    first = lax.slice_in_dim(array, 1, 2, axis=axis) - lax.slice_in_dim(array, 0, 1, axis=axis)
    last = lax.slice_in_dim(array, length - 1, length, axis=axis) - lax.slice_in_dim(array, length - 2, length - 1, axis=axis)
    return jnp.concatenate([first, inner, last], axis=axis)

def all_gradients(array):
    rank = array.ndim
    return [axis_gradient(array, rank - 3), axis_gradient(array, rank - 2), axis_gradient(array, rank - 1)]

def cholesky_solve(factor, right_side):
    middle = []
    for row in range(12):
        value = right_side[..., row]
        for col in range(row):
            value = value - factor[..., row, col] * middle[col]
        middle.append(value / factor[..., row, row])
    result = [None] * 12
    for row in range(11, -1, -1):
        value = middle[row]
        for col in range(row + 1, 12):
            value = value - factor[..., col, row] * result[col]
        result[row] = value / factor[..., row, row]
    return jnp.stack(result, axis=-1)

def normal_terms(near_slab, window, row_mask, row_coord):
    gradients = all_gradients(window)
    depth = coordinate(window.shape[-3])[:, None, None]
    across = coordinate(window.shape[-1])[None, None, :]
    rows = row_coord[None, :, None]
    basis_terms = [depth, rows, across, 1.0]
    jacobian = jnp.stack([grad_part * basis_part * row_mask for grad_part in gradients for basis_part in basis_terms])
    residual = (near_slab - window) * row_mask
    hessian = jnp.einsum('a...,b...->ab', jacobian, jacobian, precision=lax.Precision.HIGHEST)
    moment = jnp.einsum('a...,...->a', jacobian, residual, precision=lax.Precision.HIGHEST)
    return (hessian, moment)

def correct_volume(volume, affine):
    gradients = all_gradients(volume)
    depth = coordinate(volume.shape[-3])[:, None, None]
    rows = coordinate(volume.shape[-2])[None, :, None]
    across = coordinate(volume.shape[-1])[None, None, :]
    matrix = affine.reshape(3, 4)
    corrected = volume
    for axis_index in range(3):
        shift_field = matrix[axis_index, 0] * depth + matrix[axis_index, 1] * rows + matrix[axis_index, 2] * across + matrix[axis_index, 3]
        corrected = corrected + gradients[axis_index] * shift_field
    return corrected

def view_weight(gain, facing, depth_count, across_count):
    depth = coordinate(depth_count)[:, None, None]
    across = coordinate(across_count)[None, None, :]
    return gain * (0.2 + (1.0 + facing * across) / 2.0) * (1.5 + facing * depth)

def reference(volumes, initial_affine, slab_start, margin_rows, view_gain):
    row_coord = coordinate(PY)[PY - SLAB:]

    def tile_normals(tile_index):
        following = jnp.minimum(tile_index + 1, TILES - 1)
        valid = (tile_index + 1 < TILES).astype(jnp.float32)
        own_tile = lax.dynamic_index_in_dim(volumes, tile_index, 0, keepdims=False)
        next_tile = lax.dynamic_index_in_dim(volumes, following, 0, keepdims=False)
        window = lax.dynamic_slice_in_dim(next_tile, slab_start[following].astype(jnp.int32), SLAB, 2) * valid
        near_slab = own_tile[:, :, PY - SLAB:, :]
        row_mask = (jnp.arange(SLAB) < margin_rows[tile_index]).astype(jnp.float32)[None, :, None]
        return normal_terms(near_slab, window, row_mask, row_coord)
    hessian, moment = lax.map(tile_normals, jnp.arange(TILES, dtype=jnp.int32))
    hess_low = jnp.concatenate([jnp.zeros((1, 12, 12), jnp.float32), hessian[:-1]], axis=0)
    moment_low = jnp.concatenate([jnp.zeros((1, 12), jnp.float32), moment[:-1]], axis=0)
    stiffness = stiffness_factor * PZ * SLAB * PX * VIEWS
    system = hessian + hess_low + stiffness * jnp.eye(12, dtype=jnp.float32)
    factor = jnp.linalg.cholesky(system)
    params = initial_affine
    zero_row = jnp.zeros((1, 12), jnp.float32)
    for round_index in range(ROUNDS):
        above = jnp.concatenate([params[1:], zero_row], axis=0)
        below = jnp.concatenate([zero_row, params[:-1]], axis=0)
        right_side = jnp.einsum('tab,tb->ta', hessian, above, precision=lax.Precision.HIGHEST) - moment + jnp.einsum('tab,tb->ta', hess_low, below, precision=lax.Precision.HIGHEST) + moment_low + stiffness * initial_affine
        params = cholesky_solve(factor, right_side)
    refined = params

    def join_tile(tile_index):
        tile_volume = lax.dynamic_index_in_dim(volumes, tile_index, 0, keepdims=False)
        affine = lax.dynamic_index_in_dim(refined, tile_index, 0, keepdims=False)
        gains = lax.dynamic_index_in_dim(view_gain, tile_index, 0, keepdims=False)
        corrected = correct_volume(tile_volume, affine)
        facing = 1.0 - 2.0 * (jnp.arange(VIEWS) % 2).astype(jnp.float32)
        weight = jnp.stack([view_weight(gains[view_index], facing[view_index], PZ, PX) for view_index in range(VIEWS)])
        numerator = jnp.sum(weight * corrected, axis=0)
        denominator = jnp.sum(weight, axis=0)
        return numerator / denominator
    joined = lax.map(join_tile, jnp.arange(TILES, dtype=jnp.int32))
    return (joined, refined)
```

```python
import functools

import jax
import jax.numpy as jnp
from jax import lax
from jax.experimental import pallas as pl
from jax.experimental.pallas import tpu as pltpu
from jax.sharding import PartitionSpec as P

MESH = pl.DeviceIdType.MESH
F32 = jnp.float32
SLAB = 64
HALF_SLAB = 32
SENT_ROWS = 40
STIFFNESS_FACTOR = 0.25
PAD = 8
CHUNK = 64
PAIRS = ((0, 0), (0, 1), (0, 2), (1, 1), (1, 2), (2, 2))
MONOS = ((0, 0), (0, 1), (0, 2), (0, 3), (1, 1), (1, 2), (1, 3), (2, 2), (2, 3), (3, 3))


def iota(shape, dim):
    return lax.broadcasted_iota(jnp.int32, shape, dim)


def coordinate(index, count):
    return (index.astype(F32) + 0.5) * (2.0 / count) - 1.0


def x_gradient(a):
    width = a.shape[-1]
    left = pltpu.roll(a, 1, 1)
    right = pltpu.roll(a, width - 1, 1)
    lane = iota(a.shape, 1)
    inner = (right - left) * 0.5
    return jnp.where(lane == 0, right - a, jnp.where(lane == width - 1, a - left, inner))


def y_gradient(before, a, after):
    top, bottom = iota(a.shape, 0) == 0, iota(a.shape, 0) == 7
    upper = jnp.where(bottom, pltpu.roll(after, 7, 0), pltpu.roll(a, 7, 0))
    lower = jnp.where(top, pltpu.roll(before, 1, 0), pltpu.roll(a, 1, 0))
    return (upper - lower) * 0.5


def z_gradients(p):
    n = len(p)
    inner = [(p[z + 1] - p[z - 1]) * 0.5 for z in range(1, n - 1)]
    return [p[1] - p[0]] + inner + [p[n - 1] - p[n - 2]]


def kernel(
    tiles, views,
    vol, win, aff, margin, gain, out, refined,
    vp, grads, wst, wgrad, wrx, wrx_grad, nrx, mown, mlow, hacc, qacc, cols, buf1, buf2, pcol, xk, snd, rcv, obuf,
    vsem, msem, wsem, nsem, s1, r1, s2, r2, ssem, rsem, osem,
):
    depth, height, width = vol.shape[2:]
    lanes = width // 128
    half = height // 2
    chunks = half // CHUNK
    t = lax.axis_index("tile")
    v = lax.axis_index("view")

    def tile_at(k):
        return lax.rem(t + tiles + k, tiles)

    def view_at(k):
        return lax.rem(v + views + k, views)

    def dev(tile, view):
        return {"tile": tile, "view": view}

    def remote(src, dst, send, recv, device):
        return pltpu.make_async_remote_copy(
            src_ref=src, dst_ref=dst, send_sem=send, recv_sem=recv, device_id=device, device_id_type=MESH
        )

    loads = [pltpu.make_async_copy(vol.at[0, 0, z], vp.at[z, pl.ds(PAD, height)], vsem.at[z]) for z in range(depth)]
    loads.append(pltpu.make_async_copy(win, wst.at[:, pl.ds(PAD, SLAB)], vsem.at[depth]))
    for load in loads:
        load.start()
    barrier = pltpu.get_barrier_semaphore()
    partners = [dev(tile_at(k), v) for k in (-2, -1, 1, 2)] + [dev(t, view_at(k)) for k in range(1, views)]
    for partner in partners:
        pl.semaphore_signal(barrier, inc=1, device_id=partner, device_id_type=MESH)
    mown[...] = jnp.full((8, 128), margin[0], jnp.int32)
    hacc[...] = jnp.zeros_like(hacc)
    qacc[...] = jnp.zeros_like(qacc)
    cols[...] = jnp.zeros_like(cols)
    pl.semaphore_wait(barrier, len(partners))
    send_window = remote(
        win.at[:, pl.ds(0, SENT_ROWS)], wrx.at[:, pl.ds(PAD, SENT_ROWS)], wsem.at[0], wsem.at[1], dev(tile_at(-1), v)
    )
    send_window.start()
    send_margin = remote(mown, mlow, msem.at[0], msem.at[1], dev(tile_at(1), v))
    send_margin.start()
    for load in loads:
        load.wait()
    send_near = remote(
        vp.at[:, pl.ds(PAD + height - HALF_SLAB, HALF_SLAB)], nrx, nsem.at[0], nsem.at[1], dev(tile_at(1), v)
    )
    send_near.start()


    for z in range(depth):
        wst[z, PAD - 1 : PAD, :] = 2.0 * wst[z, PAD : PAD + 1, :] - wst[z, PAD + 1 : PAD + 2, :]
        last = PAD + SLAB - 1
        wst[z, last + 1 : last + 2, :] = 2.0 * wst[z, last : last + 1, :] - wst[z, last - 1 : last, :]
        vp[z, PAD - 1 : PAD, :] = 2.0 * vp[z, PAD : PAD + 1, :] - vp[z, PAD + 1 : PAD + 2, :]
        last = PAD + height - 1
        vp[z, last + 1 : last + 2, :] = 2.0 * vp[z, last : last + 1, :] - vp[z, last - 1 : last, :]

    def gradients_of(src, dst, count):
        def body(r, _):
            r = pl.multiple_of(r * 8, 8)
            planes = [src[z, pl.ds(PAD + r, 8), :] for z in range(depth)]
            for z, g in enumerate(z_gradients(planes)):
                dst[0, z, pl.ds(r, 8), :] = g
            for z in range(depth):
                before, after = src[z, pl.ds(r, 8), :], src[z, pl.ds(2 * PAD + r, 8), :]
                dst[1, z, pl.ds(r, 8), :] = y_gradient(before, planes[z], after)
                dst[2, z, pl.ds(r, 8), :] = x_gradient(planes[z])
            return 0

        lax.fori_loop(0, count // 8, body, 0)

    gradients_of(wst, wgrad, SLAB)

    zc = [(z + 0.5) / depth * 2.0 - 1.0 for z in range(depth)]

    def depth_sum(fields, power):
        return functools.reduce(lambda a, b: a + b, [f * (c**power) if power else f for f, c in zip(fields, zc)])

    sub = iota((8, 128), 0)
    lane8 = iota((8, 128), 1)

    def gradients_at(srcg, r, xs, mask):
        return [[srcg[k, z, pl.ds(r, 8), xs] * mask for z in range(depth)] for k in range(3)]

    def row_coordinate(r):
        return coordinate(sub + (r + height - SLAB), height)

    remote(mown, mlow, msem.at[0], msem.at[1], dev(tile_at(1), v)).wait_recv()
    low_rows = mlow[...]
    own_rows = mown[...]

    def matrix_lanes(xl, _):
        xs = pl.ds(pl.multiple_of(xl * 128, 128), 128)
        xv = coordinate(lane8 + xl * 128, width)

        def body(yb, carry):
            r = pl.multiple_of(yb * 8, 8)
            mask = jnp.where(sub + r < low_rows, 1.0, 0.0).astype(F32)
            g = gradients_at(wgrad, r, xs, mask)
            yv = row_coordinate(r)
            new = []
            for f, (a, b) in enumerate(PAIRS):
                fields = [g[a][z] * g[b][z] for z in range(depth)]
                p0, p1, p2 = (depth_sum(fields, k) for k in range(3))
                yp = yv * p0
                terms = (p2, yv * p1, p1, yv * yp, yp, p0)
                new += [c + term for c, term in zip(carry[6 * f : 6 * f + 6], terms)]
            return tuple(new)

        sums = lax.fori_loop(0, SLAB // 8, body, tuple(jnp.zeros((8, 128), F32) for _ in range(36)))
        for f in range(6):
            zz, zy, zo, yy, yo, oo = sums[6 * f : 6 * f + 6]
            xo = xv * oo
            for m, term in enumerate((zz, zy, xv * zo, zo, yy, xv * yo, yo, xv * xo, xo, oo)):
                hacc[f, m] += term
        return 0

    lax.fori_loop(0, lanes, matrix_lanes, 0)
    for f, (a, b) in enumerate(PAIRS):
        for m, (i, j) in enumerate(MONOS):
            row = jnp.sum(hacc[f, m], axis=0, keepdims=True)
            for p, q in {(4 * a + i, 4 * b + j), (4 * a + j, 4 * b + i), (4 * b + i, 4 * a + j), (4 * b + j, 4 * a + i)}:
                cols[p, q : q + 1, :] = row

    gradients_of(vp, grads, height)

    def moment(part, src, srcg, first, rows, near):
        def lane_block(xl, _):
            xs = pl.ds(pl.multiple_of(xl * 128, 128), 128)
            xv = coordinate(lane8 + xl * 128, width)

            def body(yb, carry):
                r = pl.multiple_of(yb * 8, 8)
                mask = jnp.where(sub + (r + first) < rows, 1.0, 0.0).astype(F32)
                g = gradients_at(srcg, pl.multiple_of(r + first, 8), xs, mask)
                window = [src[z, pl.ds(pl.multiple_of(PAD + first + r, 8), 8), xs] for z in range(depth)]
                residual = [near(z, r, xs) - window[z] for z in range(depth)]
                yv = row_coordinate(r + first)
                new = []
                for k in range(3):
                    fields = [g[k][z] * residual[z] for z in range(depth)]
                    p0, p1 = depth_sum(fields, 0), depth_sum(fields, 1)
                    new += [c + term for c, term in zip(carry[3 * k : 3 * k + 3], (p1, yv * p0, p0))]
                return tuple(new)

            sums = lax.fori_loop(0, HALF_SLAB // 8, body, tuple(jnp.zeros((8, 128), F32) for _ in range(9)))
            for k in range(3):
                zo, yo, oo = sums[3 * k : 3 * k + 3]
                for j, term in enumerate((zo, yo, xv * oo, oo)):
                    qacc[part, 4 * k + j] += term
            return 0

        lax.fori_loop(0, lanes, lane_block, 0)
        for i in range(12):
            cols[12 + part, i : i + 1, :] = jnp.sum(qacc[part, i], axis=0, keepdims=True)

    remote(nrx, nrx, nsem.at[0], nsem.at[1], dev(tile_at(1), v)).wait_recv()
    moment(0, wst, wgrad, HALF_SLAB, low_rows, lambda z, r, xs: nrx[z, pl.ds(r, 8), xs])
    send_window.wait_recv()
    for z in range(depth):
        wrx[z, PAD - 1 : PAD, :] = 2.0 * wrx[z, PAD : PAD + 1, :] - wrx[z, PAD + 1 : PAD + 2, :]
    gradients_of(wrx, wrx_grad, HALF_SLAB)
    moment(1, wrx, wrx_grad, 0, own_rows, lambda z, r, xs: vp[z, pl.ds(PAD + height - SLAB + r, 8), xs])

    row = iota((16, 128), 0)
    lane = iota((16, 128), 1)
    tile_index = row * 0 + t
    has_low = jnp.where(tile_index == 0, 0.0, 1.0).astype(F32)
    has_next = jnp.where(tile_index == tiles - 1, 0.0, 1.0).astype(F32)
    block = jnp.zeros((16, 128), F32)
    for c in range(14):
        total = jnp.sum(cols[c], axis=1, keepdims=True) * (has_next if c == 13 else has_low)
        block = jnp.where(lane == c, total, block)
    buf1[v] = block
    buf1[v, 13:14, :] = jnp.full((1, 128), gain[0, 0], F32)
    shares = [
        remote(buf1.at[v], buf1.at[v], s1.at[k - 1], r1.at[k - 1], dev(t, view_at(k))) for k in range(1, views)
    ]
    for share in shares:
        share.start()
    for k, share in enumerate(shares):
        share.wait_recv()
    total = buf1[0]
    for k in range(1, views):
        total = total + buf1[k]
    buf2[2] = jnp.where(row < 12, total, 0.0)
    buf2[2, 12:13, 0:12] = aff[...]
    passes = [
        remote(buf2.at[2], buf2.at[2 - k], s2.at[i], r2.at[i], dev(tile_at(k), v)) for i, k in enumerate((-2, -1, 1, 2))
    ]
    for passed in passes:
        passed.start()
    for passed in passes:
        passed.wait_recv()

    inside = (row < 12) & (lane < 12)
    blocks = [buf2[k] for k in range(5)]
    below2, below, here, above = [jnp.where(inside, blocks[k + 1], 0.0) for k in range(4)]
    eye = jnp.where((row == lane) & (row < 12), 1.0, 0.0).astype(F32)

    def column(a, k):
        return jnp.broadcast_to(a[:, k : k + 1], (16, 128))

    def lane_sum(a):
        return jnp.broadcast_to(jnp.sum(a, axis=1, keepdims=True), (16, 128))

    def as_row(col):
        return jnp.broadcast_to(jnp.sum(col * eye, axis=0, keepdims=True), (16, 128))

    q = [column(blocks[k + 1], 12) + column(blocks[k], 13) for k in range(4)]
    starts = [jnp.broadcast_to(blocks[k][12:13, :], (16, 128)) for k in range(5)]
    stiff = eye * (STIFFNESS_FACTOR * depth * SLAB * width * views)
    right_up = lane_sum(above * starts[4] + here * starts[2] + stiff * starts[3]) - q[3] + q[2]
    right_down = lane_sum(below * starts[2] + below2 * starts[0] + stiff * starts[1]) - q[1] + q[0]
    right_own = lane_sum(stiff * starts[2]) - q[2] + q[1]
    real = row < 12
    up = jnp.where((lane == 12) & real, right_up, above + here + stiff)
    down = jnp.where((lane == 12) & real, right_down, below + below2 + stiff)
    own = here + below + stiff + pltpu.roll(here, 12, 1) + pltpu.roll(below, 24, 1)
    own = jnp.where((lane == 36) & real, right_own, own)
    systems = [up, down, own]
    for k in range(12):
        for i in range(3):
            a = systems[i]
            col = column(a, k)
            scaled = jnp.broadcast_to(a[k : k + 1, :], (16, 128)) / jnp.broadcast_to(col[k : k + 1, :], (16, 128))
            systems[i] = jnp.where(row == k, scaled, a - col * scaled)
    up, down, own = systems
    first_up, first_down = as_row(column(up, 12)), as_row(column(down, 12))
    mix = pltpu.roll(first_up, 12, 1) + pltpu.roll(first_down, 24, 1) + jnp.where(lane == 36, 1.0, 0.0)
    params = lane_sum(own * mix)
    pcol[...] = params
    refined[...] = as_row(params)[0:1, 0:12]

    def entry(k, j):
        return jnp.broadcast_to(pcol[4 * k + j : 4 * k + j + 1, :], (8, 128))

    facing = 1.0 - 2.0 * lax.rem(v, 2).astype(F32)
    own_gain = gain[0, 0]

    across = coordinate(iota((8, width), 1), width)

    def entry_row(k, j):
        return jnp.concatenate([entry(k, j)] * lanes, axis=1)

    def tables(z, _):
        zf = coordinate(z, depth)
        for k in range(3):
            xk[z, k] = entry_row(k, 0) * zf + entry_row(k, 3) + entry_row(k, 2) * across
        xk[z, 3] = (0.2 + (1.0 + facing * across) * 0.5) * (own_gain * (1.5 + facing * zf))
        return 0

    lax.fori_loop(0, depth, tables, 0)
    slopes = [entry_row(k, 1) for k in range(3)]
    sub_row = iota((8, width), 0)

    def numerator_rows(z, first, dst, dst_first, extra, scale):
        def body(rb, _):
            r = pl.multiple_of(first + rb * 8, 8)
            d = pl.multiple_of(dst_first + rb * 8, 8)
            yv = coordinate(sub_row + r, height)
            value = vp[z, pl.ds(pl.multiple_of(PAD + r, 8), 8), :]
            for k in range(3):
                value = value + grads[k, z, pl.ds(r, 8), :] * (xk[z, k] + slopes[k] * yv)
            value = value * xk[z, 3]
            for stream in extra:
                value = value + rcv[stream, pl.ds(d, 8), :]
            if scale is not None:
                value = value * scale
            dst(d, value)
            return 0

        lax.fori_loop(0, CHUNK // 8, body, 0)

    down_view, up_view, far_view = view_at(-1), view_at(1), view_at(2)

    def hop(stream, c):
        rows = pl.ds(pl.multiple_of(c * CHUNK, CHUNK), CHUNK)
        target = down_view if stream % 2 == 0 else up_view
        return remote(
            snd.at[stream, rows], rcv.at[stream, rows], ssem.at[stream, c], rsem.at[stream, c], dev(t, target)
        )

    def send_chunk(stream, c, plane, upper, extra=()):
        def put(d, value):
            snd[stream, pl.ds(d, 8), :] = value

        c_row = pl.multiple_of(c * CHUNK, CHUNK)
        numerator_rows(plane, (half if upper else 0) + c_row, put, c_row, extra, None)
        hop(stream, c).start()

    def far(c, _):
        send_chunk(0, c, far_view, False)
        send_chunk(1, c, far_view, True)
        return 0

    def near_planes(c, _):
        send_chunk(2, c, down_view, True)
        send_chunk(3, c, up_view, False)
        return 0

    def relay(c, _):
        hop(0, c).wait_recv()
        send_chunk(4, c, down_view, False, (0,))
        hop(1, c).wait_recv()
        send_chunk(5, c, up_view, True, (1,))
        return 0

    lax.fori_loop(0, chunks, far, 0)
    lax.fori_loop(0, chunks, near_planes, 0)
    lax.fori_loop(0, chunks, relay, 0)

    zf = coordinate(v, depth)
    weights = jnp.zeros((8, width), F32)
    for k in range(views):
        s = 1.0 - 2.0 * (k % 2)
        g = jnp.concatenate([jnp.broadcast_to(buf1[k, 13:14, :], (8, 128))] * lanes, axis=1)
        weights = weights + g * (1.5 + s * zf) * (0.2 + (1.0 + s * across) * 0.5)
    inverse = 1.0 / weights

    def write_out(part, c):
        rows = pl.ds(pl.multiple_of(part * half + c * CHUNK, CHUNK), CHUNK)
        return pltpu.make_async_copy(obuf.at[rows], out.at[0, 0, rows], osem.at[part, c])

    def finish(c, _):
        c_row = pl.multiple_of(c * CHUNK, CHUNK)
        for part, streams in ((0, (3, 4)), (1, (2, 5))):
            for stream in streams:
                hop(stream, c).wait_recv()

            def put(d, value, part=part):
                obuf[pl.ds(pl.multiple_of(part * half + d, 8), 8), :] = value

            numerator_rows(v, part * half + c_row, put, c_row, streams, inverse)
            write_out(part, c).start()
        return 0

    lax.fori_loop(0, chunks, finish, 0)

    def drain(c, _):
        for stream in range(6):
            hop(stream, c).wait_send()
        for part in range(2):
            write_out(part, c).wait()
        return 0

    lax.fori_loop(0, chunks, drain, 0)
    send_margin.wait_send()
    send_near.wait_send()
    send_window.wait_send()
    for copy in shares + passes:
        copy.wait_send()


def on_device(tiles, views, volumes, initial_affine, slab_start, margin_rows, view_gain):
    depth, height, width = volumes.shape[2:]
    half = height // 2
    chunks = half // CHUNK
    window = lax.dynamic_slice_in_dim(volumes[0, 0], slab_start[0], SLAB, 1)
    smem = pl.BlockSpec(memory_space=pltpu.SMEM)
    vmem = pl.BlockSpec(memory_space=pltpu.VMEM)
    hbm = pl.BlockSpec(memory_space=pl.ANY)
    dma = pltpu.SemaphoreType.DMA
    return pl.pallas_call(
        functools.partial(kernel, tiles, views),
        out_shape=(jax.ShapeDtypeStruct((1, 1, height, width), F32), jax.ShapeDtypeStruct((1, 12), F32)),
        in_specs=[hbm, hbm, vmem, smem, smem],
        out_specs=(hbm, vmem),
        scratch_shapes=[
            pltpu.VMEM((depth, height + 2 * PAD, width), F32),
            pltpu.VMEM((3, depth, height, width), F32),
            pltpu.VMEM((depth, SLAB + 2 * PAD, width), F32),
            pltpu.VMEM((3, depth, SLAB, width), F32),
            pltpu.VMEM((depth, SENT_ROWS + PAD, width), F32),
            pltpu.VMEM((3, depth, HALF_SLAB, width), F32),
            pltpu.VMEM((depth, HALF_SLAB, width), F32),
            pltpu.VMEM((8, 128), jnp.int32),
            pltpu.VMEM((8, 128), jnp.int32),
            pltpu.VMEM((6, 10, 8, 128), F32),
            pltpu.VMEM((2, 12, 8, 128), F32),
            pltpu.VMEM((14, 16, 128), F32),
            pltpu.VMEM((views, 16, 128), F32),
            pltpu.VMEM((5, 16, 128), F32),
            pltpu.VMEM((16, 128), F32),
            pltpu.VMEM((depth, 4, 8, width), F32),
            pltpu.VMEM((6, half, width), F32),
            pltpu.VMEM((6, half, width), F32),
            pltpu.VMEM((height, width), F32),
            dma((depth + 1,)), dma((2,)), dma((2,)), dma((2,)),
            dma((views - 1,)), dma((views - 1,)), dma((4,)), dma((4,)),
            dma((6, chunks)), dma((6, chunks)), dma((2, chunks)),
        ],
        compiler_params=pltpu.CompilerParams(
            collective_id=0, has_side_effects=True, vmem_limit_bytes=48 * 1024 * 1024
        ),
        name="refine_and_join",
    )(volumes, window, initial_affine, margin_rows, view_gain)


def solution(mesh):
    placed = (
        P("tile", "view", None, None, None),
        P("tile", None),
        P("tile"),
        P("tile"),
        P("tile", "view"),
    )
    return jax.shard_map(
        functools.partial(on_device, mesh.shape["tile"], mesh.shape["view"]),
        mesh=mesh,
        in_specs=placed,
        out_specs=(P("tile", "view", None, None), P("tile", None)),
        check_vma=False,
    )
```

```python
import functools

import jax
import jax.numpy as jnp
from jax import lax
from jax.experimental import pallas as pl
from jax.experimental.pallas import tpu as pltpu
from jax.sharding import PartitionSpec as P

MESH = pl.DeviceIdType.MESH
F32 = jnp.float32
SLAB = 64
HALF_SLAB = 32
SENT_ROWS = 40
STIFFNESS_FACTOR = 0.25
PAD = 8
CHUNK = 32
RAW_CHUNKS = 5
EARLY_CHUNKS = 2
PAIRS = ((0, 0), (0, 1), (0, 2), (1, 1), (1, 2), (2, 2))
MONOS = ((0, 0), (0, 1), (0, 2), (0, 3), (1, 1), (1, 2), (1, 3), (2, 2), (2, 3), (3, 3))


def iota(shape, dim):
    return lax.broadcasted_iota(jnp.int32, shape, dim)


def coordinate(index, count):
    return (index.astype(F32) + 0.5) * (2.0 / count) - 1.0


def x_gradient(a):
    width = a.shape[-1]
    left = pltpu.roll(a, 1, 1)
    right = pltpu.roll(a, width - 1, 1)
    lane = iota(a.shape, 1)
    inner = (right - left) * 0.5
    return jnp.where(lane == 0, right - a, jnp.where(lane == width - 1, a - left, inner))


def y_gradient(before, a, after):
    top, bottom = iota(a.shape, 0) == 0, iota(a.shape, 0) == 7
    upper = jnp.where(bottom, pltpu.roll(after, 7, 0), pltpu.roll(a, 7, 0))
    lower = jnp.where(top, pltpu.roll(before, 1, 0), pltpu.roll(a, 1, 0))
    return (upper - lower) * 0.5


def z_gradients(p):
    n = len(p)
    inner = [(p[z + 1] - p[z - 1]) * 0.5 for z in range(1, n - 1)]
    return [p[1] - p[0]] + inner + [p[n - 1] - p[n - 2]]


def kernel(
    tiles, views,
    vol, win, aff, margin, gain, out, refined,
    vp, grads, wst, wgrad, wrx, wrx_grad, nrx, mown, mlow, start_affine, hacc, qacc, cols, buf1, buf2, pcol, xk, snd, rcv, obuf, rawv, rawg, wraw,
    vsem, msem, wsem, nsem, s1, r1, s2, r2, ssem, rsem, osem, rawsem,
):
    depth, height, width = vol.shape[2:]
    lanes = width // 128
    half = height // 2
    chunks = half // CHUNK
    t = lax.axis_index("tile")
    v = lax.axis_index("view")

    def tile_at(k):
        return lax.rem(t + tiles + k, tiles)

    def view_at(k):
        return lax.rem(v + views + k, views)

    def exists(k):
        return t + k >= 0 if k < 0 else t + k < tiles

    def when_tile(k, action):
        pl.when(exists(k))(action)

    def dev(tile, view):
        return {"tile": tile, "view": view}

    def remote(src, dst, send, recv, device):
        return pltpu.make_async_remote_copy(
            src_ref=src, dst_ref=dst, send_sem=send, recv_sem=recv, device_id=device, device_id_type=MESH
        )

    loads = [pltpu.make_async_copy(vol.at[0, 0, z], vp.at[z, pl.ds(PAD, height)], vsem.at[z]) for z in range(depth)]
    loads.append(pltpu.make_async_copy(win, wst.at[:, pl.ds(PAD, SLAB)], vsem.at[depth]))
    loads.append(pltpu.make_async_copy(aff, start_affine, vsem.at[depth + 1]))
    for load in loads:
        load.start()
    barrier = pltpu.get_barrier_semaphore()
    buf2[...] = jnp.zeros_like(buf2)
    tile_steps = (-2, -1, 1, 2)

    def greet(device):
        pl.semaphore_signal(barrier, inc=1, device_id=device, device_id_type=MESH)

    for k in tile_steps:
        when_tile(k, functools.partial(greet, dev(tile_at(k), v)))
    for k in range(1, views):
        greet(dev(t, view_at(k)))
    mown[...] = jnp.full((8, 128), margin[0], jnp.int32)
    hacc[...] = jnp.zeros_like(hacc)
    qacc[...] = jnp.zeros_like(qacc)
    cols[...] = jnp.zeros_like(cols)
    peers = views - 1
    for k in tile_steps:
        peers = peers + jnp.where(exists(k), 1, 0)
    pl.semaphore_wait(barrier, peers)
    send_window = remote(
        win.at[:, pl.ds(0, SENT_ROWS)], wrx.at[:, pl.ds(PAD, SENT_ROWS)], wsem.at[0], wsem.at[1], dev(tile_at(-1), v)
    )
    when_tile(-1, send_window.start)
    send_margin = remote(mown, mlow, msem.at[0], msem.at[1], dev(tile_at(1), v))
    when_tile(1, send_margin.start)
    for load in loads:
        load.wait()
    send_near = remote(
        vp.at[:, pl.ds(PAD + height - HALF_SLAB, HALF_SLAB)], nrx, nsem.at[0], nsem.at[1], dev(tile_at(1), v)
    )
    when_tile(1, send_near.start)

    for z in range(depth):
        vp[z, PAD - 1 : PAD, :] = 2.0 * vp[z, PAD : PAD + 1, :] - vp[z, PAD + 1 : PAD + 2, :]
        last = PAD + height - 1
        vp[z, last + 1 : last + 2, :] = 2.0 * vp[z, last : last + 1, :] - vp[z, last - 1 : last, :]

    def depth_gradients_of(src, dst, count):
        def body(r, _):
            r = pl.multiple_of(r * 8, 8)
            planes = [src[z, pl.ds(pl.multiple_of(PAD + r, 8), 8), :] for z in range(depth)]
            for z, g in enumerate(z_gradients(planes)):
                dst[0, z, pl.ds(r, 8), :] = g
            return 0

        lax.fori_loop(0, count // 8, body, 0)

    depth_gradients_of(vp, grads, height)

    down_view, up_view, far_view = view_at(-1), view_at(1), view_at(2)
    raws = []
    for part, (first, end) in enumerate(((0, EARLY_CHUNKS * CHUNK), (EARLY_CHUNKS * CHUNK, RAW_CHUNKS * CHUNK))):
        for side, target in ((0, down_view), (1, up_view)):
            begin = first + 2 * PAD if part else first
            size = end + 2 * PAD - begin
            sems = [rawsem.at[k, 4 * part + side] for k in range(2)]
            raws.append(
                remote(
                    vp.at[far_view, pl.ds(side * half + begin, size)], rawv.at[side, pl.ds(begin, size)], *sems, dev(t, target)
                )
            )
            sems = [rawsem.at[k, 4 * part + 2 + side] for k in range(2)]
            rows = pl.ds(side * half + first, end - first)
            raws.append(
                remote(grads.at[0, far_view, rows], rawg.at[side, pl.ds(first, end - first)], *sems, dev(t, target))
            )
    for raw in raws[:4]:
        raw.start()

    for z in range(depth):
        wst[z, PAD - 1 : PAD, :] = 2.0 * wst[z, PAD : PAD + 1, :] - wst[z, PAD + 1 : PAD + 2, :]
        last = PAD + SLAB - 1
        wst[z, last + 1 : last + 2, :] = 2.0 * wst[z, last : last + 1, :] - wst[z, last - 1 : last, :]

    def gradients_of(src, dst, first, end):
        def body(r, _):
            r = pl.multiple_of(r * 8, 8)
            planes = [src[z, pl.ds(PAD + r, 8), :] for z in range(depth)]
            for z in range(depth):
                before, after = src[z, pl.ds(r, 8), :], src[z, pl.ds(2 * PAD + r, 8), :]
                dst[1, z, pl.ds(r, 8), :] = y_gradient(before, planes[z], after)
                dst[2, z, pl.ds(r, 8), :] = x_gradient(planes[z])
            return 0

        lax.fori_loop(first // 8, end // 8, body, 0)

    depth_gradients_of(wst, wgrad, SLAB)
    gradients_of(wst, wgrad, 0, SLAB)

    zc = [(z + 0.5) / depth * 2.0 - 1.0 for z in range(depth)]

    def depth_sum(fields, power):
        return functools.reduce(lambda a, b: a + b, [f * (c**power) if power else f for f, c in zip(fields, zc)])

    sub = iota((8, 128), 0)
    lane8 = iota((8, 128), 1)

    def gradients_at(srcg, r, xs, mask):
        return [[srcg[k, z, pl.ds(r, 8), xs] * mask for z in range(depth)] for k in range(3)]

    def row_coordinate(r):
        return coordinate(sub + (r + height - SLAB), height)

    when_tile(-1, send_margin.wait_recv)
    low_rows = mlow[...]
    own_rows = mown[...]

    def matrix_lanes(xl, _):
        xs = pl.ds(pl.multiple_of(xl * 128, 128), 128)
        xv = coordinate(lane8 + xl * 128, width)

        def body(yb, carry):
            r = pl.multiple_of(yb * 8, 8)
            mask = jnp.where(sub + r < low_rows, 1.0, 0.0).astype(F32)
            g = gradients_at(wgrad, r, xs, mask)
            yv = row_coordinate(r)
            new = []
            for f, (a, b) in enumerate(PAIRS):
                fields = [g[a][z] * g[b][z] for z in range(depth)]
                p0, p1, p2 = (depth_sum(fields, k) for k in range(3))
                yp = yv * p0
                terms = (p2, yv * p1, p1, yv * yp, yp, p0)
                new += [c + term for c, term in zip(carry[6 * f : 6 * f + 6], terms)]
            return tuple(new)

        sums = lax.fori_loop(0, SLAB // 8, body, tuple(jnp.zeros((8, 128), F32) for _ in range(36)))
        for f in range(6):
            zz, zy, zo, yy, yo, oo = sums[6 * f : 6 * f + 6]
            xo = xv * oo
            for m, term in enumerate((zz, zy, xv * zo, zo, yy, xv * yo, yo, xv * xo, xo, oo)):
                hacc[f, m] += term
        return 0

    lax.fori_loop(0, lanes, matrix_lanes, 0)
    for f, (a, b) in enumerate(PAIRS):
        for m, (i, j) in enumerate(MONOS):
            row = jnp.sum(hacc[f, m], axis=0, keepdims=True)
            for p, q in {(4 * a + i, 4 * b + j), (4 * a + j, 4 * b + i), (4 * b + i, 4 * a + j), (4 * b + j, 4 * a + i)}:
                cols[p, q : q + 1, :] = row

    def moment(part, src, srcg, first, rows, near):
        def lane_block(xl, _):
            xs = pl.ds(pl.multiple_of(xl * 128, 128), 128)
            xv = coordinate(lane8 + xl * 128, width)

            def body(yb, carry):
                r = pl.multiple_of(yb * 8, 8)
                mask = jnp.where(sub + (r + first) < rows, 1.0, 0.0).astype(F32)
                g = gradients_at(srcg, pl.multiple_of(r + first, 8), xs, mask)
                window = [src[z, pl.ds(pl.multiple_of(PAD + first + r, 8), 8), xs] for z in range(depth)]
                residual = [near(z, r, xs) - window[z] for z in range(depth)]
                yv = row_coordinate(r + first)
                new = []
                for k in range(3):
                    fields = [g[k][z] * residual[z] for z in range(depth)]
                    p0, p1 = depth_sum(fields, 0), depth_sum(fields, 1)
                    new += [c + term for c, term in zip(carry[3 * k : 3 * k + 3], (p1, yv * p0, p0))]
                return tuple(new)

            sums = lax.fori_loop(0, HALF_SLAB // 8, body, tuple(jnp.zeros((8, 128), F32) for _ in range(9)))
            for k in range(3):
                zo, yo, oo = sums[3 * k : 3 * k + 3]
                for j, term in enumerate((zo, yo, xv * oo, oo)):
                    qacc[part, 4 * k + j] += term
            return 0

        lax.fori_loop(0, lanes, lane_block, 0)
        for i in range(12):
            cols[12 + part, i : i + 1, :] = jnp.sum(qacc[part, i], axis=0, keepdims=True)

    when_tile(-1, send_near.wait_recv)
    moment(0, wst, wgrad, HALF_SLAB, low_rows, lambda z, r, xs: nrx[z, pl.ds(r, 8), xs])
    when_tile(1, send_window.wait_recv)
    for z in range(depth):
        wrx[z, PAD - 1 : PAD, :] = 2.0 * wrx[z, PAD : PAD + 1, :] - wrx[z, PAD + 1 : PAD + 2, :]
    depth_gradients_of(wrx, wrx_grad, HALF_SLAB)
    gradients_of(wrx, wrx_grad, 0, HALF_SLAB)
    moment(1, wrx, wrx_grad, 0, own_rows, lambda z, r, xs: vp[z, pl.ds(PAD + height - SLAB + r, 8), xs])

    row = iota((16, 128), 0)
    lane = iota((16, 128), 1)
    tile_index = row * 0 + t
    has_low, has_next = tile_index > 0, tile_index < tiles - 1
    block = jnp.zeros((16, 128), F32)
    for c in range(14):
        total = jnp.sum(cols[c], axis=1, keepdims=True)
        block = jnp.where((lane == c) & (has_next if c == 13 else has_low), total, block)
    buf1[v] = block
    buf1[v, 13:14, :] = jnp.full((1, 128), gain[0, 0], F32)
    shares = [
        remote(buf1.at[v], buf1.at[v], s1.at[k - 1], r1.at[k - 1], dev(t, view_at(k))) for k in range(1, views)
    ]
    for share in shares:
        share.start()
    gradients_of(vp, grads, 0, half)
    for k, share in enumerate(shares):
        share.wait_recv()
    for raw in raws[4:]:
        raw.start()
    total = buf1[0]
    for k in range(1, views):
        total = total + buf1[k]
    buf2[2] = jnp.where(row < 12, total, 0.0)
    buf2[2, 12:13, 0:12] = start_affine[...]
    passes = [
        remote(buf2.at[2], buf2.at[2 - k], s2.at[i], r2.at[i], dev(tile_at(k), v)) for i, k in enumerate(tile_steps)
    ]
    for k, passed in zip(tile_steps, passes):
        when_tile(k, passed.start)
    gradients_of(vp, grads, half, height)
    for k, passed in zip(tile_steps, passes):
        when_tile(-k, passed.wait_recv)

    inside = (row < 12) & (lane < 12)
    blocks = [buf2[k] for k in range(5)]
    below2, below, here, above = [jnp.where(inside, blocks[k + 1], 0.0) for k in range(4)]
    eye = jnp.where((row == lane) & (row < 12), 1.0, 0.0).astype(F32)

    def column(a, k):
        return jnp.broadcast_to(a[:, k : k + 1], (16, 128))

    def lane_sum(a):
        return jnp.broadcast_to(jnp.sum(a, axis=1, keepdims=True), (16, 128))

    def as_row(col):
        return jnp.broadcast_to(jnp.sum(col * eye, axis=0, keepdims=True), (16, 128))

    q = [column(blocks[k + 1], 12) + column(blocks[k], 13) for k in range(4)]
    starts = [jnp.broadcast_to(blocks[k][12:13, :], (16, 128)) for k in range(5)]
    stiff = eye * (STIFFNESS_FACTOR * depth * SLAB * width * views)
    right_up = lane_sum(above * starts[4] + here * starts[2] + stiff * starts[3]) - q[3] + q[2]
    right_down = lane_sum(below * starts[2] + below2 * starts[0] + stiff * starts[1]) - q[1] + q[0]
    right_own = lane_sum(stiff * starts[2]) - q[2] + q[1]
    real = row < 12
    up = jnp.where((lane == 12) & real, right_up, above + here + stiff)
    down = jnp.where((lane == 12) & real, right_down, below + below2 + stiff)
    own = here + below + stiff + pltpu.roll(here, 12, 1) + pltpu.roll(below, 24, 1)
    own = jnp.where((lane == 36) & real, right_own, own)
    systems = [up, down, own]
    for k in range(12):
        for i in range(3):
            a = systems[i]
            col = column(a, k)
            scaled = jnp.broadcast_to(a[k : k + 1, :], (16, 128)) / jnp.broadcast_to(col[k : k + 1, :], (16, 128))
            systems[i] = jnp.where(row == k, scaled, a - col * scaled)
    up, down, own = systems
    first_up, first_down = as_row(column(up, 12)), as_row(column(down, 12))
    mix = pltpu.roll(first_up, 12, 1) + pltpu.roll(first_down, 24, 1) + jnp.where(lane == 36, 1.0, 0.0)
    params = lane_sum(own * mix)
    pcol[...] = params
    refined[...] = as_row(params)[0:1, 0:12]

    def entry(k, j):
        return jnp.broadcast_to(pcol[4 * k + j : 4 * k + j + 1, :], (8, 128))

    facing = 1.0 - 2.0 * lax.rem(v, 2).astype(F32)
    own_gain = gain[0, 0]

    across = coordinate(iota((8, width), 1), width)

    def entry_row(k, j):
        return jnp.concatenate([entry(k, j)] * lanes, axis=1)

    def tables(z, _):
        zf = coordinate(z, depth)
        for k in range(3):
            xk[z, k] = entry_row(k, 0) * zf + entry_row(k, 3) + entry_row(k, 2) * across
        xk[z, 3] = (0.2 + (1.0 + facing * across) * 0.5) * (own_gain * (1.5 + facing * zf))
        return 0

    lax.fori_loop(0, depth, tables, 0)
    slopes = [entry_row(k, 1) for k in range(3)]
    sub_row = iota((8, width), 0)

    def numerator_rows(z, first, dst, dst_first, extra, scale):
        def body(rb, _):
            r = pl.multiple_of(first + rb * 8, 8)
            d = pl.multiple_of(dst_first + rb * 8, 8)
            yv = coordinate(sub_row + r, height)
            value = vp[z, pl.ds(pl.multiple_of(PAD + r, 8), 8), :]
            for k in range(3):
                value = value + grads[k, z, pl.ds(r, 8), :] * (xk[z, k] + slopes[k] * yv)
            value = value * xk[z, 3]
            for stream in extra:
                value = value + rcv[stream, pl.ds(d, 8), :]
            if scale is not None:
                value = value * scale
            dst(d, value)
            return 0

        lax.fori_loop(0, CHUNK // 8, body, 0)

    def hop(stream, c):
        rows = pl.ds(pl.multiple_of(c * CHUNK, CHUNK), CHUNK)
        target = down_view if stream % 2 == 0 else up_view
        return remote(
            snd.at[stream, rows], rcv.at[stream, rows], ssem.at[stream, c], rsem.at[stream, c], dev(t, target)
        )

    def send_chunk(stream, c, plane, upper, extra=()):
        def put(d, value):
            snd[stream, pl.ds(d, 8), :] = value

        c_row = pl.multiple_of(c * CHUNK, CHUNK)
        numerator_rows(plane, (half if upper else 0) + c_row, put, c_row, extra, None)
        hop(stream, c).start()

    def relay_raw(side, c):
        plane = (down_view, up_view)[side]
        stream = 4 + side
        c_row = pl.multiple_of(c * CHUNK, CHUNK)

        def body(rb, _):
            d = pl.multiple_of(c_row + rb * 8, 8)
            r = pl.multiple_of(side * half + d, 8)
            yv = coordinate(sub_row + r, height)
            shifts = [xk[plane, k] + slopes[k] * yv for k in range(3)]
            value = vp[plane, pl.ds(pl.multiple_of(PAD + r, 8), 8), :]
            for k in range(3):
                value = value + grads[k, plane, pl.ds(r, 8), :] * shifts[k]
            before, here_v, after = [rawv[side, pl.ds(pl.multiple_of(d + k * PAD, 8), 8), :] for k in range(3)]
            other = here_v + rawg[side, pl.ds(d, 8), :] * shifts[0]
            other = other + y_gradient(before, here_v, after) * shifts[1] + x_gradient(here_v) * shifts[2]
            snd[stream, pl.ds(d, 8), :] = value * xk[plane, 3] + other * wraw[side]
            return 0

        lax.fori_loop(0, CHUNK // 8, body, 0)
        hop(stream, c).start()

    for side, plane, source in ((0, down_view, up_view), (1, up_view, down_view)):
        g = jnp.concatenate([jnp.broadcast_to(buf1[source, 13:14, :], (8, 128))] * lanes, axis=1)
        wraw[side] = (0.2 + (1.0 - facing * across) * 0.5) * (g * (1.5 - facing * coordinate(plane, depth)))

    def far(c, _):
        send_chunk(0, c, far_view, False)
        send_chunk(1, c, far_view, True)
        return 0

    def near_planes(c, _):
        send_chunk(2, c, down_view, True)
        send_chunk(3, c, up_view, False)
        return 0

    def relay(c, _):
        hop(0, c).wait_recv()
        send_chunk(4, c, down_view, False, (0,))
        hop(1, c).wait_recv()
        send_chunk(5, c, up_view, True, (1,))
        return 0

    def relay_both(c, _):
        relay_raw(0, c)
        relay_raw(1, c)
        return 0

    lax.fori_loop(RAW_CHUNKS, chunks, far, 0)
    lax.fori_loop(0, chunks, near_planes, 0)
    for raw in raws:
        raw.wait_recv()
    lax.fori_loop(0, RAW_CHUNKS, relay_both, 0)
    lax.fori_loop(RAW_CHUNKS, chunks, relay, 0)

    zf = coordinate(v, depth)
    weights = jnp.zeros((8, width), F32)
    for k in range(views):
        s = 1.0 - 2.0 * (k % 2)
        g = jnp.concatenate([jnp.broadcast_to(buf1[k, 13:14, :], (8, 128))] * lanes, axis=1)
        weights = weights + g * (1.5 + s * zf) * (0.2 + (1.0 + s * across) * 0.5)
    inverse = 1.0 / weights

    def write_out(part, c):
        rows = pl.ds(pl.multiple_of(part * half + c * CHUNK, CHUNK), CHUNK)
        return pltpu.make_async_copy(obuf.at[rows], out.at[0, 0, rows], osem.at[part, c])

    def finish(c, _):
        c_row = pl.multiple_of(c * CHUNK, CHUNK)
        for part, streams in ((0, (3, 4)), (1, (2, 5))):
            for stream in streams:
                hop(stream, c).wait_recv()

            def put(d, value, part=part):
                obuf[pl.ds(pl.multiple_of(part * half + d, 8), 8), :] = value

            numerator_rows(v, part * half + c_row, put, c_row, streams, inverse)
            write_out(part, c).start()
        return 0

    lax.fori_loop(0, chunks, finish, 0)

    def drain(c, _):
        for stream in range(2, 6):
            hop(stream, c).wait_send()
        for part in range(2):
            write_out(part, c).wait()
        return 0

    def drain_far(c, _):
        hop(0, c).wait_send()
        hop(1, c).wait_send()
        return 0

    lax.fori_loop(0, chunks, drain, 0)
    lax.fori_loop(RAW_CHUNKS, chunks, drain_far, 0)
    when_tile(1, send_margin.wait_send)
    when_tile(1, send_near.wait_send)
    when_tile(-1, send_window.wait_send)
    for k, passed in zip(tile_steps, passes):
        when_tile(k, passed.wait_send)
    for copy in shares + raws:
        copy.wait_send()


def on_device(tiles, views, volumes, initial_affine, slab_start, margin_rows, view_gain):
    depth, height, width = volumes.shape[2:]
    half = height // 2
    chunks = half // CHUNK
    window = lax.dynamic_slice_in_dim(volumes[0, 0], slab_start[0], SLAB, 1)
    smem = pl.BlockSpec(memory_space=pltpu.SMEM)
    vmem = pl.BlockSpec(memory_space=pltpu.VMEM)
    anywhere = pl.BlockSpec(memory_space=pl.ANY)
    dma = pltpu.SemaphoreType.DMA
    return pl.pallas_call(
        functools.partial(kernel, tiles, views),
        out_shape=(jax.ShapeDtypeStruct((1, 1, height, width), F32), jax.ShapeDtypeStruct((1, 12), F32)),
        in_specs=[pl.BlockSpec(memory_space=pltpu.HBM), anywhere, pl.BlockSpec(memory_space=pltpu.HBM), smem, smem],
        out_specs=(anywhere, vmem),
        scratch_shapes=[
            pltpu.VMEM((depth, height + 2 * PAD, width), F32),
            pltpu.VMEM((3, depth, height, width), F32),
            pltpu.VMEM((depth, SLAB + 2 * PAD, width), F32),
            pltpu.VMEM((3, depth, SLAB, width), F32),
            pltpu.VMEM((depth, SENT_ROWS + PAD, width), F32),
            pltpu.VMEM((3, depth, HALF_SLAB, width), F32),
            pltpu.VMEM((depth, HALF_SLAB, width), F32),
            pltpu.VMEM((8, 128), jnp.int32),
            pltpu.VMEM((8, 128), jnp.int32),
            pltpu.VMEM((1, 12), F32),
            pltpu.VMEM((6, 10, 8, 128), F32),
            pltpu.VMEM((2, 12, 8, 128), F32),
            pltpu.VMEM((14, 16, 128), F32),
            pltpu.VMEM((views, 16, 128), F32),
            pltpu.VMEM((5, 16, 128), F32),
            pltpu.VMEM((16, 128), F32),
            pltpu.VMEM((depth, 4, 8, width), F32),
            pltpu.VMEM((6, half, width), F32),
            pltpu.VMEM((6, half, width), F32),
            pltpu.VMEM((height, width), F32),
            pltpu.VMEM((2, RAW_CHUNKS * CHUNK + 2 * PAD, width), F32),
            pltpu.VMEM((2, RAW_CHUNKS * CHUNK, width), F32),
            pltpu.VMEM((2, 8, width), F32),
            dma((depth + 2,)), dma((2,)), dma((2,)), dma((2,)),
            dma((views - 1,)), dma((views - 1,)), dma((4,)), dma((4,)),
            dma((6, chunks)), dma((6, chunks)), dma((2, chunks)), dma((2, 8)),
        ],
        compiler_params=pltpu.CompilerParams(
            collective_id=0, has_side_effects=True, vmem_limit_bytes=52 * 1024 * 1024
        ),
        name="refine_and_join",
    )(
        pltpu.with_memory_space_constraint(volumes, pltpu.HBM),
        window,
        pltpu.with_memory_space_constraint(initial_affine, pltpu.HBM),
        margin_rows,
        view_gain,
    )


def solution(mesh):
    placed = (
        P("tile", "view", None, None, None),
        P("tile", None),
        P("tile"),
        P("tile"),
        P("tile", "view"),
    )
    return jax.shard_map(
        functools.partial(on_device, mesh.shape["tile"], mesh.shape["view"]),
        mesh=mesh,
        in_specs=placed,
        out_specs=(P("tile", "view", None, None), P("tile", None)),
        check_vma=False,
    )
```

```python
import functools

import jax
import jax.numpy as jnp
from jax import lax
from jax.experimental import pallas as pl
from jax.experimental.pallas import tpu as pltpu
from jax.sharding import PartitionSpec as P

MESH = pl.DeviceIdType.MESH
F32 = jnp.float32
SLAB = 64
HALF_SLAB = 32
SENT_ROWS = 40
STIFFNESS_FACTOR = 0.25
PAD = 8
CHUNK = 32
RAW_CHUNKS = 5
EARLY_ROWS = 96
PAIRS = ((0, 0), (0, 1), (0, 2), (1, 1), (1, 2), (2, 2))
MONOS = ((0, 0), (0, 1), (0, 2), (0, 3), (1, 1), (1, 2), (1, 3), (2, 2), (2, 3), (3, 3))


def iota(shape, dim):
    return lax.broadcasted_iota(jnp.int32, shape, dim)


def coordinate(index, count):
    return (index.astype(F32) + 0.5) * (2.0 / count) - 1.0


def x_gradient(a):
    width = a.shape[-1]
    left = pltpu.roll(a, 1, 1)
    right = pltpu.roll(a, width - 1, 1)
    lane = iota(a.shape, 1)
    inner = (right - left) * 0.5
    return jnp.where(lane == 0, right - a, jnp.where(lane == width - 1, a - left, inner))


def y_gradient(before, a, after):
    top, bottom = iota(a.shape, 0) == 0, iota(a.shape, 0) == 7
    upper = jnp.where(bottom, pltpu.roll(after, 7, 0), pltpu.roll(a, 7, 0))
    lower = jnp.where(top, pltpu.roll(before, 1, 0), pltpu.roll(a, 1, 0))
    return (upper - lower) * 0.5


def z_gradients(p):
    n = len(p)
    inner = [(p[z + 1] - p[z - 1]) * 0.5 for z in range(1, n - 1)]
    return [p[1] - p[0]] + inner + [p[n - 1] - p[n - 2]]


def kernel(
    tiles, views,
    vol, aff, slab, margin, gain, out, refined,
    vp, grads, wst, wgrad, wrx, wrx_grad, nrx, mown, mlow, start_affine, hacc, qacc, cols, buf1, buf2, pcol, xk, snd, rcv, obuf, rawv, rawg, wraw,
    vsem, msem, wsem, nsem, s1, r1, s2, r2, ssem, rsem, osem, rawsem,
):
    depth, height, width = vol.shape[2:]
    lanes = width // 128
    half = height // 2
    chunks = half // CHUNK
    t = lax.axis_index("tile")
    v = lax.axis_index("view")

    def tile_at(k):
        return lax.rem(t + tiles + k, tiles)

    def view_at(k):
        return lax.rem(v + views + k, views)

    def exists(k):
        return t + k >= 0 if k < 0 else t + k < tiles

    def when_tile(k, action):
        pl.when(exists(k))(action)

    def dev(tile, view):
        return {"tile": tile, "view": view}

    def remote(src, dst, send, recv, device):
        return pltpu.make_async_remote_copy(
            src_ref=src, dst_ref=dst, send_sem=send, recv_sem=recv, device_id=device, device_id_type=MESH
        )

    loads = [pltpu.make_async_copy(vol.at[0, 0, z], vp.at[z, pl.ds(PAD, height)], vsem.at[z]) for z in range(depth)]
    loads.append(pltpu.make_async_copy(aff, start_affine, vsem.at[depth]))
    for load in loads:
        load.start()
    barrier = pltpu.get_barrier_semaphore()
    buf2[...] = jnp.zeros_like(buf2)
    tile_steps = (-2, -1, 1, 2)

    def greet(device):
        pl.semaphore_signal(barrier, inc=1, device_id=device, device_id_type=MESH)

    for k in tile_steps:
        when_tile(k, functools.partial(greet, dev(tile_at(k), v)))
    for k in range(1, views):
        greet(dev(t, view_at(k)))
    mown[...] = jnp.full((8, 128), margin[0], jnp.int32)
    hacc[...] = jnp.zeros_like(hacc)
    qacc[...] = jnp.zeros_like(qacc)
    cols[...] = jnp.zeros_like(cols)
    peers = views - 1
    for k in tile_steps:
        peers = peers + jnp.where(exists(k), 1, 0)
    pl.semaphore_wait(barrier, peers)
    send_margin = remote(mown, mlow, msem.at[0], msem.at[1], dev(tile_at(1), v))
    when_tile(1, send_margin.start)
    send_near = remote(
        vol.at[0, 0, :, pl.ds(height - HALF_SLAB, HALF_SLAB)], nrx, nsem.at[0], nsem.at[1], dev(tile_at(1), v)
    )
    when_tile(1, send_near.start)

    down_view, up_view, far_view = view_at(-1), view_at(1), view_at(2)
    raws = []
    for part, (first, end) in enumerate(((0, EARLY_ROWS), (EARLY_ROWS, RAW_CHUNKS * CHUNK))):
        for side, target in ((0, down_view), (1, up_view)):
            begin = first + PAD if part else first - side * PAD
            source = vol.at[0, 0, far_view, pl.ds(side * half + begin, end + PAD - begin)]
            landing = rawv.at[side, pl.ds(PAD + begin, end + PAD - begin)]
            raws.append(remote(source, landing, rawsem.at[0, 4 * part + side], rawsem.at[1, 4 * part + side], dev(t, target)))
        for side, target in ((0, down_view), (1, up_view)):
            sems = [rawsem.at[k, 4 * part + 2 + side] for k in range(2)]
            rows = pl.ds(side * half + first, end - first)
            raws.append(
                remote(grads.at[0, far_view, rows], rawg.at[side, pl.ds(first, end - first)], *sems, dev(t, target))
            )
    for raw in raws[:2]:
        raw.start()
    for load in loads:
        load.wait()
    start = slab[0]
    aligned = lax.div(start, 8) * 8
    shift = jnp.full((SLAB + 8, width), start - aligned, jnp.int32)
    moves = [(k, lax.bitwise_and(shift, k) != 0) for k in (1, 2, 4)]
    for z in range(depth):
        rows = vp[z, pl.ds(aligned + PAD, SLAB + 8), :]
        for k, moved in moves:
            rows = jnp.where(moved, pltpu.roll(rows, SLAB + 8 - k, 0), rows)
        wst[z, PAD : PAD + SLAB, :] = rows[:SLAB]
    send_window = remote(
        wst.at[:, pl.ds(PAD, SENT_ROWS)], wrx.at[:, pl.ds(PAD, SENT_ROWS)], wsem.at[0], wsem.at[1], dev(tile_at(-1), v)
    )
    when_tile(-1, send_window.start)
    for z in range(depth):
        vp[z, PAD - 1 : PAD, :] = 2.0 * vp[z, PAD : PAD + 1, :] - vp[z, PAD + 1 : PAD + 2, :]
        last = PAD + height - 1
        vp[z, last + 1 : last + 2, :] = 2.0 * vp[z, last : last + 1, :] - vp[z, last - 1 : last, :]

    def depth_gradients_of(src, dst, count):
        def body(r, _):
            r = pl.multiple_of(r * 8, 8)
            planes = [src[z, pl.ds(pl.multiple_of(PAD + r, 8), 8), :] for z in range(depth)]
            for z, g in enumerate(z_gradients(planes)):
                dst[0, z, pl.ds(r, 8), :] = g
            return 0

        lax.fori_loop(0, count // 8, body, 0)

    depth_gradients_of(vp, grads, height)

    for raw in raws[2:4]:
        raw.start()

    for z in range(depth):
        wst[z, PAD - 1 : PAD, :] = 2.0 * wst[z, PAD : PAD + 1, :] - wst[z, PAD + 1 : PAD + 2, :]
        last = PAD + SLAB - 1
        wst[z, last + 1 : last + 2, :] = 2.0 * wst[z, last : last + 1, :] - wst[z, last - 1 : last, :]

    def gradients_of(src, dst, first, end):
        def body(r, _):
            r = pl.multiple_of(r * 8, 8)
            planes = [src[z, pl.ds(PAD + r, 8), :] for z in range(depth)]
            for z in range(depth):
                before, after = src[z, pl.ds(r, 8), :], src[z, pl.ds(2 * PAD + r, 8), :]
                dst[1, z, pl.ds(r, 8), :] = y_gradient(before, planes[z], after)
                dst[2, z, pl.ds(r, 8), :] = x_gradient(planes[z])
            return 0

        lax.fori_loop(first // 8, end // 8, body, 0)

    depth_gradients_of(wst, wgrad, SLAB)
    gradients_of(wst, wgrad, 0, SLAB)

    zc = [(z + 0.5) / depth * 2.0 - 1.0 for z in range(depth)]

    def depth_sum(fields, power):
        return functools.reduce(lambda a, b: a + b, [f * (c**power) if power else f for f, c in zip(fields, zc)])

    sub = iota((8, 128), 0)
    lane8 = iota((8, 128), 1)

    def gradients_at(srcg, r, xs, mask):
        return [[srcg[k, z, pl.ds(r, 8), xs] * mask for z in range(depth)] for k in range(3)]

    def row_coordinate(r):
        return coordinate(sub + (r + height - SLAB), height)

    when_tile(-1, send_margin.wait_recv)
    low_rows = mlow[...]
    own_rows = mown[...]

    def matrix_lanes(xl, _):
        xs = pl.ds(pl.multiple_of(xl * 128, 128), 128)
        xv = coordinate(lane8 + xl * 128, width)

        def body(yb, carry):
            r = pl.multiple_of(yb * 8, 8)
            mask = jnp.where(sub + r < low_rows, 1.0, 0.0).astype(F32)
            g = gradients_at(wgrad, r, xs, mask)
            yv = row_coordinate(r)
            new = []
            for f, (a, b) in enumerate(PAIRS):
                fields = [g[a][z] * g[b][z] for z in range(depth)]
                p0, p1, p2 = (depth_sum(fields, k) for k in range(3))
                yp = yv * p0
                terms = (p2, yv * p1, p1, yv * yp, yp, p0)
                new += [c + term for c, term in zip(carry[6 * f : 6 * f + 6], terms)]
            return tuple(new)

        sums = lax.fori_loop(0, SLAB // 8, body, tuple(jnp.zeros((8, 128), F32) for _ in range(36)))
        for f in range(6):
            zz, zy, zo, yy, yo, oo = sums[6 * f : 6 * f + 6]
            xo = xv * oo
            for m, term in enumerate((zz, zy, xv * zo, zo, yy, xv * yo, yo, xv * xo, xo, oo)):
                hacc[f, m] += term
        return 0

    lax.fori_loop(0, lanes, matrix_lanes, 0)
    for f, (a, b) in enumerate(PAIRS):
        for m, (i, j) in enumerate(MONOS):
            row = jnp.sum(hacc[f, m], axis=0, keepdims=True)
            for p, q in {(4 * a + i, 4 * b + j), (4 * a + j, 4 * b + i), (4 * b + i, 4 * a + j), (4 * b + j, 4 * a + i)}:
                cols[p, q : q + 1, :] = row

    def moment(part, src, srcg, first, rows, near):
        def lane_block(xl, _):
            xs = pl.ds(pl.multiple_of(xl * 128, 128), 128)
            xv = coordinate(lane8 + xl * 128, width)

            def body(yb, carry):
                r = pl.multiple_of(yb * 8, 8)
                mask = jnp.where(sub + (r + first) < rows, 1.0, 0.0).astype(F32)
                g = gradients_at(srcg, pl.multiple_of(r + first, 8), xs, mask)
                window = [src[z, pl.ds(pl.multiple_of(PAD + first + r, 8), 8), xs] for z in range(depth)]
                residual = [near(z, r, xs) - window[z] for z in range(depth)]
                yv = row_coordinate(r + first)
                new = []
                for k in range(3):
                    fields = [g[k][z] * residual[z] for z in range(depth)]
                    p0, p1 = depth_sum(fields, 0), depth_sum(fields, 1)
                    new += [c + term for c, term in zip(carry[3 * k : 3 * k + 3], (p1, yv * p0, p0))]
                return tuple(new)

            sums = lax.fori_loop(0, HALF_SLAB // 8, body, tuple(jnp.zeros((8, 128), F32) for _ in range(9)))
            for k in range(3):
                zo, yo, oo = sums[3 * k : 3 * k + 3]
                for j, term in enumerate((zo, yo, xv * oo, oo)):
                    qacc[part, 4 * k + j] += term
            return 0

        lax.fori_loop(0, lanes, lane_block, 0)
        for i in range(12):
            cols[12 + part, i : i + 1, :] = jnp.sum(qacc[part, i], axis=0, keepdims=True)

    when_tile(-1, send_near.wait_recv)
    moment(0, wst, wgrad, HALF_SLAB, low_rows, lambda z, r, xs: nrx[z, pl.ds(r, 8), xs])
    when_tile(1, send_window.wait_recv)
    for z in range(depth):
        wrx[z, PAD - 1 : PAD, :] = 2.0 * wrx[z, PAD : PAD + 1, :] - wrx[z, PAD + 1 : PAD + 2, :]
    depth_gradients_of(wrx, wrx_grad, HALF_SLAB)
    gradients_of(wrx, wrx_grad, 0, HALF_SLAB)
    moment(1, wrx, wrx_grad, 0, own_rows, lambda z, r, xs: vp[z, pl.ds(PAD + height - SLAB + r, 8), xs])

    row = iota((16, 128), 0)
    lane = iota((16, 128), 1)
    tile_index = row * 0 + t
    has_low, has_next = tile_index > 0, tile_index < tiles - 1
    block = jnp.zeros((16, 128), F32)
    for c in range(14):
        total = jnp.sum(cols[c], axis=1, keepdims=True)
        block = jnp.where((lane == c) & (has_next if c == 13 else has_low), total, block)
    buf1[v] = block
    buf1[v, 13:14, :] = jnp.full((1, 128), gain[0, 0], F32)
    shares = [
        remote(buf1.at[v], buf1.at[v], s1.at[k - 1], r1.at[k - 1], dev(t, view_at(k))) for k in range(1, views)
    ]
    for share in shares:
        share.start()
    gradients_of(vp, grads, 0, half)
    for k, share in enumerate(shares):
        share.wait_recv()
    total = buf1[0]
    for k in range(1, views):
        total = total + buf1[k]
    buf2[2] = jnp.where(row < 12, total, 0.0)
    buf2[2, 12:13, 0:12] = start_affine[...]
    passes = [
        remote(buf2.at[2], buf2.at[2 - k], s2.at[i], r2.at[i], dev(tile_at(k), v)) for i, k in enumerate(tile_steps)
    ]
    for k, passed in zip(tile_steps, passes):
        when_tile(k, passed.start)
    for raw in raws[4:]:
        raw.start()
    gradients_of(vp, grads, half, height)
    across = coordinate(iota((8, width), 1), width)
    facing = 1.0 - 2.0 * lax.rem(v, 2).astype(F32)

    def plane_weights(z, _):
        xk[z, 3] = (0.2 + (1.0 + facing * across) * 0.5) * (gain[0, 0] * (1.5 + facing * coordinate(z, depth)))
        return 0

    lax.fori_loop(0, depth, plane_weights, 0)
    for side, plane, source in ((0, down_view, up_view), (1, up_view, down_view)):
        g = jnp.concatenate([jnp.broadcast_to(buf1[source, 13:14, :], (8, 128))] * lanes, axis=1)
        wraw[side] = (0.2 + (1.0 - facing * across) * 0.5) * (g * (1.5 - facing * coordinate(plane, depth)))

    zf = coordinate(v, depth)
    weights = jnp.zeros((8, width), F32)
    for k in range(views):
        s = 1.0 - 2.0 * (k % 2)
        g = jnp.concatenate([jnp.broadcast_to(buf1[k, 13:14, :], (8, 128))] * lanes, axis=1)
        weights = weights + g * (1.5 + s * zf) * (0.2 + (1.0 + s * across) * 0.5)
    inverse = 1.0 / weights

    for k, passed in zip(tile_steps, passes):
        when_tile(-k, passed.wait_recv)

    inside = (row < 12) & (lane < 12)
    blocks = [buf2[k] for k in range(5)]
    below2, below, here, above = [jnp.where(inside, blocks[k + 1], 0.0) for k in range(4)]
    eye = jnp.where((row == lane) & (row < 12), 1.0, 0.0).astype(F32)

    def column(a, k):
        return jnp.broadcast_to(a[:, k : k + 1], (16, 128))

    def lane_sum(a):
        return jnp.broadcast_to(jnp.sum(a, axis=1, keepdims=True), (16, 128))

    def as_row(col):
        return jnp.broadcast_to(jnp.sum(col * eye, axis=0, keepdims=True), (16, 128))

    q = [column(blocks[k + 1], 12) + column(blocks[k], 13) for k in range(4)]
    starts = [jnp.broadcast_to(blocks[k][12:13, :], (16, 128)) for k in range(5)]
    stiff = eye * (STIFFNESS_FACTOR * depth * SLAB * width * views)
    right_up = lane_sum(above * starts[4] + here * starts[2] + stiff * starts[3]) - q[3] + q[2]
    right_down = lane_sum(below * starts[2] + below2 * starts[0] + stiff * starts[1]) - q[1] + q[0]
    right_own = lane_sum(stiff * starts[2]) - q[2] + q[1]
    real = row < 12
    up = jnp.where((lane == 12) & real, right_up, above + here + stiff)
    down = jnp.where((lane == 12) & real, right_down, below + below2 + stiff)
    own = here + below + stiff + pltpu.roll(here, 12, 1) + pltpu.roll(below, 24, 1)
    own = jnp.where((lane == 36) & real, right_own, own)
    systems = [up, down, own]
    for k in range(12):
        for i in range(3):
            a = systems[i]
            col = column(a, k)
            scaled = jnp.broadcast_to(a[k : k + 1, :] / col[k : k + 1, :], (16, 128))
            systems[i] = jnp.where(row == k, scaled, a - col * scaled)
    up, down, own = systems
    first_up, first_down = as_row(column(up, 12)), as_row(column(down, 12))
    mix = pltpu.roll(first_up, 12, 1) + pltpu.roll(first_down, 24, 1) + jnp.where(lane == 36, 1.0, 0.0)
    params = lane_sum(own * mix)
    pcol[...] = params
    refined[...] = as_row(params)[0:1, 0:12]

    def entry(k, j):
        return jnp.broadcast_to(pcol[4 * k + j : 4 * k + j + 1, :], (8, 128))

    def entry_row(k, j):
        return jnp.concatenate([entry(k, j)] * lanes, axis=1)

    def tables(z, _):
        zf = coordinate(z, depth)
        for k in range(3):
            xk[z, k] = entry_row(k, 0) * zf + entry_row(k, 3) + entry_row(k, 2) * across
        return 0

    lax.fori_loop(0, depth, tables, 0)
    slopes = [entry_row(k, 1) for k in range(3)]
    sub_row = iota((8, width), 0)

    def numerator_rows(z, first, dst, dst_first, extra, scale):
        def body(rb, _):
            r = pl.multiple_of(first + rb * 8, 8)
            d = pl.multiple_of(dst_first + rb * 8, 8)
            yv = coordinate(sub_row + r, height)
            value = vp[z, pl.ds(pl.multiple_of(PAD + r, 8), 8), :]
            for k in range(3):
                value = value + grads[k, z, pl.ds(r, 8), :] * (xk[z, k] + slopes[k] * yv)
            value = value * xk[z, 3]
            for stream in extra:
                value = value + rcv[stream, pl.ds(d, 8), :]
            if scale is not None:
                value = value * scale
            dst(d, value)
            return 0

        lax.fori_loop(0, CHUNK // 8, body, 0)

    def hop(stream, c):
        rows = pl.ds(pl.multiple_of(c * CHUNK, CHUNK), CHUNK)
        target = down_view if stream % 2 == 0 else up_view
        return remote(
            snd.at[stream, rows], rcv.at[stream, rows], ssem.at[stream, c], rsem.at[stream, c], dev(t, target)
        )

    def send_chunk(stream, c, plane, upper, extra=()):
        def put(d, value):
            snd[stream, pl.ds(d, 8), :] = value

        c_row = pl.multiple_of(c * CHUNK, CHUNK)
        numerator_rows(plane, (half if upper else 0) + c_row, put, c_row, extra, None)
        hop(stream, c).start()

    def relay_raw(side, c):
        plane = (down_view, up_view)[side]
        stream = 4 + side
        c_row = pl.multiple_of(c * CHUNK, CHUNK)

        def body(rb, _):
            d = pl.multiple_of(c_row + rb * 8, 8)
            r = pl.multiple_of(side * half + d, 8)
            yv = coordinate(sub_row + r, height)
            shifts = [xk[plane, k] + slopes[k] * yv for k in range(3)]
            value = vp[plane, pl.ds(pl.multiple_of(PAD + r, 8), 8), :]
            for k in range(3):
                value = value + grads[k, plane, pl.ds(r, 8), :] * shifts[k]
            before, here_v, after = [rawv[side, pl.ds(pl.multiple_of(d + k * PAD, 8), 8), :] for k in range(3)]
            other = here_v + rawg[side, pl.ds(d, 8), :] * shifts[0]
            other = other + y_gradient(before, here_v, after) * shifts[1] + x_gradient(here_v) * shifts[2]
            snd[stream, pl.ds(d, 8), :] = value * xk[plane, 3] + other * wraw[side]
            return 0

        lax.fori_loop(0, CHUNK // 8, body, 0)
        hop(stream, c).start()

    def far(c, _):
        send_chunk(0, c, far_view, False)
        send_chunk(1, c, far_view, True)
        return 0

    def near_planes(c, _):
        send_chunk(2, c, down_view, True)
        send_chunk(3, c, up_view, False)
        return 0

    def relay(c, _):
        hop(0, c).wait_recv()
        send_chunk(4, c, down_view, False, (0,))
        hop(1, c).wait_recv()
        send_chunk(5, c, up_view, True, (1,))
        return 0

    def relay_both(c, _):
        relay_raw(0, c)
        relay_raw(1, c)
        return 0

    lax.fori_loop(RAW_CHUNKS, chunks, far, 0)
    lax.fori_loop(0, chunks, near_planes, 0)
    for raw in raws:
        raw.wait_recv()
    rawv[0, PAD - 1 : PAD, :] = 2.0 * rawv[0, PAD : PAD + 1, :] - rawv[0, PAD + 1 : PAD + 2, :]
    lax.fori_loop(0, RAW_CHUNKS, relay_both, 0)
    lax.fori_loop(RAW_CHUNKS, chunks, relay, 0)

    def write_out(part, c):
        rows = pl.ds(pl.multiple_of(part * half + c * CHUNK, CHUNK), CHUNK)
        return pltpu.make_async_copy(obuf.at[rows], out.at[0, 0, rows], osem.at[part, c])

    def finish(c, _):
        c_row = pl.multiple_of(c * CHUNK, CHUNK)
        for part, streams in ((0, (3, 4)), (1, (2, 5))):
            for stream in streams:
                hop(stream, c).wait_recv()

            def put(d, value, part=part):
                obuf[pl.ds(pl.multiple_of(part * half + d, 8), 8), :] = value

            numerator_rows(v, part * half + c_row, put, c_row, streams, inverse)
            write_out(part, c).start()
        return 0

    lax.fori_loop(0, chunks, finish, 0)

    def drain(c, _):
        for stream in range(2, 6):
            hop(stream, c).wait_send()
        for part in range(2):
            write_out(part, c).wait()
        return 0

    def drain_far(c, _):
        hop(0, c).wait_send()
        hop(1, c).wait_send()
        return 0

    lax.fori_loop(0, chunks, drain, 0)
    lax.fori_loop(RAW_CHUNKS, chunks, drain_far, 0)
    when_tile(1, send_margin.wait_send)
    when_tile(1, send_near.wait_send)
    when_tile(-1, send_window.wait_send)
    for k, passed in zip(tile_steps, passes):
        when_tile(k, passed.wait_send)
    for copy in shares + raws:
        copy.wait_send()


def on_device(tiles, views, volumes, initial_affine, slab_start, margin_rows, view_gain):
    depth, height, width = volumes.shape[2:]
    half = height // 2
    chunks = half // CHUNK
    smem = pl.BlockSpec(memory_space=pltpu.SMEM)
    vmem = pl.BlockSpec(memory_space=pltpu.VMEM)
    anywhere = pl.BlockSpec(memory_space=pl.ANY)
    dma = pltpu.SemaphoreType.DMA
    return pl.pallas_call(
        functools.partial(kernel, tiles, views),
        out_shape=(jax.ShapeDtypeStruct((1, 1, height, width), F32), jax.ShapeDtypeStruct((1, 12), F32)),
        in_specs=[pl.BlockSpec(memory_space=pltpu.HBM), pl.BlockSpec(memory_space=pltpu.HBM), smem, smem, smem],
        out_specs=(anywhere, vmem),
        scratch_shapes=[
            pltpu.VMEM((depth, height + 2 * PAD, width), F32),
            pltpu.VMEM((3, depth, height, width), F32),
            pltpu.VMEM((depth, SLAB + 2 * PAD, width), F32),
            pltpu.VMEM((3, depth, SLAB, width), F32),
            pltpu.VMEM((depth, SENT_ROWS + PAD, width), F32),
            pltpu.VMEM((3, depth, HALF_SLAB, width), F32),
            pltpu.VMEM((depth, HALF_SLAB, width), F32),
            pltpu.VMEM((8, 128), jnp.int32),
            pltpu.VMEM((8, 128), jnp.int32),
            pltpu.VMEM((1, 12), F32),
            pltpu.VMEM((6, 10, 8, 128), F32),
            pltpu.VMEM((2, 12, 8, 128), F32),
            pltpu.VMEM((14, 16, 128), F32),
            pltpu.VMEM((views, 16, 128), F32),
            pltpu.VMEM((5, 16, 128), F32),
            pltpu.VMEM((16, 128), F32),
            pltpu.VMEM((depth, 4, 8, width), F32),
            pltpu.VMEM((6, half, width), F32),
            pltpu.VMEM((6, half, width), F32),
            pltpu.VMEM((height, width), F32),
            pltpu.VMEM((2, RAW_CHUNKS * CHUNK + 2 * PAD, width), F32),
            pltpu.VMEM((2, RAW_CHUNKS * CHUNK, width), F32),
            pltpu.VMEM((2, 8, width), F32),
            dma((depth + 1,)), dma((2,)), dma((2,)), dma((2,)),
            dma((views - 1,)), dma((views - 1,)), dma((4,)), dma((4,)),
            dma((6, chunks)), dma((6, chunks)), dma((2, chunks)), dma((2, 8)),
        ],
        compiler_params=pltpu.CompilerParams(
            collective_id=0, has_side_effects=True, vmem_limit_bytes=52 * 1024 * 1024
        ),
        name="refine_and_join",
    )(
        pltpu.with_memory_space_constraint(volumes, pltpu.HBM),
        pltpu.with_memory_space_constraint(initial_affine, pltpu.HBM),
        slab_start,
        margin_rows,
        view_gain,
    )


def solution(mesh):
    placed = (
        P("tile", "view", None, None, None),
        P("tile", None),
        P("tile"),
        P("tile"),
        P("tile", "view"),
    )
    return jax.shard_map(
        functools.partial(on_device, mesh.shape["tile"], mesh.shape["view"]),
        mesh=mesh,
        in_specs=placed,
        out_specs=(P("tile", "view", None, None), P("tile", None)),
        check_vma=False,
    )
```

```python
import functools

import jax
import jax.numpy as jnp
from jax import lax
from jax.experimental import pallas as pl
from jax.experimental.pallas import tpu as pltpu
from jax.sharding import PartitionSpec as P

MESH = pl.DeviceIdType.MESH
F32 = jnp.float32
SLAB = 64
HALF_SLAB = 32
SENT_ROWS = 40
STIFFNESS_FACTOR = 0.25
PAD = 8
CHUNK = 32
RAW_CHUNKS = 5
EARLY_ROWS = 96
PAIRS = ((0, 0), (0, 1), (0, 2), (1, 1), (1, 2), (2, 2))
MONOS = ((0, 0), (0, 1), (0, 2), (0, 3), (1, 1), (1, 2), (1, 3), (2, 2), (2, 3), (3, 3))


def iota(shape, dim):
    return lax.broadcasted_iota(jnp.int32, shape, dim)


def coordinate(index, count):
    return (index.astype(F32) + 0.5) * (2.0 / count) - 1.0


def x_gradient(a):
    width = a.shape[-1]
    left = pltpu.roll(a, 1, 1)
    right = pltpu.roll(a, width - 1, 1)
    lane = iota(a.shape, 1)
    inner = (right - left) * 0.5
    return jnp.where(lane == 0, right - a, jnp.where(lane == width - 1, a - left, inner))


def y_gradient(before, a, after):
    top, bottom = iota(a.shape, 0) == 0, iota(a.shape, 0) == 7
    upper = jnp.where(bottom, pltpu.roll(after, 7, 0), pltpu.roll(a, 7, 0))
    lower = jnp.where(top, pltpu.roll(before, 1, 0), pltpu.roll(a, 1, 0))
    return (upper - lower) * 0.5


def z_gradients(p):
    n = len(p)
    inner = [(p[z + 1] - p[z - 1]) * 0.5 for z in range(1, n - 1)]
    return [p[1] - p[0]] + inner + [p[n - 1] - p[n - 2]]


def kernel(
    tiles, views,
    vol, aff, slab, margin, gain, out, refined,
    vp, grads, wst, wgrad, wrx, wrx_grad, nrx, mown, mlow, start_affine, hacc, qacc, cols, buf1, buf2, pcol, xk, snd, rcv, rawv, rawg, wraw,
    vsem, msem, wsem, nsem, s1, r1, s2, r2, ssem, rsem, rawsem,
):
    depth, height, width = vol.shape[2:]
    lanes = width // 128
    half = height // 2
    chunks = half // CHUNK
    t = lax.axis_index("tile")
    v = lax.axis_index("view")

    def tile_at(k):
        return lax.rem(t + tiles + k, tiles)

    def view_at(k):
        return lax.rem(v + views + k, views)

    def exists(k):
        return t + k >= 0 if k < 0 else t + k < tiles

    def when_tile(k, action):
        pl.when(exists(k))(action)

    def dev(tile, view):
        return {"tile": tile, "view": view}

    def remote(src, dst, send, recv, device):
        return pltpu.make_async_remote_copy(
            src_ref=src, dst_ref=dst, send_sem=send, recv_sem=recv, device_id=device, device_id_type=MESH
        )

    loads = [pltpu.make_async_copy(vol.at[0, 0, z], vp.at[z, pl.ds(PAD, height)], vsem.at[z]) for z in range(depth)]
    loads.append(pltpu.make_async_copy(aff, start_affine, vsem.at[depth]))
    for load in loads:
        load.start()
    barrier = pltpu.get_barrier_semaphore()
    buf2[...] = jnp.zeros_like(buf2)
    tile_steps = (-2, -1, 1, 2)

    def greet(device):
        pl.semaphore_signal(barrier, inc=1, device_id=device, device_id_type=MESH)

    for k in tile_steps:
        when_tile(k, functools.partial(greet, dev(tile_at(k), v)))
    for k in range(1, views):
        greet(dev(t, view_at(k)))
    mown[...] = jnp.full((8, 128), margin[0], jnp.int32)
    hacc[...] = jnp.zeros_like(hacc)
    qacc[...] = jnp.zeros_like(qacc)
    cols[...] = jnp.zeros_like(cols)
    peers = views - 1
    for k in tile_steps:
        peers = peers + jnp.where(exists(k), 1, 0)
    pl.semaphore_wait(barrier, peers)
    send_margin = remote(mown, mlow, msem.at[0], msem.at[1], dev(tile_at(1), v))
    when_tile(1, send_margin.start)
    send_near = remote(
        vol.at[0, 0, :, pl.ds(height - HALF_SLAB, HALF_SLAB)], nrx, nsem.at[0], nsem.at[1], dev(tile_at(1), v)
    )
    when_tile(1, send_near.start)

    down_view, up_view, far_view = view_at(-1), view_at(1), view_at(2)
    raws = []
    for part, (first, end) in enumerate(((0, EARLY_ROWS), (EARLY_ROWS, RAW_CHUNKS * CHUNK))):
        for side, target in ((0, down_view), (1, up_view)):
            begin = first + PAD if part else first - side * PAD
            source = vol.at[0, 0, far_view, pl.ds(side * half + begin, end + PAD - begin)]
            landing = rawv.at[side, pl.ds(PAD + begin, end + PAD - begin)]
            raws.append(remote(source, landing, rawsem.at[0, 4 * part + side], rawsem.at[1, 4 * part + side], dev(t, target)))
        for side, target in ((0, down_view), (1, up_view)):
            sems = [rawsem.at[k, 4 * part + 2 + side] for k in range(2)]
            rows = pl.ds(side * half + first, end - first)
            raws.append(
                remote(grads.at[0, far_view, rows], rawg.at[side, pl.ds(first, end - first)], *sems, dev(t, target))
            )
    for raw in raws[:2]:
        raw.start()
    start = slab[0]
    aligned = lax.div(start, 8) * 8
    shift = jnp.full((SLAB + 8, width), start - aligned, jnp.int32)
    moves = [(k, lax.bitwise_and(shift, k) != 0) for k in (1, 2, 4)]
    for load in loads:
        load.wait()
    send_windows = []
    for z in range(depth):
        rows = vp[z, pl.ds(aligned + PAD, SLAB + 8), :]
        for k, moved in moves:
            rows = jnp.where(moved, pltpu.roll(rows, SLAB + 8 - k, 0), rows)
        wst[z, PAD : PAD + SLAB, :] = rows[:SLAB]
        sent = pl.ds(PAD, SENT_ROWS)
        send_windows.append(
            remote(wst.at[z, sent], wrx.at[z, sent], wsem.at[0, z], wsem.at[1, z], dev(tile_at(-1), v))
        )
        when_tile(-1, send_windows[z].start)
    for z in range(depth):
        vp[z, PAD - 1 : PAD, :] = 2.0 * vp[z, PAD : PAD + 1, :] - vp[z, PAD + 1 : PAD + 2, :]
        last = PAD + height - 1
        vp[z, last + 1 : last + 2, :] = 2.0 * vp[z, last : last + 1, :] - vp[z, last - 1 : last, :]

    def depth_gradients_of(src, dst, count):
        def body(r, _):
            r = pl.multiple_of(r * 8, 8)
            planes = [src[z, pl.ds(pl.multiple_of(PAD + r, 8), 8), :] for z in range(depth)]
            for z, g in enumerate(z_gradients(planes)):
                dst[0, z, pl.ds(r, 8), :] = g
            return 0

        lax.fori_loop(0, count // 8, body, 0)

    depth_gradients_of(vp, grads, height)

    for raw in raws[2:4]:
        raw.start()

    for z in range(depth):
        wst[z, PAD - 1 : PAD, :] = 2.0 * wst[z, PAD : PAD + 1, :] - wst[z, PAD + 1 : PAD + 2, :]
        last = PAD + SLAB - 1
        wst[z, last + 1 : last + 2, :] = 2.0 * wst[z, last : last + 1, :] - wst[z, last - 1 : last, :]

    def gradients_of(src, dst, first, end):
        def body(r, _):
            r = pl.multiple_of(r * 8, 8)
            planes = [src[z, pl.ds(PAD + r, 8), :] for z in range(depth)]
            for z in range(depth):
                before, after = src[z, pl.ds(r, 8), :], src[z, pl.ds(2 * PAD + r, 8), :]
                dst[1, z, pl.ds(r, 8), :] = y_gradient(before, planes[z], after)
                dst[2, z, pl.ds(r, 8), :] = x_gradient(planes[z])
            return 0

        lax.fori_loop(first // 8, end // 8, body, 0)

    depth_gradients_of(wst, wgrad, SLAB)
    gradients_of(wst, wgrad, 0, SLAB)

    zc = [(z + 0.5) / depth * 2.0 - 1.0 for z in range(depth)]

    def depth_sum(fields, power):
        return functools.reduce(lambda a, b: a + b, [f * (c**power) if power else f for f, c in zip(fields, zc)])

    sub = iota((8, 128), 0)
    lane8 = iota((8, 128), 1)

    def gradients_at(srcg, r, xs, mask):
        return [[srcg[k, z, pl.ds(r, 8), xs] * mask for z in range(depth)] for k in range(3)]

    def row_coordinate(r):
        return coordinate(sub + (r + height - SLAB), height)

    when_tile(-1, send_margin.wait_recv)
    low_rows = mlow[...]
    own_rows = mown[...]

    def matrix_lanes(xl, _):
        xs = pl.ds(pl.multiple_of(xl * 128, 128), 128)
        xv = coordinate(lane8 + xl * 128, width)

        def body(yb, carry):
            r = pl.multiple_of(yb * 8, 8)
            mask = jnp.where(sub + r < low_rows, 1.0, 0.0).astype(F32)
            g = gradients_at(wgrad, r, xs, mask)
            yv = row_coordinate(r)
            new = []
            for f, (a, b) in enumerate(PAIRS):
                fields = [g[a][z] * g[b][z] for z in range(depth)]
                p0, p1, p2 = (depth_sum(fields, k) for k in range(3))
                yp = yv * p0
                terms = (p2, yv * p1, p1, yv * yp, yp, p0)
                new += [c + term for c, term in zip(carry[6 * f : 6 * f + 6], terms)]
            return tuple(new)

        sums = lax.fori_loop(0, SLAB // 8, body, tuple(jnp.zeros((8, 128), F32) for _ in range(36)))
        for f in range(6):
            zz, zy, zo, yy, yo, oo = sums[6 * f : 6 * f + 6]
            xo = xv * oo
            for m, term in enumerate((zz, zy, xv * zo, zo, yy, xv * yo, yo, xv * xo, xo, oo)):
                hacc[f, m] += term
        return 0

    lax.fori_loop(0, lanes, matrix_lanes, 0)
    for f, (a, b) in enumerate(PAIRS):
        for m, (i, j) in enumerate(MONOS):
            row = jnp.sum(hacc[f, m], axis=0, keepdims=True)
            for p, q in {(4 * a + i, 4 * b + j), (4 * a + j, 4 * b + i), (4 * b + i, 4 * a + j), (4 * b + j, 4 * a + i)}:
                cols[p, q : q + 1, :] = row

    def moment(part, src, srcg, first, rows, near):
        def lane_block(xl, _):
            xs = pl.ds(pl.multiple_of(xl * 128, 128), 128)
            xv = coordinate(lane8 + xl * 128, width)

            def body(yb, carry):
                r = pl.multiple_of(yb * 8, 8)
                mask = jnp.where(sub + (r + first) < rows, 1.0, 0.0).astype(F32)
                g = gradients_at(srcg, pl.multiple_of(r + first, 8), xs, mask)
                window = [src[z, pl.ds(pl.multiple_of(PAD + first + r, 8), 8), xs] for z in range(depth)]
                residual = [near(z, r, xs) - window[z] for z in range(depth)]
                yv = row_coordinate(r + first)
                new = []
                for k in range(3):
                    fields = [g[k][z] * residual[z] for z in range(depth)]
                    p0, p1 = depth_sum(fields, 0), depth_sum(fields, 1)
                    new += [c + term for c, term in zip(carry[3 * k : 3 * k + 3], (p1, yv * p0, p0))]
                return tuple(new)

            sums = lax.fori_loop(0, HALF_SLAB // 8, body, tuple(jnp.zeros((8, 128), F32) for _ in range(9)))
            for k in range(3):
                zo, yo, oo = sums[3 * k : 3 * k + 3]
                for j, term in enumerate((zo, yo, xv * oo, oo)):
                    qacc[part, 4 * k + j] += term
            return 0

        lax.fori_loop(0, lanes, lane_block, 0)
        for i in range(12):
            cols[12 + part, i : i + 1, :] = jnp.sum(qacc[part, i], axis=0, keepdims=True)

    row = iota((16, 128), 0)
    lane = iota((16, 128), 1)
    tile_index = row * 0 + t
    has_low, has_next = tile_index > 0, tile_index < tiles - 1
    block = jnp.zeros((16, 128), F32)

    def placed(block, c):
        total = jnp.sum(cols[c], axis=1, keepdims=True)
        return jnp.where((lane == c) & (has_next if c == 13 else has_low), total, block)

    for c in range(12):
        block = placed(block, c)
    when_tile(-1, send_near.wait_recv)
    moment(0, wst, wgrad, HALF_SLAB, low_rows, lambda z, r, xs: nrx[z, pl.ds(r, 8), xs])
    for send_window in send_windows:
        when_tile(1, send_window.wait_recv)
    for z in range(depth):
        wrx[z, PAD - 1 : PAD, :] = 2.0 * wrx[z, PAD : PAD + 1, :] - wrx[z, PAD + 1 : PAD + 2, :]
    depth_gradients_of(wrx, wrx_grad, HALF_SLAB)
    gradients_of(wrx, wrx_grad, 0, HALF_SLAB)
    moment(1, wrx, wrx_grad, 0, own_rows, lambda z, r, xs: vp[z, pl.ds(PAD + height - SLAB + r, 8), xs])

    block = placed(block, 12)
    block = placed(block, 13)
    buf1[v] = block
    buf1[v, 13:14, :] = jnp.full((1, 128), gain[0, 0], F32)
    shares = [
        remote(buf1.at[v], buf1.at[v], s1.at[k - 1], r1.at[k - 1], dev(t, view_at(k))) for k in range(1, views)
    ]
    for share in shares:
        share.start()
    gradients_of(vp, grads, 0, half)
    for k, share in enumerate(shares):
        share.wait_recv()
    total = buf1[0]
    for k in range(1, views):
        total = total + buf1[k]
    buf2[2] = jnp.where(row < 12, total, 0.0)
    buf2[2, 12:13, 0:12] = start_affine[...]
    passes = [
        remote(buf2.at[2], buf2.at[2 - k], s2.at[i], r2.at[i], dev(tile_at(k), v)) for i, k in enumerate(tile_steps)
    ]
    for k, passed in zip(tile_steps, passes):
        when_tile(k, passed.start)
    for raw in raws[4:]:
        raw.start()
    gradients_of(vp, grads, half, height)
    across = coordinate(iota((8, width), 1), width)
    facing = 1.0 - 2.0 * lax.rem(v, 2).astype(F32)

    def plane_weights(z, _):
        xk[z, 3] = (0.2 + (1.0 + facing * across) * 0.5) * (gain[0, 0] * (1.5 + facing * coordinate(z, depth)))
        return 0

    lax.fori_loop(0, depth, plane_weights, 0)
    for side, plane, source in ((0, down_view, up_view), (1, up_view, down_view)):
        g = jnp.concatenate([jnp.broadcast_to(buf1[source, 13:14, :], (8, 128))] * lanes, axis=1)
        wraw[side] = (0.2 + (1.0 - facing * across) * 0.5) * (g * (1.5 - facing * coordinate(plane, depth)))

    zf = coordinate(v, depth)
    weights = jnp.zeros((8, width), F32)
    for k in range(views):
        s = 1.0 - 2.0 * (k % 2)
        g = jnp.concatenate([jnp.broadcast_to(buf1[k, 13:14, :], (8, 128))] * lanes, axis=1)
        weights = weights + g * (1.5 + s * zf) * (0.2 + (1.0 + s * across) * 0.5)
    inverse = 1.0 / weights

    for k, passed in zip(tile_steps, passes):
        when_tile(-k, passed.wait_recv)

    inside = (row < 12) & (lane < 12)
    blocks = [buf2[k] for k in range(5)]
    below2, below, here, above = [jnp.where(inside, blocks[k + 1], 0.0) for k in range(4)]
    eye = jnp.where((row == lane) & (row < 12), 1.0, 0.0).astype(F32)

    def column(a, k):
        return jnp.broadcast_to(a[:, k : k + 1], (16, 128))

    def lane_sum(a):
        return jnp.broadcast_to(jnp.sum(a, axis=1, keepdims=True), (16, 128))

    def as_row(col):
        return jnp.broadcast_to(jnp.sum(col * eye, axis=0, keepdims=True), (16, 128))

    q = [column(blocks[k + 1], 12) + column(blocks[k], 13) for k in range(4)]
    starts = [jnp.broadcast_to(blocks[k][12:13, :], (16, 128)) for k in range(5)]
    stiff = eye * (STIFFNESS_FACTOR * depth * SLAB * width * views)
    right_up = lane_sum(above * starts[4] + here * starts[2] + stiff * starts[3]) - q[3] + q[2]
    right_down = lane_sum(below * starts[2] + below2 * starts[0] + stiff * starts[1]) - q[1] + q[0]
    right_own = lane_sum(stiff * starts[2]) - q[2] + q[1]
    real = row < 12
    up = jnp.where((lane == 12) & real, right_up, above + here + stiff)
    down = jnp.where((lane == 12) & real, right_down, below + below2 + stiff)
    own = here + below + stiff + pltpu.roll(here, 12, 1) + pltpu.roll(below, 24, 1)
    own = jnp.where((lane == 36) & real, right_own, own)
    systems = [up, down, own]
    for k in range(12):
        for i in range(3):
            a = systems[i]
            col = column(a, k)
            scaled = jnp.broadcast_to(a[k : k + 1, :] / col[k : k + 1, :], (16, 128))
            systems[i] = jnp.where(row == k, scaled, a - col * scaled)
    up, down, own = systems
    first_up, first_down = as_row(column(up, 12)), as_row(column(down, 12))
    mix = pltpu.roll(first_up, 12, 1) + pltpu.roll(first_down, 24, 1) + jnp.where(lane == 36, 1.0, 0.0)
    params = lane_sum(own * mix)
    pcol[...] = params
    refined[...] = as_row(params)[0:1, 0:12]

    def entry(k, j):
        return jnp.broadcast_to(pcol[4 * k + j : 4 * k + j + 1, :], (8, 128))

    def entry_row(k, j):
        return jnp.concatenate([entry(k, j)] * lanes, axis=1)

    def tables(z, _):
        zf = coordinate(z, depth)
        for k in range(3):
            xk[z, k] = entry_row(k, 0) * zf + entry_row(k, 3) + entry_row(k, 2) * across
        return 0

    lax.fori_loop(0, depth, tables, 0)
    slopes = [entry_row(k, 1) for k in range(3)]
    sub_row = iota((8, width), 0)

    def numerator_rows(z, first, dst, dst_first, extra, scale):
        def body(rb, _):
            r = pl.multiple_of(first + rb * 8, 8)
            d = pl.multiple_of(dst_first + rb * 8, 8)
            yv = coordinate(sub_row + r, height)
            value = vp[z, pl.ds(pl.multiple_of(PAD + r, 8), 8), :]
            for k in range(3):
                value = value + grads[k, z, pl.ds(r, 8), :] * (xk[z, k] + slopes[k] * yv)
            value = value * xk[z, 3]
            for stream in extra:
                value = value + rcv[stream, pl.ds(d, 8), :]
            if scale is not None:
                value = value * scale
            dst(d, value)
            return 0

        lax.fori_loop(0, CHUNK // 8, body, 0)

    def hop(stream, c):
        rows = pl.ds(pl.multiple_of(c * CHUNK, CHUNK), CHUNK)
        target = down_view if stream % 2 == 0 else up_view
        return remote(
            snd.at[stream, rows], rcv.at[stream, rows], ssem.at[stream, c], rsem.at[stream, c], dev(t, target)
        )

    def send_chunk(stream, c, plane, upper, extra=()):
        def put(d, value):
            snd[stream, pl.ds(d, 8), :] = value

        c_row = pl.multiple_of(c * CHUNK, CHUNK)
        numerator_rows(plane, (half if upper else 0) + c_row, put, c_row, extra, None)
        hop(stream, c).start()

    def relay_raw(side, c):
        plane = (down_view, up_view)[side]
        stream = 4 + side
        c_row = pl.multiple_of(c * CHUNK, CHUNK)

        def body(rb, _):
            d = pl.multiple_of(c_row + rb * 8, 8)
            r = pl.multiple_of(side * half + d, 8)
            yv = coordinate(sub_row + r, height)
            shifts = [xk[plane, k] + slopes[k] * yv for k in range(3)]
            value = vp[plane, pl.ds(pl.multiple_of(PAD + r, 8), 8), :]
            for k in range(3):
                value = value + grads[k, plane, pl.ds(r, 8), :] * shifts[k]
            before, here_v, after = [rawv[side, pl.ds(pl.multiple_of(d + k * PAD, 8), 8), :] for k in range(3)]
            other = here_v + rawg[side, pl.ds(d, 8), :] * shifts[0]
            other = other + y_gradient(before, here_v, after) * shifts[1] + x_gradient(here_v) * shifts[2]
            snd[stream, pl.ds(d, 8), :] = value * xk[plane, 3] + other * wraw[side]
            return 0

        lax.fori_loop(0, CHUNK // 8, body, 0)
        hop(stream, c).start()

    def far(c, _):
        send_chunk(0, c, far_view, False)
        send_chunk(1, c, far_view, True)
        return 0

    def near_planes(c, _):
        send_chunk(2, c, down_view, True)
        send_chunk(3, c, up_view, False)
        return 0

    def relay(c, _):
        hop(0, c).wait_recv()
        send_chunk(4, c, down_view, False, (0,))
        hop(1, c).wait_recv()
        send_chunk(5, c, up_view, True, (1,))
        return 0

    def relay_both(c, _):
        relay_raw(0, c)
        relay_raw(1, c)
        return 0

    lax.fori_loop(RAW_CHUNKS, chunks, far, 0)
    lax.fori_loop(0, chunks, near_planes, 0)
    for raw in raws:
        raw.wait_recv()
    rawv[0, PAD - 1 : PAD, :] = 2.0 * rawv[0, PAD : PAD + 1, :] - rawv[0, PAD + 1 : PAD + 2, :]
    lax.fori_loop(0, RAW_CHUNKS, relay_both, 0)
    lax.fori_loop(RAW_CHUNKS, chunks, relay, 0)

    def finish(c, _):
        c_row = pl.multiple_of(c * CHUNK, CHUNK)
        for part, streams in ((0, (3, 4)), (1, (2, 5))):
            for stream in streams:
                hop(stream, c).wait_recv()

            def put(d, value, part=part):
                out[0, 0, pl.ds(pl.multiple_of(part * half + d, 8), 8), :] = value

            numerator_rows(v, part * half + c_row, put, c_row, streams, inverse)
        return 0

    lax.fori_loop(0, chunks, finish, 0)

    def drain(c, _):
        for stream in range(2, 6):
            hop(stream, c).wait_send()
        return 0

    def drain_far(c, _):
        hop(0, c).wait_send()
        hop(1, c).wait_send()
        return 0

    lax.fori_loop(0, chunks, drain, 0)
    lax.fori_loop(RAW_CHUNKS, chunks, drain_far, 0)
    when_tile(1, send_margin.wait_send)
    when_tile(1, send_near.wait_send)
    for send_window in send_windows:
        when_tile(-1, send_window.wait_send)
    for k, passed in zip(tile_steps, passes):
        when_tile(k, passed.wait_send)
    for copy in shares + raws:
        copy.wait_send()


def on_device(tiles, views, volumes, initial_affine, slab_start, margin_rows, view_gain):
    depth, height, width = volumes.shape[2:]
    half = height // 2
    chunks = half // CHUNK
    smem = pl.BlockSpec(memory_space=pltpu.SMEM)
    vmem = pl.BlockSpec(memory_space=pltpu.VMEM)
    dma = pltpu.SemaphoreType.DMA
    return pl.pallas_call(
        functools.partial(kernel, tiles, views),
        out_shape=(jax.ShapeDtypeStruct((1, 1, height, width), F32), jax.ShapeDtypeStruct((1, 12), F32)),
        in_specs=[pl.BlockSpec(memory_space=pltpu.HBM), pl.BlockSpec(memory_space=pltpu.HBM), smem, smem, smem],
        out_specs=(vmem, vmem),
        scratch_shapes=[
            pltpu.VMEM((depth, height + 2 * PAD, width), F32),
            pltpu.VMEM((3, depth, height, width), F32),
            pltpu.VMEM((depth, SLAB + 2 * PAD, width), F32),
            pltpu.VMEM((3, depth, SLAB, width), F32),
            pltpu.VMEM((depth, SENT_ROWS + PAD, width), F32),
            pltpu.VMEM((3, depth, HALF_SLAB, width), F32),
            pltpu.VMEM((depth, HALF_SLAB, width), F32),
            pltpu.VMEM((8, 128), jnp.int32),
            pltpu.VMEM((8, 128), jnp.int32),
            pltpu.VMEM((1, 12), F32),
            pltpu.VMEM((6, 10, 8, 128), F32),
            pltpu.VMEM((2, 12, 8, 128), F32),
            pltpu.VMEM((14, 16, 128), F32),
            pltpu.VMEM((views, 16, 128), F32),
            pltpu.VMEM((5, 16, 128), F32),
            pltpu.VMEM((16, 128), F32),
            pltpu.VMEM((depth, 4, 8, width), F32),
            pltpu.VMEM((6, half, width), F32),
            pltpu.VMEM((6, half, width), F32),
            pltpu.VMEM((2, RAW_CHUNKS * CHUNK + 2 * PAD, width), F32),
            pltpu.VMEM((2, RAW_CHUNKS * CHUNK, width), F32),
            pltpu.VMEM((2, 8, width), F32),
            dma((depth + 1,)), dma((2,)), dma((2, depth)), dma((2,)),
            dma((views - 1,)), dma((views - 1,)), dma((4,)), dma((4,)),
            dma((6, chunks)), dma((6, chunks)), dma((2, 8)),
        ],
        compiler_params=pltpu.CompilerParams(
            collective_id=0, has_side_effects=True, vmem_limit_bytes=52 * 1024 * 1024
        ),
        name="refine_and_join",
    )(
        pltpu.with_memory_space_constraint(volumes, pltpu.HBM),
        pltpu.with_memory_space_constraint(initial_affine, pltpu.HBM),
        slab_start,
        margin_rows,
        view_gain,
    )


def solution(mesh):
    placed = (
        P("tile", "view", None, None, None),
        P("tile", None),
        P("tile"),
        P("tile"),
        P("tile", "view"),
    )
    return jax.shard_map(
        functools.partial(on_device, mesh.shape["tile"], mesh.shape["view"]),
        mesh=mesh,
        in_specs=placed,
        out_specs=(P("tile", "view", None, None), P("tile", None)),
        check_vma=False,
    )
```

```python
import functools

import jax
import jax.numpy as jnp
from jax import lax
from jax.experimental import pallas as pl
from jax.experimental.pallas import tpu as pltpu
from jax.sharding import PartitionSpec as P

MESH = pl.DeviceIdType.MESH
F32 = jnp.float32
SLAB = 64
FIRST_ROWS = 16
REST_ROWS = SLAB - FIRST_ROWS
SENT_ROWS = FIRST_ROWS + 8
STIFFNESS_FACTOR = 0.25
PAD = 8
CHUNK = 32
RAW_CHUNKS = 5
EARLY_ROWS = 96
PAIRS = ((0, 0), (0, 1), (0, 2), (1, 1), (1, 2), (2, 2))
MONOS = ((0, 0), (0, 1), (0, 2), (0, 3), (1, 1), (1, 2), (1, 3), (2, 2), (2, 3), (3, 3))


def iota(shape, dim):
    return lax.broadcasted_iota(jnp.int32, shape, dim)


def coordinate(index, count):
    return (index.astype(F32) + 0.5) * (2.0 / count) - 1.0


def x_gradient(a):
    width = a.shape[-1]
    left = pltpu.roll(a, 1, 1)
    right = pltpu.roll(a, width - 1, 1)
    lane = iota(a.shape, 1)
    inner = (right - left) * 0.5
    return jnp.where(lane == 0, right - a, jnp.where(lane == width - 1, a - left, inner))


def y_gradient(before, a, after):
    top, bottom = iota(a.shape, 0) == 0, iota(a.shape, 0) == 7
    upper = jnp.where(bottom, pltpu.roll(after, 7, 0), pltpu.roll(a, 7, 0))
    lower = jnp.where(top, pltpu.roll(before, 1, 0), pltpu.roll(a, 1, 0))
    return (upper - lower) * 0.5


def z_gradients(p):
    n = len(p)
    inner = [(p[z + 1] - p[z - 1]) * 0.5 for z in range(1, n - 1)]
    return [p[1] - p[0]] + inner + [p[n - 1] - p[n - 2]]


def kernel(
    tiles, views,
    vol, aff, slab, margin, gain, out, refined,
    vp, grads, wst, wgrad, wrx, wrx_grad, nrx, mown, mlow, start_affine, hacc, qacc, cols, buf1, buf2, pcol, xk, snd, rcv, rawv, rawg, wraw,
    vsem, msem, wsem, nsem, s1, r1, s2, r2, ssem, rsem, rawsem,
):
    depth, height, width = vol.shape[2:]
    lanes = width // 128
    half = height // 2
    chunks = half // CHUNK
    t = lax.axis_index("tile")
    v = lax.axis_index("view")

    def tile_at(k):
        return lax.rem(t + tiles + k, tiles)

    def view_at(k):
        return lax.rem(v + views + k, views)

    def exists(k):
        return t + k >= 0 if k < 0 else t + k < tiles

    def when_tile(k, action):
        pl.when(exists(k))(action)

    def dev(tile, view):
        return {"tile": tile, "view": view}

    def remote(src, dst, send, recv, device):
        return pltpu.make_async_remote_copy(
            src_ref=src, dst_ref=dst, send_sem=send, recv_sem=recv, device_id=device, device_id_type=MESH
        )

    loads = [pltpu.make_async_copy(vol.at[0, 0, z], vp.at[z, pl.ds(PAD, height)], vsem.at[z]) for z in range(depth)]
    loads.append(pltpu.make_async_copy(aff, start_affine, vsem.at[depth]))
    for load in loads:
        load.start()
    barrier = pltpu.get_barrier_semaphore()
    buf2[...] = jnp.zeros_like(buf2)
    tile_steps = (-2, -1, 1, 2)

    def greet(device):
        pl.semaphore_signal(barrier, inc=1, device_id=device, device_id_type=MESH)

    for k in tile_steps:
        when_tile(k, functools.partial(greet, dev(tile_at(k), v)))
    for k in range(1, views):
        greet(dev(t, view_at(k)))
    mown[...] = jnp.full((8, 128), margin[0], jnp.int32)
    hacc[...] = jnp.zeros_like(hacc)
    qacc[...] = jnp.zeros_like(qacc)
    cols[...] = jnp.zeros_like(cols)
    peers = views - 1
    for k in tile_steps:
        peers = peers + jnp.where(exists(k), 1, 0)
    pl.semaphore_wait(barrier, peers)
    send_margin = remote(mown, mlow, msem.at[0], msem.at[1], dev(tile_at(1), v))
    when_tile(1, send_margin.start)
    send_near = remote(
        vol.at[0, 0, :, pl.ds(height - REST_ROWS, REST_ROWS)], nrx, nsem.at[0], nsem.at[1], dev(tile_at(1), v)
    )
    when_tile(1, send_near.start)

    down_view, up_view, far_view = view_at(-1), view_at(1), view_at(2)
    raws = []
    for part, (first, end) in enumerate(((0, EARLY_ROWS), (EARLY_ROWS, RAW_CHUNKS * CHUNK))):
        for side, target in ((0, down_view), (1, up_view)):
            begin = first + PAD if part else first - side * PAD
            source = vol.at[0, 0, far_view, pl.ds(side * half + begin, end + PAD - begin)]
            landing = rawv.at[side, pl.ds(PAD + begin, end + PAD - begin)]
            raws.append(remote(source, landing, rawsem.at[0, 4 * part + side], rawsem.at[1, 4 * part + side], dev(t, target)))
        for side, target in ((0, down_view), (1, up_view)):
            sems = [rawsem.at[k, 4 * part + 2 + side] for k in range(2)]
            rows = pl.ds(side * half + first, end - first)
            raws.append(
                remote(grads.at[0, far_view, rows], rawg.at[side, pl.ds(first, end - first)], *sems, dev(t, target))
            )
    for raw in raws[:2]:
        raw.start()
    start = slab[0]
    aligned = lax.div(start, 8) * 8
    shift = jnp.full((SLAB + 8, width), start - aligned, jnp.int32)
    moves = [(k, lax.bitwise_and(shift, k) != 0) for k in (1, 2, 4)]
    for load in loads:
        load.wait()
    send_windows = []
    for z in range(depth):
        rows = vp[z, pl.ds(aligned + PAD, SLAB + 8), :]
        for k, moved in moves:
            rows = jnp.where(moved, pltpu.roll(rows, SLAB + 8 - k, 0), rows)
        wst[z, PAD : PAD + SLAB, :] = rows[:SLAB]
        sent = pl.ds(PAD, SENT_ROWS)
        send_windows.append(
            remote(wst.at[z, sent], wrx.at[z, sent], wsem.at[0, z], wsem.at[1, z], dev(tile_at(-1), v))
        )
        when_tile(-1, send_windows[z].start)
    for z in range(depth):
        vp[z, PAD - 1 : PAD, :] = 2.0 * vp[z, PAD : PAD + 1, :] - vp[z, PAD + 1 : PAD + 2, :]
        last = PAD + height - 1
        vp[z, last + 1 : last + 2, :] = 2.0 * vp[z, last : last + 1, :] - vp[z, last - 1 : last, :]

    def depth_gradients_of(src, dst, count):
        def body(r, _):
            r = pl.multiple_of(r * 8, 8)
            planes = [src[z, pl.ds(pl.multiple_of(PAD + r, 8), 8), :] for z in range(depth)]
            for z, g in enumerate(z_gradients(planes)):
                dst[0, z, pl.ds(r, 8), :] = g
            return 0

        lax.fori_loop(0, count // 8, body, 0)

    depth_gradients_of(vp, grads, height)

    for raw in raws[2:4]:
        raw.start()

    for z in range(depth):
        wst[z, PAD - 1 : PAD, :] = 2.0 * wst[z, PAD : PAD + 1, :] - wst[z, PAD + 1 : PAD + 2, :]
        last = PAD + SLAB - 1
        wst[z, last + 1 : last + 2, :] = 2.0 * wst[z, last : last + 1, :] - wst[z, last - 1 : last, :]

    def gradients_of(src, dst, first, end):
        def body(r, _):
            r = pl.multiple_of(r * 8, 8)
            planes = [src[z, pl.ds(PAD + r, 8), :] for z in range(depth)]
            for z in range(depth):
                before, after = src[z, pl.ds(r, 8), :], src[z, pl.ds(2 * PAD + r, 8), :]
                dst[1, z, pl.ds(r, 8), :] = y_gradient(before, planes[z], after)
                dst[2, z, pl.ds(r, 8), :] = x_gradient(planes[z])
            return 0

        lax.fori_loop(first // 8, end // 8, body, 0)

    depth_gradients_of(wst, wgrad, SLAB)
    gradients_of(wst, wgrad, 0, SLAB)

    zc = [(z + 0.5) / depth * 2.0 - 1.0 for z in range(depth)]

    def depth_sum(fields, power):
        return functools.reduce(lambda a, b: a + b, [f * (c**power) if power else f for f, c in zip(fields, zc)])

    sub = iota((8, 128), 0)
    lane8 = iota((8, 128), 1)

    def gradients_at(srcg, r, xs, mask):
        return [[srcg[k, z, pl.ds(r, 8), xs] * mask for z in range(depth)] for k in range(3)]

    def row_coordinate(r):
        return coordinate(sub + (r + height - SLAB), height)

    when_tile(-1, send_margin.wait_recv)
    low_rows = mlow[...]
    own_rows = mown[...]

    def matrix_lanes(xl, _):
        xs = pl.ds(pl.multiple_of(xl * 128, 128), 128)
        xv = coordinate(lane8 + xl * 128, width)

        def body(yb, carry):
            r = pl.multiple_of(yb * 8, 8)
            mask = jnp.where(sub + r < low_rows, 1.0, 0.0).astype(F32)
            g = gradients_at(wgrad, r, xs, mask)
            yv = row_coordinate(r)
            new = []
            for f, (a, b) in enumerate(PAIRS):
                fields = [g[a][z] * g[b][z] for z in range(depth)]
                p0, p1, p2 = (depth_sum(fields, k) for k in range(3))
                yp = yv * p0
                terms = (p2, yv * p1, p1, yv * yp, yp, p0)
                new += [c + term for c, term in zip(carry[6 * f : 6 * f + 6], terms)]
            return tuple(new)

        sums = lax.fori_loop(0, SLAB // 8, body, tuple(jnp.zeros((8, 128), F32) for _ in range(36)))
        for f in range(6):
            zz, zy, zo, yy, yo, oo = sums[6 * f : 6 * f + 6]
            xo = xv * oo
            for m, term in enumerate((zz, zy, xv * zo, zo, yy, xv * yo, yo, xv * xo, xo, oo)):
                hacc[f, m] += term
        return 0

    lax.fori_loop(0, lanes, matrix_lanes, 0)
    for f, (a, b) in enumerate(PAIRS):
        for m, (i, j) in enumerate(MONOS):
            row = jnp.sum(hacc[f, m], axis=0, keepdims=True)
            for p, q in {(4 * a + i, 4 * b + j), (4 * a + j, 4 * b + i), (4 * b + i, 4 * a + j), (4 * b + j, 4 * a + i)}:
                cols[p, q : q + 1, :] = row

    def moment(part, src, srcg, first, count, rows, near):
        def lane_block(xl, _):
            xs = pl.ds(pl.multiple_of(xl * 128, 128), 128)
            xv = coordinate(lane8 + xl * 128, width)

            def body(yb, carry):
                r = pl.multiple_of(yb * 8, 8)
                mask = jnp.where(sub + (r + first) < rows, 1.0, 0.0).astype(F32)
                g = gradients_at(srcg, pl.multiple_of(r + first, 8), xs, mask)
                window = [src[z, pl.ds(pl.multiple_of(PAD + first + r, 8), 8), xs] for z in range(depth)]
                residual = [near(z, r, xs) - window[z] for z in range(depth)]
                yv = row_coordinate(r + first)
                new = []
                for k in range(3):
                    fields = [g[k][z] * residual[z] for z in range(depth)]
                    p0, p1 = depth_sum(fields, 0), depth_sum(fields, 1)
                    new += [c + term for c, term in zip(carry[3 * k : 3 * k + 3], (p1, yv * p0, p0))]
                return tuple(new)

            sums = lax.fori_loop(0, count // 8, body, tuple(jnp.zeros((8, 128), F32) for _ in range(9)))
            for k in range(3):
                zo, yo, oo = sums[3 * k : 3 * k + 3]
                for j, term in enumerate((zo, yo, xv * oo, oo)):
                    qacc[part, 4 * k + j] += term
            return 0

        lax.fori_loop(0, lanes, lane_block, 0)
        for i in range(12):
            cols[12 + part, i : i + 1, :] = jnp.sum(qacc[part, i], axis=0, keepdims=True)

    row = iota((16, 128), 0)
    lane = iota((16, 128), 1)
    tile_index = row * 0 + t
    has_low, has_next = tile_index > 0, tile_index < tiles - 1
    block = jnp.zeros((16, 128), F32)

    def placed(block, c):
        total = jnp.sum(cols[c], axis=1, keepdims=True)
        return jnp.where((lane == c) & (has_next if c == 13 else has_low), total, block)

    for c in range(12):
        block = placed(block, c)
    when_tile(-1, send_near.wait_recv)
    moment(0, wst, wgrad, FIRST_ROWS, REST_ROWS, low_rows, lambda z, r, xs: nrx[z, pl.ds(r, 8), xs])
    for send_window in send_windows:
        when_tile(1, send_window.wait_recv)
    for z in range(depth):
        wrx[z, PAD - 1 : PAD, :] = 2.0 * wrx[z, PAD : PAD + 1, :] - wrx[z, PAD + 1 : PAD + 2, :]
    depth_gradients_of(wrx, wrx_grad, FIRST_ROWS)
    gradients_of(wrx, wrx_grad, 0, FIRST_ROWS)
    moment(1, wrx, wrx_grad, 0, FIRST_ROWS, own_rows, lambda z, r, xs: vp[z, pl.ds(PAD + height - SLAB + r, 8), xs])

    block = placed(block, 12)
    block = placed(block, 13)
    buf1[v] = block
    buf1[v, 13:14, :] = jnp.full((1, 128), gain[0, 0], F32)
    shares = [
        remote(buf1.at[v], buf1.at[v], s1.at[k - 1], r1.at[k - 1], dev(t, view_at(k))) for k in range(1, views)
    ]
    for share in shares:
        share.start()
    gradients_of(vp, grads, 0, half)
    for k, share in enumerate(shares):
        share.wait_recv()
    total = buf1[0]
    for k in range(1, views):
        total = total + buf1[k]
    buf2[2] = jnp.where(row < 12, total, 0.0)
    buf2[2, 12:13, 0:12] = start_affine[...]
    passes = [
        remote(buf2.at[2], buf2.at[2 - k], s2.at[i], r2.at[i], dev(tile_at(k), v)) for i, k in enumerate(tile_steps)
    ]
    for k, passed in zip(tile_steps, passes):
        when_tile(k, passed.start)
    for raw in raws[4:]:
        raw.start()
    gradients_of(vp, grads, half, height)
    across = coordinate(iota((8, width), 1), width)
    facing = 1.0 - 2.0 * lax.rem(v, 2).astype(F32)

    def plane_weights(z, _):
        xk[z, 3] = (0.2 + (1.0 + facing * across) * 0.5) * (gain[0, 0] * (1.5 + facing * coordinate(z, depth)))
        return 0

    lax.fori_loop(0, depth, plane_weights, 0)
    for side, plane, source in ((0, down_view, up_view), (1, up_view, down_view)):
        g = jnp.concatenate([jnp.broadcast_to(buf1[source, 13:14, :], (8, 128))] * lanes, axis=1)
        wraw[side] = (0.2 + (1.0 - facing * across) * 0.5) * (g * (1.5 - facing * coordinate(plane, depth)))

    zf = coordinate(v, depth)
    weights = jnp.zeros((8, width), F32)
    for k in range(views):
        s = 1.0 - 2.0 * (k % 2)
        g = jnp.concatenate([jnp.broadcast_to(buf1[k, 13:14, :], (8, 128))] * lanes, axis=1)
        weights = weights + g * (1.5 + s * zf) * (0.2 + (1.0 + s * across) * 0.5)
    inverse = 1.0 / weights

    for k, passed in zip(tile_steps, passes):
        when_tile(-k, passed.wait_recv)

    inside = (row < 12) & (lane < 12)
    blocks = [buf2[k] for k in range(5)]
    below2, below, here, above = [jnp.where(inside, blocks[k + 1], 0.0) for k in range(4)]
    eye = jnp.where((row == lane) & (row < 12), 1.0, 0.0).astype(F32)

    def column(a, k):
        return jnp.broadcast_to(a[:, k : k + 1], (16, 128))

    def lane_sum(a):
        return jnp.broadcast_to(jnp.sum(a, axis=1, keepdims=True), (16, 128))

    def as_row(col):
        return jnp.broadcast_to(jnp.sum(col * eye, axis=0, keepdims=True), (16, 128))

    q = [column(blocks[k + 1], 12) + column(blocks[k], 13) for k in range(4)]
    starts = [jnp.broadcast_to(blocks[k][12:13, :], (16, 128)) for k in range(5)]
    stiff = eye * (STIFFNESS_FACTOR * depth * SLAB * width * views)
    right_up = lane_sum(above * starts[4] + here * starts[2] + stiff * starts[3]) - q[3] + q[2]
    right_down = lane_sum(below * starts[2] + below2 * starts[0] + stiff * starts[1]) - q[1] + q[0]
    right_own = lane_sum(stiff * starts[2]) - q[2] + q[1]
    real = row < 12
    up = jnp.where((lane == 12) & real, right_up, above + here + stiff)
    down = jnp.where((lane == 12) & real, right_down, below + below2 + stiff)
    own = here + below + stiff + pltpu.roll(here, 12, 1) + pltpu.roll(below, 24, 1)
    own = jnp.where((lane == 36) & real, right_own, own)
    systems = [up, down, own]
    for k in range(12):
        for i in range(3):
            a = systems[i]
            col = column(a, k)
            scaled = jnp.broadcast_to(a[k : k + 1, :] / col[k : k + 1, :], (16, 128))
            systems[i] = jnp.where(row == k, scaled, a - col * scaled)
    up, down, own = systems
    first_up, first_down = as_row(column(up, 12)), as_row(column(down, 12))
    mix = pltpu.roll(first_up, 12, 1) + pltpu.roll(first_down, 24, 1) + jnp.where(lane == 36, 1.0, 0.0)
    params = lane_sum(own * mix)
    pcol[...] = params
    refined[...] = as_row(params)[0:1, 0:12]

    def entry(k, j):
        return jnp.broadcast_to(pcol[4 * k + j : 4 * k + j + 1, :], (8, 128))

    def entry_row(k, j):
        return jnp.concatenate([entry(k, j)] * lanes, axis=1)

    def tables(z, _):
        zf = coordinate(z, depth)
        for k in range(3):
            xk[z, k] = entry_row(k, 0) * zf + entry_row(k, 3) + entry_row(k, 2) * across
        return 0

    lax.fori_loop(0, depth, tables, 0)
    slopes = [entry_row(k, 1) for k in range(3)]
    sub_row = iota((8, width), 0)

    def numerator_rows(z, first, dst, dst_first, extra, scale):
        def body(rb, _):
            r = pl.multiple_of(first + rb * 8, 8)
            d = pl.multiple_of(dst_first + rb * 8, 8)
            yv = coordinate(sub_row + r, height)
            value = vp[z, pl.ds(pl.multiple_of(PAD + r, 8), 8), :]
            for k in range(3):
                value = value + grads[k, z, pl.ds(r, 8), :] * (xk[z, k] + slopes[k] * yv)
            value = value * xk[z, 3]
            for stream in extra:
                value = value + rcv[stream, pl.ds(d, 8), :]
            if scale is not None:
                value = value * scale
            dst(d, value)
            return 0

        lax.fori_loop(0, CHUNK // 8, body, 0)

    def hop(stream, c):
        rows = pl.ds(pl.multiple_of(c * CHUNK, CHUNK), CHUNK)
        target = down_view if stream % 2 == 0 else up_view
        return remote(
            snd.at[stream, rows], rcv.at[stream, rows], ssem.at[stream, c], rsem.at[stream, c], dev(t, target)
        )

    def send_chunk(stream, c, plane, upper, extra=()):
        def put(d, value):
            snd[stream, pl.ds(d, 8), :] = value

        c_row = pl.multiple_of(c * CHUNK, CHUNK)
        numerator_rows(plane, (half if upper else 0) + c_row, put, c_row, extra, None)
        hop(stream, c).start()

    def relay_raw(side, c):
        plane = (down_view, up_view)[side]
        stream = 4 + side
        c_row = pl.multiple_of(c * CHUNK, CHUNK)

        def body(rb, _):
            d = pl.multiple_of(c_row + rb * 8, 8)
            r = pl.multiple_of(side * half + d, 8)
            yv = coordinate(sub_row + r, height)
            shifts = [xk[plane, k] + slopes[k] * yv for k in range(3)]
            value = vp[plane, pl.ds(pl.multiple_of(PAD + r, 8), 8), :]
            for k in range(3):
                value = value + grads[k, plane, pl.ds(r, 8), :] * shifts[k]
            before, here_v, after = [rawv[side, pl.ds(pl.multiple_of(d + k * PAD, 8), 8), :] for k in range(3)]
            other = here_v + rawg[side, pl.ds(d, 8), :] * shifts[0]
            other = other + y_gradient(before, here_v, after) * shifts[1] + x_gradient(here_v) * shifts[2]
            snd[stream, pl.ds(d, 8), :] = value * xk[plane, 3] + other * wraw[side]
            return 0

        lax.fori_loop(0, CHUNK // 8, body, 0)
        hop(stream, c).start()

    def far(c, _):
        send_chunk(0, c, far_view, False)
        send_chunk(1, c, far_view, True)
        return 0

    def near_planes(c, _):
        send_chunk(2, c, down_view, True)
        send_chunk(3, c, up_view, False)
        return 0

    def relay(c, _):
        hop(0, c).wait_recv()
        send_chunk(4, c, down_view, False, (0,))
        hop(1, c).wait_recv()
        send_chunk(5, c, up_view, True, (1,))
        return 0

    def relay_both(c, _):
        relay_raw(0, c)
        relay_raw(1, c)
        return 0

    lax.fori_loop(RAW_CHUNKS, chunks, far, 0)
    lax.fori_loop(0, chunks, near_planes, 0)
    for raw in raws:
        raw.wait_recv()
    rawv[0, PAD - 1 : PAD, :] = 2.0 * rawv[0, PAD : PAD + 1, :] - rawv[0, PAD + 1 : PAD + 2, :]
    lax.fori_loop(0, RAW_CHUNKS, relay_both, 0)
    lax.fori_loop(RAW_CHUNKS, chunks, relay, 0)

    def finish(c, _):
        c_row = pl.multiple_of(c * CHUNK, CHUNK)
        for part, streams in ((0, (3, 4)), (1, (2, 5))):
            for stream in streams:
                hop(stream, c).wait_recv()

            def put(d, value, part=part):
                out[0, 0, pl.ds(pl.multiple_of(part * half + d, 8), 8), :] = value

            numerator_rows(v, part * half + c_row, put, c_row, streams, inverse)
        return 0

    lax.fori_loop(0, chunks, finish, 0)

    def drain(c, _):
        for stream in range(2, 6):
            hop(stream, c).wait_send()
        return 0

    def drain_far(c, _):
        hop(0, c).wait_send()
        hop(1, c).wait_send()
        return 0

    lax.fori_loop(0, chunks, drain, 0)
    lax.fori_loop(RAW_CHUNKS, chunks, drain_far, 0)
    when_tile(1, send_margin.wait_send)
    when_tile(1, send_near.wait_send)
    for send_window in send_windows:
        when_tile(-1, send_window.wait_send)
    for k, passed in zip(tile_steps, passes):
        when_tile(k, passed.wait_send)
    for copy in shares + raws:
        copy.wait_send()


def on_device(tiles, views, volumes, initial_affine, slab_start, margin_rows, view_gain):
    depth, height, width = volumes.shape[2:]
    half = height // 2
    chunks = half // CHUNK
    smem = pl.BlockSpec(memory_space=pltpu.SMEM)
    vmem = pl.BlockSpec(memory_space=pltpu.VMEM)
    dma = pltpu.SemaphoreType.DMA
    return pl.pallas_call(
        functools.partial(kernel, tiles, views),
        out_shape=(jax.ShapeDtypeStruct((1, 1, height, width), F32), jax.ShapeDtypeStruct((1, 12), F32)),
        in_specs=[pl.BlockSpec(memory_space=pltpu.HBM), pl.BlockSpec(memory_space=pltpu.HBM), smem, smem, smem],
        out_specs=(vmem, vmem),
        scratch_shapes=[
            pltpu.VMEM((depth, height + 2 * PAD, width), F32),
            pltpu.VMEM((3, depth, height, width), F32),
            pltpu.VMEM((depth, SLAB + 2 * PAD, width), F32),
            pltpu.VMEM((3, depth, SLAB, width), F32),
            pltpu.VMEM((depth, SENT_ROWS + PAD, width), F32),
            pltpu.VMEM((3, depth, FIRST_ROWS, width), F32),
            pltpu.VMEM((depth, REST_ROWS, width), F32),
            pltpu.VMEM((8, 128), jnp.int32),
            pltpu.VMEM((8, 128), jnp.int32),
            pltpu.VMEM((1, 12), F32),
            pltpu.VMEM((6, 10, 8, 128), F32),
            pltpu.VMEM((2, 12, 8, 128), F32),
            pltpu.VMEM((14, 16, 128), F32),
            pltpu.VMEM((views, 16, 128), F32),
            pltpu.VMEM((5, 16, 128), F32),
            pltpu.VMEM((16, 128), F32),
            pltpu.VMEM((depth, 4, 8, width), F32),
            pltpu.VMEM((6, half, width), F32),
            pltpu.VMEM((6, half, width), F32),
            pltpu.VMEM((2, RAW_CHUNKS * CHUNK + 2 * PAD, width), F32),
            pltpu.VMEM((2, RAW_CHUNKS * CHUNK, width), F32),
            pltpu.VMEM((2, 8, width), F32),
            dma((depth + 1,)), dma((2,)), dma((2, depth)), dma((2,)),
            dma((views - 1,)), dma((views - 1,)), dma((4,)), dma((4,)),
            dma((6, chunks)), dma((6, chunks)), dma((2, 8)),
        ],
        compiler_params=pltpu.CompilerParams(
            collective_id=0, has_side_effects=True, vmem_limit_bytes=52 * 1024 * 1024
        ),
        name="refine_and_join",
    )(
        pltpu.with_memory_space_constraint(volumes, pltpu.HBM),
        pltpu.with_memory_space_constraint(initial_affine, pltpu.HBM),
        slab_start,
        margin_rows,
        view_gain,
    )


def solution(mesh):
    placed = (
        P("tile", "view", None, None, None),
        P("tile", None),
        P("tile"),
        P("tile"),
        P("tile", "view"),
    )
    return jax.shard_map(
        functools.partial(on_device, mesh.shape["tile"], mesh.shape["view"]),
        mesh=mesh,
        in_specs=placed,
        out_specs=(P("tile", "view", None, None), P("tile", None)),
        check_vma=False,
    )
```

```python
import functools

import jax
import jax.numpy as jnp
from jax import lax
from jax.experimental import pallas as pl
from jax.experimental.pallas import tpu as pltpu
from jax.sharding import PartitionSpec as P

MESH = pl.DeviceIdType.MESH
F32 = jnp.float32
SLAB = 64
FIRST_ROWS = 16
REST_ROWS = SLAB - FIRST_ROWS
SENT_ROWS = FIRST_ROWS + 8
STIFFNESS_FACTOR = 0.25
PAD = 8
CHUNK = 32
RAW_CHUNKS = 5
EARLY_ROWS = 96
PAIRS = ((0, 0), (0, 1), (0, 2), (1, 1), (1, 2), (2, 2))
MONOS = ((0, 0), (0, 1), (0, 2), (0, 3), (1, 1), (1, 2), (1, 3), (2, 2), (2, 3), (3, 3))


def iota(shape, dim):
    return lax.broadcasted_iota(jnp.int32, shape, dim)


def coordinate(index, count):
    return (index.astype(F32) + 0.5) * (2.0 / count) - 1.0


def x_gradient(a):
    width = a.shape[-1]
    left = pltpu.roll(a, 1, 1)
    right = pltpu.roll(a, width - 1, 1)
    lane = iota(a.shape, 1)
    inner = (right - left) * 0.5
    return jnp.where(lane == 0, right - a, jnp.where(lane == width - 1, a - left, inner))


def y_gradient(before, a, after):
    top, bottom = iota(a.shape, 0) == 0, iota(a.shape, 0) == 7
    upper = jnp.where(bottom, pltpu.roll(after, 7, 0), pltpu.roll(a, 7, 0))
    lower = jnp.where(top, pltpu.roll(before, 1, 0), pltpu.roll(a, 1, 0))
    return (upper - lower) * 0.5


def z_gradients(p):
    n = len(p)
    inner = [(p[z + 1] - p[z - 1]) * 0.5 for z in range(1, n - 1)]
    return [p[1] - p[0]] + inner + [p[n - 1] - p[n - 2]]


def kernel(
    tiles, views,
    vol, aff, slab, margin, gain, out, refined,
    vp, grads, wst, wgrad, wrx, wrx_grad, nrx, mown, mlow, start_affine, hacc, qacc, cols, buf1, buf2, pcol, xk, snd, rcv, rawv, rawg, wraw,
    vsem, msem, wsem, nsem, s1, r1, s2, r2, ssem, rsem, rawsem,
):
    depth, height, width = vol.shape[2:]
    lanes = width // 128
    half = height // 2
    chunks = half // CHUNK
    t = lax.axis_index("tile")
    v = lax.axis_index("view")

    def tile_at(k):
        return lax.rem(t + tiles + k, tiles)

    def view_at(k):
        return lax.rem(v + views + k, views)

    def exists(k):
        return t + k >= 0 if k < 0 else t + k < tiles

    def when_tile(k, action):
        pl.when(exists(k))(action)

    def dev(tile, view):
        return {"tile": tile, "view": view}

    def remote(src, dst, send, recv, device):
        return pltpu.make_async_remote_copy(
            src_ref=src, dst_ref=dst, send_sem=send, recv_sem=recv, device_id=device, device_id_type=MESH
        )

    loads = [pltpu.make_async_copy(vol.at[0, 0, z], vp.at[z, pl.ds(PAD, height)], vsem.at[z]) for z in range(depth)]
    loads.append(pltpu.make_async_copy(aff, start_affine, vsem.at[depth]))
    for load in loads:
        load.start()
    barrier = pltpu.get_barrier_semaphore()
    buf2[...] = jnp.zeros_like(buf2)
    tile_steps = (-2, -1, 1, 2)

    def greet(device):
        pl.semaphore_signal(barrier, inc=1, device_id=device, device_id_type=MESH)

    for k in tile_steps:
        when_tile(k, functools.partial(greet, dev(tile_at(k), v)))
    for k in range(1, views):
        greet(dev(t, view_at(k)))
    mown[...] = jnp.full((8, 128), margin[0], jnp.int32)
    hacc[...] = jnp.zeros_like(hacc)
    qacc[...] = jnp.zeros_like(qacc)
    cols[...] = jnp.zeros_like(cols)
    peers = views - 1
    for k in tile_steps:
        peers = peers + jnp.where(exists(k), 1, 0)
    pl.semaphore_wait(barrier, peers)
    send_margin = remote(mown, mlow, msem.at[0], msem.at[1], dev(tile_at(1), v))
    when_tile(1, send_margin.start)
    send_near = remote(
        vol.at[0, 0, :, pl.ds(height - REST_ROWS, REST_ROWS)], nrx, nsem.at[0], nsem.at[1], dev(tile_at(1), v)
    )
    when_tile(1, send_near.start)

    down_view, up_view, far_view = view_at(-1), view_at(1), view_at(2)
    raws = []
    for part, (first, end) in enumerate(((0, EARLY_ROWS), (EARLY_ROWS, RAW_CHUNKS * CHUNK))):
        for side, target in ((0, down_view), (1, up_view)):
            begin = first + PAD if part else first - side * PAD
            source = vol.at[0, 0, far_view, pl.ds(side * half + begin, end + PAD - begin)]
            landing = rawv.at[side, pl.ds(PAD + begin, end + PAD - begin)]
            raws.append(remote(source, landing, rawsem.at[0, 4 * part + side], rawsem.at[1, 4 * part + side], dev(t, target)))
        for side, target in ((0, down_view), (1, up_view)):
            sems = [rawsem.at[k, 4 * part + 2 + side] for k in range(2)]
            rows = pl.ds(side * half + first, end - first)
            raws.append(
                remote(grads.at[0, far_view, rows], rawg.at[side, pl.ds(first, end - first)], *sems, dev(t, target))
            )
    for raw in raws[:2]:
        raw.start()
    start = slab[0]
    aligned = lax.div(start, 8) * 8
    shift = jnp.full((SLAB + 8, width), start - aligned, jnp.int32)
    moves = [(k, lax.bitwise_and(shift, k) != 0) for k in (1, 2, 4)]
    for load in loads:
        load.wait()
    send_windows = []
    for z in range(depth):
        rows = vp[z, pl.ds(aligned + PAD, SLAB + 8), :]
        for k, moved in moves:
            rows = jnp.where(moved, pltpu.roll(rows, SLAB + 8 - k, 0), rows)
        wst[z, PAD : PAD + SLAB, :] = rows[:SLAB]
        sent = pl.ds(PAD, SENT_ROWS)
        send_windows.append(
            remote(wst.at[z, sent], wrx.at[z, sent], wsem.at[0, z], wsem.at[1, z], dev(tile_at(-1), v))
        )
        when_tile(-1, send_windows[z].start)
    for z in range(depth):
        vp[z, PAD - 1 : PAD, :] = 2.0 * vp[z, PAD : PAD + 1, :] - vp[z, PAD + 1 : PAD + 2, :]
        last = PAD + height - 1
        vp[z, last + 1 : last + 2, :] = 2.0 * vp[z, last : last + 1, :] - vp[z, last - 1 : last, :]

    def depth_gradients_of(src, dst, count):
        def body(r, _):
            r = pl.multiple_of(r * 8, 8)
            planes = [src[z, pl.ds(pl.multiple_of(PAD + r, 8), 8), :] for z in range(depth)]
            for z, g in enumerate(z_gradients(planes)):
                dst[0, z, pl.ds(r, 8), :] = g
            return 0

        lax.fori_loop(0, count // 8, body, 0)

    depth_gradients_of(vp, grads, height)

    for raw in raws[2:4]:
        raw.start()

    for z in range(depth):
        wst[z, PAD - 1 : PAD, :] = 2.0 * wst[z, PAD : PAD + 1, :] - wst[z, PAD + 1 : PAD + 2, :]
        last = PAD + SLAB - 1
        wst[z, last + 1 : last + 2, :] = 2.0 * wst[z, last : last + 1, :] - wst[z, last - 1 : last, :]

    def gradients_of(src, dst, first, end):
        def body(r, _):
            r = pl.multiple_of(r * 8, 8)
            planes = [src[z, pl.ds(PAD + r, 8), :] for z in range(depth)]
            for z in range(depth):
                before, after = src[z, pl.ds(r, 8), :], src[z, pl.ds(2 * PAD + r, 8), :]
                dst[1, z, pl.ds(r, 8), :] = y_gradient(before, planes[z], after)
                dst[2, z, pl.ds(r, 8), :] = x_gradient(planes[z])
            return 0

        lax.fori_loop(first // 8, end // 8, body, 0)

    depth_gradients_of(wst, wgrad, SLAB)
    gradients_of(wst, wgrad, 0, SLAB)

    zc = [(z + 0.5) / depth * 2.0 - 1.0 for z in range(depth)]

    def depth_sum(fields, power):
        return functools.reduce(lambda a, b: a + b, [f * (c**power) if power else f for f, c in zip(fields, zc)])

    sub = iota((8, 128), 0)
    lane8 = iota((8, 128), 1)

    def gradients_at(srcg, r, xs, mask):
        return [[srcg[k, z, pl.ds(r, 8), xs] * mask for z in range(depth)] for k in range(3)]

    def row_coordinate(r):
        return coordinate(sub + (r + height - SLAB), height)

    when_tile(-1, send_margin.wait_recv)
    low_rows = mlow[...]
    own_rows = mown[...]

    def matrix_lanes(xl, _):
        xs = pl.ds(pl.multiple_of(xl * 128, 128), 128)
        xv = coordinate(lane8 + xl * 128, width)

        def body(yb, carry):
            r = pl.multiple_of(yb * 8, 8)
            mask = jnp.where(sub + r < low_rows, 1.0, 0.0).astype(F32)
            g = gradients_at(wgrad, r, xs, mask)
            yv = row_coordinate(r)
            new = []
            for f, (a, b) in enumerate(PAIRS):
                fields = [g[a][z] * g[b][z] for z in range(depth)]
                p0, p1, p2 = (depth_sum(fields, k) for k in range(3))
                yp = yv * p0
                terms = (p2, yv * p1, p1, yv * yp, yp, p0)
                new += [c + term for c, term in zip(carry[6 * f : 6 * f + 6], terms)]
            return tuple(new)

        sums = lax.fori_loop(0, SLAB // 8, body, tuple(jnp.zeros((8, 128), F32) for _ in range(36)))
        for f in range(6):
            zz, zy, zo, yy, yo, oo = sums[6 * f : 6 * f + 6]
            xo = xv * oo
            for m, term in enumerate((zz, zy, xv * zo, zo, yy, xv * yo, yo, xv * xo, xo, oo)):
                hacc[f, m] += term
        return 0

    lax.fori_loop(0, lanes, matrix_lanes, 0)
    for f, (a, b) in enumerate(PAIRS):
        for m, (i, j) in enumerate(MONOS):
            row = jnp.sum(hacc[f, m], axis=0, keepdims=True)
            for p, q in {(4 * a + i, 4 * b + j), (4 * a + j, 4 * b + i), (4 * b + i, 4 * a + j), (4 * b + j, 4 * a + i)}:
                cols[p, q : q + 1, :] = row

    def moment(part, src, srcg, first, count, rows, near):
        def lane_block(xl, _):
            xs = pl.ds(pl.multiple_of(xl * 128, 128), 128)
            xv = coordinate(lane8 + xl * 128, width)

            def body(yb, carry):
                r = pl.multiple_of(yb * 8, 8)
                mask = jnp.where(sub + (r + first) < rows, 1.0, 0.0).astype(F32)
                g = gradients_at(srcg, pl.multiple_of(r + first, 8), xs, mask)
                window = [src[z, pl.ds(pl.multiple_of(PAD + first + r, 8), 8), xs] for z in range(depth)]
                residual = [near(z, r, xs) - window[z] for z in range(depth)]
                yv = row_coordinate(r + first)
                new = []
                for k in range(3):
                    fields = [g[k][z] * residual[z] for z in range(depth)]
                    p0, p1 = depth_sum(fields, 0), depth_sum(fields, 1)
                    new += [c + term for c, term in zip(carry[3 * k : 3 * k + 3], (p1, yv * p0, p0))]
                return tuple(new)

            sums = lax.fori_loop(0, count // 8, body, tuple(jnp.zeros((8, 128), F32) for _ in range(9)))
            for k in range(3):
                zo, yo, oo = sums[3 * k : 3 * k + 3]
                for j, term in enumerate((zo, yo, xv * oo, oo)):
                    qacc[part, 4 * k + j] += term
            return 0

        lax.fori_loop(0, lanes, lane_block, 0)
        for i in range(12):
            cols[12 + part, i : i + 1, :] = jnp.sum(qacc[part, i], axis=0, keepdims=True)

    row = iota((16, 128), 0)
    lane = iota((16, 128), 1)
    tile_index = row * 0 + t
    has_low, has_next = tile_index > 0, tile_index < tiles - 1
    block = jnp.zeros((16, 128), F32)

    def placed(block, c):
        total = jnp.sum(cols[c], axis=1, keepdims=True)
        return jnp.where((lane == c) & (has_next if c == 13 else has_low), total, block)

    for c in range(12):
        block = placed(block, c)
    when_tile(-1, send_near.wait_recv)
    moment(0, wst, wgrad, FIRST_ROWS, REST_ROWS, low_rows, lambda z, r, xs: nrx[z, pl.ds(r, 8), xs])
    for send_window in send_windows:
        when_tile(1, send_window.wait_recv)
    for z in range(depth):
        wrx[z, PAD - 1 : PAD, :] = 2.0 * wrx[z, PAD : PAD + 1, :] - wrx[z, PAD + 1 : PAD + 2, :]
    depth_gradients_of(wrx, wrx_grad, FIRST_ROWS)
    gradients_of(wrx, wrx_grad, 0, FIRST_ROWS)
    moment(1, wrx, wrx_grad, 0, FIRST_ROWS, own_rows, lambda z, r, xs: vp[z, pl.ds(PAD + height - SLAB + r, 8), xs])

    block = placed(block, 12)
    block = placed(block, 13)
    buf1[v] = block
    buf1[v, 13:14, :] = jnp.full((1, 128), gain[0, 0], F32)
    shares = [
        remote(buf1.at[v], buf1.at[v], s1.at[k - 1], r1.at[k - 1], dev(t, view_at(k))) for k in range(1, views)
    ]
    for share in shares:
        share.start()
    for raw in raws[4:]:
        raw.start()
    gradients_of(vp, grads, 0, half)
    for k, share in enumerate(shares):
        share.wait_recv()
    total = buf1[0]
    for k in range(1, views):
        total = total + buf1[k]
    buf2[2] = jnp.where(row < 12, total, 0.0)
    buf2[2, 12:13, 0:12] = start_affine[...]
    passes = [
        remote(buf2.at[2], buf2.at[2 - k], s2.at[i], r2.at[i], dev(tile_at(k), v)) for i, k in enumerate(tile_steps)
    ]
    for k, passed in zip(tile_steps, passes):
        when_tile(k, passed.start)
    gradients_of(vp, grads, half, height)
    across = coordinate(iota((8, width), 1), width)
    facing = 1.0 - 2.0 * lax.rem(v, 2).astype(F32)

    def plane_weights(z, _):
        xk[z, 3] = (0.2 + (1.0 + facing * across) * 0.5) * (gain[0, 0] * (1.5 + facing * coordinate(z, depth)))
        return 0

    lax.fori_loop(0, depth, plane_weights, 0)
    for side, plane, source in ((0, down_view, up_view), (1, up_view, down_view)):
        g = jnp.concatenate([jnp.broadcast_to(buf1[source, 13:14, :], (8, 128))] * lanes, axis=1)
        wraw[side] = (0.2 + (1.0 - facing * across) * 0.5) * (g * (1.5 - facing * coordinate(plane, depth)))

    zf = coordinate(v, depth)
    weights = jnp.zeros((8, width), F32)
    for k in range(views):
        s = 1.0 - 2.0 * (k % 2)
        g = jnp.concatenate([jnp.broadcast_to(buf1[k, 13:14, :], (8, 128))] * lanes, axis=1)
        weights = weights + g * (1.5 + s * zf) * (0.2 + (1.0 + s * across) * 0.5)
    inverse = 1.0 / weights

    for k, passed in zip(tile_steps, passes):
        when_tile(-k, passed.wait_recv)

    inside = (row < 12) & (lane < 12)
    blocks = [buf2[k] for k in range(5)]
    below2, below, here, above = [jnp.where(inside, blocks[k + 1], 0.0) for k in range(4)]
    eye = jnp.where((row == lane) & (row < 12), 1.0, 0.0).astype(F32)

    def column(a, k):
        return jnp.broadcast_to(a[:, k : k + 1], (16, 128))

    def lane_sum(a):
        return jnp.broadcast_to(jnp.sum(a, axis=1, keepdims=True), (16, 128))

    def as_row(col):
        return jnp.broadcast_to(jnp.sum(col * eye, axis=0, keepdims=True), (16, 128))

    q = [column(blocks[k + 1], 12) + column(blocks[k], 13) for k in range(4)]
    starts = [jnp.broadcast_to(blocks[k][12:13, :], (16, 128)) for k in range(5)]
    stiff = eye * (STIFFNESS_FACTOR * depth * SLAB * width * views)
    right_up = lane_sum(above * starts[4] + here * starts[2] + stiff * starts[3]) - q[3] + q[2]
    right_down = lane_sum(below * starts[2] + below2 * starts[0] + stiff * starts[1]) - q[1] + q[0]
    right_own = lane_sum(stiff * starts[2]) - q[2] + q[1]
    real = row < 12
    up = jnp.where((lane == 12) & real, right_up, above + here + stiff)
    down = jnp.where((lane == 12) & real, right_down, below + below2 + stiff)
    own = here + below + stiff + pltpu.roll(here, 12, 1) + pltpu.roll(below, 24, 1)
    own = jnp.where((lane == 36) & real, right_own, own)
    systems = [up, down, own]
    for k in range(12):
        for i in range(3):
            a = systems[i]
            col = column(a, k)
            scaled = jnp.broadcast_to(a[k : k + 1, :] / col[k : k + 1, :], (16, 128))
            systems[i] = jnp.where(row == k, scaled, a - col * scaled)
    up, down, own = systems
    first_up, first_down = as_row(column(up, 12)), as_row(column(down, 12))
    mix = pltpu.roll(first_up, 12, 1) + pltpu.roll(first_down, 24, 1) + jnp.where(lane == 36, 1.0, 0.0)
    params = lane_sum(own * mix)
    pcol[...] = params
    refined[...] = as_row(params)[0:1, 0:12]

    def entry(k, j):
        return jnp.broadcast_to(pcol[4 * k + j : 4 * k + j + 1, :], (8, 128))

    def entry_row(k, j):
        return jnp.concatenate([entry(k, j)] * lanes, axis=1)

    def tables(z, _):
        zf = coordinate(z, depth)
        for k in range(3):
            xk[z, k] = entry_row(k, 0) * zf + entry_row(k, 3) + entry_row(k, 2) * across
        return 0

    lax.fori_loop(0, depth, tables, 0)
    slopes = [entry_row(k, 1) for k in range(3)]
    sub_row = iota((8, width), 0)

    def numerator_rows(z, first, dst, dst_first, extra, scale):
        def body(rb, _):
            r = pl.multiple_of(first + rb * 8, 8)
            d = pl.multiple_of(dst_first + rb * 8, 8)
            yv = coordinate(sub_row + r, height)
            value = vp[z, pl.ds(pl.multiple_of(PAD + r, 8), 8), :]
            for k in range(3):
                value = value + grads[k, z, pl.ds(r, 8), :] * (xk[z, k] + slopes[k] * yv)
            value = value * xk[z, 3]
            for stream in extra:
                value = value + rcv[stream, pl.ds(d, 8), :]
            if scale is not None:
                value = value * scale
            dst(d, value)
            return 0

        lax.fori_loop(0, CHUNK // 8, body, 0)

    def hop(stream, c):
        rows = pl.ds(pl.multiple_of(c * CHUNK, CHUNK), CHUNK)
        target = down_view if stream % 2 == 0 else up_view
        return remote(
            snd.at[stream, rows], rcv.at[stream, rows], ssem.at[stream, c], rsem.at[stream, c], dev(t, target)
        )

    def send_chunk(stream, c, plane, upper, extra=()):
        def put(d, value):
            snd[stream, pl.ds(d, 8), :] = value

        c_row = pl.multiple_of(c * CHUNK, CHUNK)
        numerator_rows(plane, (half if upper else 0) + c_row, put, c_row, extra, None)
        hop(stream, c).start()

    def relay_raw(side, c):
        plane = (down_view, up_view)[side]
        stream = 4 + side
        c_row = pl.multiple_of(c * CHUNK, CHUNK)

        def body(rb, _):
            d = pl.multiple_of(c_row + rb * 8, 8)
            r = pl.multiple_of(side * half + d, 8)
            yv = coordinate(sub_row + r, height)
            shifts = [xk[plane, k] + slopes[k] * yv for k in range(3)]
            value = vp[plane, pl.ds(pl.multiple_of(PAD + r, 8), 8), :]
            for k in range(3):
                value = value + grads[k, plane, pl.ds(r, 8), :] * shifts[k]
            before, here_v, after = [rawv[side, pl.ds(pl.multiple_of(d + k * PAD, 8), 8), :] for k in range(3)]
            other = here_v + rawg[side, pl.ds(d, 8), :] * shifts[0]
            other = other + y_gradient(before, here_v, after) * shifts[1] + x_gradient(here_v) * shifts[2]
            snd[stream, pl.ds(d, 8), :] = value * xk[plane, 3] + other * wraw[side]
            return 0

        lax.fori_loop(0, CHUNK // 8, body, 0)
        hop(stream, c).start()

    def far(c, _):
        send_chunk(0, c, far_view, False)
        send_chunk(1, c, far_view, True)
        return 0

    def near_planes(c, _):
        send_chunk(2, c, down_view, True)
        send_chunk(3, c, up_view, False)
        return 0

    def relay(c, _):
        hop(0, c).wait_recv()
        send_chunk(4, c, down_view, False, (0,))
        hop(1, c).wait_recv()
        send_chunk(5, c, up_view, True, (1,))
        return 0

    def relay_both(c, _):
        relay_raw(0, c)
        relay_raw(1, c)
        return 0

    lax.fori_loop(RAW_CHUNKS, chunks, far, 0)
    lax.fori_loop(0, chunks, near_planes, 0)
    for raw in raws:
        raw.wait_recv()
    rawv[0, PAD - 1 : PAD, :] = 2.0 * rawv[0, PAD : PAD + 1, :] - rawv[0, PAD + 1 : PAD + 2, :]
    lax.fori_loop(0, RAW_CHUNKS, relay_both, 0)
    lax.fori_loop(RAW_CHUNKS, chunks, relay, 0)

    def finish(c, _):
        c_row = pl.multiple_of(c * CHUNK, CHUNK)
        for part, streams in ((0, (3, 4)), (1, (2, 5))):
            for stream in streams:
                hop(stream, c).wait_recv()

            def put(d, value, part=part):
                out[0, 0, pl.ds(pl.multiple_of(part * half + d, 8), 8), :] = value

            numerator_rows(v, part * half + c_row, put, c_row, streams, inverse)
        return 0

    lax.fori_loop(0, chunks, finish, 0)

    def drain(c, _):
        for stream in range(2, 6):
            hop(stream, c).wait_send()
        return 0

    def drain_far(c, _):
        hop(0, c).wait_send()
        hop(1, c).wait_send()
        return 0

    lax.fori_loop(0, chunks, drain, 0)
    lax.fori_loop(RAW_CHUNKS, chunks, drain_far, 0)
    when_tile(1, send_margin.wait_send)
    when_tile(1, send_near.wait_send)
    for send_window in send_windows:
        when_tile(-1, send_window.wait_send)
    for k, passed in zip(tile_steps, passes):
        when_tile(k, passed.wait_send)
    for copy in shares + raws:
        copy.wait_send()


def on_device(tiles, views, volumes, initial_affine, slab_start, margin_rows, view_gain):
    depth, height, width = volumes.shape[2:]
    half = height // 2
    chunks = half // CHUNK
    smem = pl.BlockSpec(memory_space=pltpu.SMEM)
    vmem = pl.BlockSpec(memory_space=pltpu.VMEM)
    dma = pltpu.SemaphoreType.DMA
    return pl.pallas_call(
        functools.partial(kernel, tiles, views),
        out_shape=(jax.ShapeDtypeStruct((1, 1, height, width), F32), jax.ShapeDtypeStruct((1, 12), F32)),
        in_specs=[pl.BlockSpec(memory_space=pltpu.HBM), pl.BlockSpec(memory_space=pltpu.HBM), smem, smem, smem],
        out_specs=(vmem, vmem),
        scratch_shapes=[
            pltpu.VMEM((depth, height + 2 * PAD, width), F32),
            pltpu.VMEM((3, depth, height, width), F32),
            pltpu.VMEM((depth, SLAB + 2 * PAD, width), F32),
            pltpu.VMEM((3, depth, SLAB, width), F32),
            pltpu.VMEM((depth, SENT_ROWS + PAD, width), F32),
            pltpu.VMEM((3, depth, FIRST_ROWS, width), F32),
            pltpu.VMEM((depth, REST_ROWS, width), F32),
            pltpu.VMEM((8, 128), jnp.int32),
            pltpu.VMEM((8, 128), jnp.int32),
            pltpu.VMEM((1, 12), F32),
            pltpu.VMEM((6, 10, 8, 128), F32),
            pltpu.VMEM((2, 12, 8, 128), F32),
            pltpu.VMEM((14, 16, 128), F32),
            pltpu.VMEM((views, 16, 128), F32),
            pltpu.VMEM((5, 16, 128), F32),
            pltpu.VMEM((16, 128), F32),
            pltpu.VMEM((depth, 4, 8, width), F32),
            pltpu.VMEM((6, half, width), F32),
            pltpu.VMEM((6, half, width), F32),
            pltpu.VMEM((2, RAW_CHUNKS * CHUNK + 2 * PAD, width), F32),
            pltpu.VMEM((2, RAW_CHUNKS * CHUNK, width), F32),
            pltpu.VMEM((2, 8, width), F32),
            dma((depth + 1,)), dma((2,)), dma((2, depth)), dma((2,)),
            dma((views - 1,)), dma((views - 1,)), dma((4,)), dma((4,)),
            dma((6, chunks)), dma((6, chunks)), dma((2, 8)),
        ],
        compiler_params=pltpu.CompilerParams(
            collective_id=0, has_side_effects=True, vmem_limit_bytes=52 * 1024 * 1024
        ),
        name="refine_and_join",
    )(
        pltpu.with_memory_space_constraint(volumes, pltpu.HBM),
        pltpu.with_memory_space_constraint(initial_affine, pltpu.HBM),
        slab_start,
        margin_rows,
        view_gain,
    )


def solution(mesh):
    placed = (
        P("tile", "view", None, None, None),
        P("tile", None),
        P("tile"),
        P("tile"),
        P("tile", "view"),
    )
    return jax.shard_map(
        functools.partial(on_device, mesh.shape["tile"], mesh.shape["view"]),
        mesh=mesh,
        in_specs=placed,
        out_specs=(P("tile", "view", None, None), P("tile", None)),
        check_vma=False,
    )
```

```python
import functools

import jax
import jax.numpy as jnp
from jax import lax
from jax.experimental import pallas as pl
from jax.experimental.pallas import tpu as pltpu
from jax.sharding import PartitionSpec as P

MESH = pl.DeviceIdType.MESH
F32 = jnp.float32
SLAB = 64
FIRST_ROWS = 16
REST_ROWS = SLAB - FIRST_ROWS
SENT_ROWS = FIRST_ROWS + 8
STIFFNESS_FACTOR = 0.25
PAD = 8
CHUNK = 32
RAW_CHUNKS = 5
EARLY_ROWS = 80
PAIRS = ((0, 0), (0, 1), (0, 2), (1, 1), (1, 2), (2, 2))
MONOS = ((0, 0), (0, 1), (0, 2), (0, 3), (1, 1), (1, 2), (1, 3), (2, 2), (2, 3), (3, 3))


def iota(shape, dim):
    return lax.broadcasted_iota(jnp.int32, shape, dim)


def coordinate(index, count):
    return (index.astype(F32) + 0.5) * (2.0 / count) - 1.0


def x_gradient(a):
    width = a.shape[-1]
    left = pltpu.roll(a, 1, 1)
    right = pltpu.roll(a, width - 1, 1)
    lane = iota(a.shape, 1)
    inner = (right - left) * 0.5
    return jnp.where(lane == 0, right - a, jnp.where(lane == width - 1, a - left, inner))


def y_gradient(before, a, after):
    top, bottom = iota(a.shape, 0) == 0, iota(a.shape, 0) == 7
    upper = jnp.where(bottom, pltpu.roll(after, 7, 0), pltpu.roll(a, 7, 0))
    lower = jnp.where(top, pltpu.roll(before, 1, 0), pltpu.roll(a, 1, 0))
    return (upper - lower) * 0.5


def z_gradients(p):
    n = len(p)
    inner = [(p[z + 1] - p[z - 1]) * 0.5 for z in range(1, n - 1)]
    return [p[1] - p[0]] + inner + [p[n - 1] - p[n - 2]]


def kernel(
    tiles, views,
    vol, aff, slab, margin, gain, out, refined,
    vp, grads, wst, wgrad, wrx, wrx_grad, nrx, mown, mlow, start_affine, hacc, qacc, cols, buf1, buf2, pcol, xk, snd, rcv, rawv, rawg, wraw,
    vsem, msem, wsem, nsem, s1, r1, s2, r2, ssem, rsem, rawsem,
):
    depth, height, width = vol.shape[2:]
    lanes = width // 128
    half = height // 2
    chunks = half // CHUNK
    t = lax.axis_index("tile")
    v = lax.axis_index("view")

    def tile_at(k):
        return lax.rem(t + tiles + k, tiles)

    def view_at(k):
        return lax.rem(v + views + k, views)

    def exists(k):
        return t + k >= 0 if k < 0 else t + k < tiles

    def when_tile(k, action):
        pl.when(exists(k))(action)

    def dev(tile, view):
        return {"tile": tile, "view": view}

    def remote(src, dst, send, recv, device):
        return pltpu.make_async_remote_copy(
            src_ref=src, dst_ref=dst, send_sem=send, recv_sem=recv, device_id=device, device_id_type=MESH
        )

    loads = [pltpu.make_async_copy(vol.at[0, 0, z], vp.at[z, pl.ds(PAD, height)], vsem.at[z]) for z in range(depth)]
    loads.append(pltpu.make_async_copy(aff, start_affine, vsem.at[depth]))
    for load in loads:
        load.start()
    barrier = pltpu.get_barrier_semaphore()
    buf2[...] = jnp.zeros_like(buf2)
    tile_steps = (-2, -1, 1, 2)

    def greet(device):
        pl.semaphore_signal(barrier, inc=1, device_id=device, device_id_type=MESH)

    for k in tile_steps:
        when_tile(k, functools.partial(greet, dev(tile_at(k), v)))
    for k in range(1, views):
        greet(dev(t, view_at(k)))
    mown[...] = jnp.full((8, 128), margin[0], jnp.int32)
    hacc[...] = jnp.zeros_like(hacc)
    qacc[...] = jnp.zeros_like(qacc)
    cols[...] = jnp.zeros_like(cols)
    peers = views - 1
    for k in tile_steps:
        peers = peers + jnp.where(exists(k), 1, 0)
    pl.semaphore_wait(barrier, peers)
    send_margin = remote(mown, mlow, msem.at[0], msem.at[1], dev(tile_at(1), v))
    when_tile(1, send_margin.start)
    send_near = remote(
        vol.at[0, 0, :, pl.ds(height - REST_ROWS, REST_ROWS)], nrx, nsem.at[0], nsem.at[1], dev(tile_at(1), v)
    )
    when_tile(1, send_near.start)

    down_view, up_view, far_view = view_at(-1), view_at(1), view_at(2)
    raws = []
    for part, (first, end) in enumerate(((0, EARLY_ROWS), (EARLY_ROWS, RAW_CHUNKS * CHUNK))):
        for side, target in ((0, down_view), (1, up_view)):
            begin = first + PAD if part else first - side * PAD
            source = vol.at[0, 0, far_view, pl.ds(side * half + begin, end + PAD - begin)]
            landing = rawv.at[side, pl.ds(PAD + begin, end + PAD - begin)]
            raws.append(remote(source, landing, rawsem.at[0, 4 * part + side], rawsem.at[1, 4 * part + side], dev(t, target)))
        for side, target in ((0, down_view), (1, up_view)):
            sems = [rawsem.at[k, 4 * part + 2 + side] for k in range(2)]
            rows = pl.ds(side * half + first, end - first)
            raws.append(
                remote(grads.at[0, far_view, rows], rawg.at[side, pl.ds(first, end - first)], *sems, dev(t, target))
            )
    for raw in raws[:2]:
        raw.start()
    start = slab[0]
    aligned = lax.div(start, 8) * 8
    shift = jnp.full((SLAB + 8, width), start - aligned, jnp.int32)
    moves = [(k, lax.bitwise_and(shift, k) != 0) for k in (1, 2, 4)]
    for load in loads:
        load.wait()
    send_windows = []
    for z in range(depth):
        rows = vp[z, pl.ds(aligned + PAD, SLAB + 8), :]
        for k, moved in moves:
            rows = jnp.where(moved, pltpu.roll(rows, SLAB + 8 - k, 0), rows)
        wst[z, PAD : PAD + SLAB, :] = rows[:SLAB]
        sent = pl.ds(PAD, SENT_ROWS)
        send_windows.append(
            remote(wst.at[z, sent], wrx.at[z, sent], wsem.at[0, z], wsem.at[1, z], dev(tile_at(-1), v))
        )
        when_tile(-1, send_windows[z].start)
    for z in range(depth):
        vp[z, PAD - 1 : PAD, :] = 2.0 * vp[z, PAD : PAD + 1, :] - vp[z, PAD + 1 : PAD + 2, :]
        last = PAD + height - 1
        vp[z, last + 1 : last + 2, :] = 2.0 * vp[z, last : last + 1, :] - vp[z, last - 1 : last, :]

    def depth_gradients_of(src, dst, count):
        def body(r, _):
            r = pl.multiple_of(r * 8, 8)
            planes = [src[z, pl.ds(pl.multiple_of(PAD + r, 8), 8), :] for z in range(depth)]
            for z, g in enumerate(z_gradients(planes)):
                dst[0, z, pl.ds(r, 8), :] = g
            return 0

        lax.fori_loop(0, count // 8, body, 0)

    depth_gradients_of(vp, grads, height)

    for raw in raws[2:4]:
        raw.start()

    for z in range(depth):
        wst[z, PAD - 1 : PAD, :] = 2.0 * wst[z, PAD : PAD + 1, :] - wst[z, PAD + 1 : PAD + 2, :]
        last = PAD + SLAB - 1
        wst[z, last + 1 : last + 2, :] = 2.0 * wst[z, last : last + 1, :] - wst[z, last - 1 : last, :]

    def gradients_of(src, dst, first, end):
        def body(r, _):
            r = pl.multiple_of(r * 8, 8)
            planes = [src[z, pl.ds(PAD + r, 8), :] for z in range(depth)]
            for z in range(depth):
                before, after = src[z, pl.ds(r, 8), :], src[z, pl.ds(2 * PAD + r, 8), :]
                dst[1, z, pl.ds(r, 8), :] = y_gradient(before, planes[z], after)
                dst[2, z, pl.ds(r, 8), :] = x_gradient(planes[z])
            return 0

        lax.fori_loop(first // 8, end // 8, body, 0)

    depth_gradients_of(wst, wgrad, SLAB)
    gradients_of(wst, wgrad, 0, SLAB)

    zc = [(z + 0.5) / depth * 2.0 - 1.0 for z in range(depth)]

    def depth_sum(fields, power):
        return functools.reduce(lambda a, b: a + b, [f * (c**power) if power else f for f, c in zip(fields, zc)])

    sub = iota((8, 128), 0)
    lane8 = iota((8, 128), 1)

    def gradients_at(srcg, r, xs, mask):
        return [[srcg[k, z, pl.ds(r, 8), xs] * mask for z in range(depth)] for k in range(3)]

    def row_coordinate(r):
        return coordinate(sub + (r + height - SLAB), height)

    when_tile(-1, send_margin.wait_recv)
    low_rows = mlow[...]
    own_rows = mown[...]

    def matrix_lanes(xl, _):
        xs = pl.ds(pl.multiple_of(xl * 128, 128), 128)
        xv = coordinate(lane8 + xl * 128, width)

        def body(yb, carry):
            r = pl.multiple_of(yb * 8, 8)
            mask = jnp.where(sub + r < low_rows, 1.0, 0.0).astype(F32)
            g = gradients_at(wgrad, r, xs, mask)
            yv = row_coordinate(r)
            new = []
            for f, (a, b) in enumerate(PAIRS):
                fields = [g[a][z] * g[b][z] for z in range(depth)]
                p0, p1, p2 = (depth_sum(fields, k) for k in range(3))
                yp = yv * p0
                terms = (p2, yv * p1, p1, yv * yp, yp, p0)
                new += [c + term for c, term in zip(carry[6 * f : 6 * f + 6], terms)]
            return tuple(new)

        sums = lax.fori_loop(0, SLAB // 8, body, tuple(jnp.zeros((8, 128), F32) for _ in range(36)))
        for f in range(6):
            zz, zy, zo, yy, yo, oo = sums[6 * f : 6 * f + 6]
            xo = xv * oo
            for m, term in enumerate((zz, zy, xv * zo, zo, yy, xv * yo, yo, xv * xo, xo, oo)):
                hacc[f, m] += term
        return 0

    lax.fori_loop(0, lanes, matrix_lanes, 0)
    for f, (a, b) in enumerate(PAIRS):
        for m, (i, j) in enumerate(MONOS):
            row = jnp.sum(hacc[f, m], axis=0, keepdims=True)
            for p, q in {(4 * a + i, 4 * b + j), (4 * a + j, 4 * b + i), (4 * b + i, 4 * a + j), (4 * b + j, 4 * a + i)}:
                cols[p, q : q + 1, :] = row

    def moment(part, src, srcg, first, count, rows, near):
        def lane_block(xl, _):
            xs = pl.ds(pl.multiple_of(xl * 128, 128), 128)
            xv = coordinate(lane8 + xl * 128, width)

            def body(yb, carry):
                r = pl.multiple_of(yb * 8, 8)
                mask = jnp.where(sub + (r + first) < rows, 1.0, 0.0).astype(F32)
                g = gradients_at(srcg, pl.multiple_of(r + first, 8), xs, mask)
                window = [src[z, pl.ds(pl.multiple_of(PAD + first + r, 8), 8), xs] for z in range(depth)]
                residual = [near(z, r, xs) - window[z] for z in range(depth)]
                yv = row_coordinate(r + first)
                new = []
                for k in range(3):
                    fields = [g[k][z] * residual[z] for z in range(depth)]
                    p0, p1 = depth_sum(fields, 0), depth_sum(fields, 1)
                    new += [c + term for c, term in zip(carry[3 * k : 3 * k + 3], (p1, yv * p0, p0))]
                return tuple(new)

            sums = lax.fori_loop(0, count // 8, body, tuple(jnp.zeros((8, 128), F32) for _ in range(9)))
            for k in range(3):
                zo, yo, oo = sums[3 * k : 3 * k + 3]
                for j, term in enumerate((zo, yo, xv * oo, oo)):
                    qacc[part, 4 * k + j] += term
            return 0

        lax.fori_loop(0, lanes, lane_block, 0)
        for i in range(12):
            cols[12 + part, i : i + 1, :] = jnp.sum(qacc[part, i], axis=0, keepdims=True)

    row = iota((16, 128), 0)
    lane = iota((16, 128), 1)
    tile_index = row * 0 + t
    has_low, has_next = tile_index > 0, tile_index < tiles - 1
    block = jnp.zeros((16, 128), F32)

    def placed(block, c):
        total = jnp.sum(cols[c], axis=1, keepdims=True)
        return jnp.where((lane == c) & (has_next if c == 13 else has_low), total, block)

    for c in range(12):
        block = placed(block, c)
    when_tile(-1, send_near.wait_recv)
    moment(0, wst, wgrad, FIRST_ROWS, REST_ROWS, low_rows, lambda z, r, xs: nrx[z, pl.ds(r, 8), xs])
    for send_window in send_windows:
        when_tile(1, send_window.wait_recv)
    for z in range(depth):
        wrx[z, PAD - 1 : PAD, :] = 2.0 * wrx[z, PAD : PAD + 1, :] - wrx[z, PAD + 1 : PAD + 2, :]
    depth_gradients_of(wrx, wrx_grad, FIRST_ROWS)
    gradients_of(wrx, wrx_grad, 0, FIRST_ROWS)
    moment(1, wrx, wrx_grad, 0, FIRST_ROWS, own_rows, lambda z, r, xs: vp[z, pl.ds(PAD + height - SLAB + r, 8), xs])

    block = placed(block, 12)
    block = placed(block, 13)
    buf1[v] = block
    buf1[v, 13:14, :] = jnp.full((1, 128), gain[0, 0], F32)
    shares = [
        remote(buf1.at[v], buf1.at[v], s1.at[k - 1], r1.at[k - 1], dev(t, view_at(k))) for k in range(1, views)
    ]
    for share in shares:
        share.start()
    for raw in raws[4:]:
        raw.start()
    gradients_of(vp, grads, 0, half)
    for k, share in enumerate(shares):
        share.wait_recv()
    total = buf1[0]
    for k in range(1, views):
        total = total + buf1[k]
    buf2[2] = jnp.where(row < 12, total, 0.0)
    buf2[2, 12:13, 0:12] = start_affine[...]
    passes = [
        remote(buf2.at[2], buf2.at[2 - k], s2.at[i], r2.at[i], dev(tile_at(k), v)) for i, k in enumerate(tile_steps)
    ]
    for k, passed in zip(tile_steps, passes):
        when_tile(k, passed.start)
    gradients_of(vp, grads, half, height)
    across = coordinate(iota((8, width), 1), width)
    facing = 1.0 - 2.0 * lax.rem(v, 2).astype(F32)

    def plane_weights(z, _):
        xk[z, 3] = (0.2 + (1.0 + facing * across) * 0.5) * (gain[0, 0] * (1.5 + facing * coordinate(z, depth)))
        return 0

    lax.fori_loop(0, depth, plane_weights, 0)
    for side, plane, source in ((0, down_view, up_view), (1, up_view, down_view)):
        g = jnp.concatenate([jnp.broadcast_to(buf1[source, 13:14, :], (8, 128))] * lanes, axis=1)
        wraw[side] = (0.2 + (1.0 - facing * across) * 0.5) * (g * (1.5 - facing * coordinate(plane, depth)))

    zf = coordinate(v, depth)
    weights = jnp.zeros((8, width), F32)
    for k in range(views):
        s = 1.0 - 2.0 * (k % 2)
        g = jnp.concatenate([jnp.broadcast_to(buf1[k, 13:14, :], (8, 128))] * lanes, axis=1)
        weights = weights + g * (1.5 + s * zf) * (0.2 + (1.0 + s * across) * 0.5)
    inverse = 1.0 / weights

    for k, passed in zip(tile_steps, passes):
        when_tile(-k, passed.wait_recv)

    inside = (row < 12) & (lane < 12)
    blocks = [buf2[k] for k in range(5)]
    below2, below, here, above = [jnp.where(inside, blocks[k + 1], 0.0) for k in range(4)]
    eye = jnp.where((row == lane) & (row < 12), 1.0, 0.0).astype(F32)

    def column(a, k):
        return jnp.broadcast_to(a[:, k : k + 1], (16, 128))

    def lane_sum(a):
        return jnp.broadcast_to(jnp.sum(a, axis=1, keepdims=True), (16, 128))

    def as_row(col):
        return jnp.broadcast_to(jnp.sum(col * eye, axis=0, keepdims=True), (16, 128))

    q = [column(blocks[k + 1], 12) + column(blocks[k], 13) for k in range(4)]
    starts = [jnp.broadcast_to(blocks[k][12:13, :], (16, 128)) for k in range(5)]
    stiff = eye * (STIFFNESS_FACTOR * depth * SLAB * width * views)
    right_up = lane_sum(above * starts[4] + here * starts[2] + stiff * starts[3]) - q[3] + q[2]
    right_down = lane_sum(below * starts[2] + below2 * starts[0] + stiff * starts[1]) - q[1] + q[0]
    right_own = lane_sum(stiff * starts[2]) - q[2] + q[1]
    real = row < 12
    up = jnp.where((lane == 12) & real, right_up, above + here + stiff)
    down = jnp.where((lane == 12) & real, right_down, below + below2 + stiff)
    own = here + below + stiff + pltpu.roll(here, 12, 1) + pltpu.roll(below, 24, 1)
    own = jnp.where((lane == 36) & real, right_own, own)
    systems = [up, down, own]
    for k in range(12):
        for i in range(3):
            a = systems[i]
            col = column(a, k)
            scaled = jnp.broadcast_to(a[k : k + 1, :] / col[k : k + 1, :], (16, 128))
            systems[i] = jnp.where(row == k, scaled, a - col * scaled)
    up, down, own = systems
    first_up, first_down = as_row(column(up, 12)), as_row(column(down, 12))
    mix = pltpu.roll(first_up, 12, 1) + pltpu.roll(first_down, 24, 1) + jnp.where(lane == 36, 1.0, 0.0)
    params = lane_sum(own * mix)
    pcol[...] = params
    refined[...] = as_row(params)[0:1, 0:12]

    def entry(k, j):
        return jnp.broadcast_to(pcol[4 * k + j : 4 * k + j + 1, :], (8, 128))

    def entry_row(k, j):
        return jnp.concatenate([entry(k, j)] * lanes, axis=1)

    def tables(z, _):
        zf = coordinate(z, depth)
        for k in range(3):
            xk[z, k] = entry_row(k, 0) * zf + entry_row(k, 3) + entry_row(k, 2) * across
        return 0

    lax.fori_loop(0, depth, tables, 0)
    slopes = [entry_row(k, 1) for k in range(3)]
    sub_row = iota((8, width), 0)

    def numerator_rows(z, first, dst, dst_first, extra, scale):
        def body(rb, _):
            r = pl.multiple_of(first + rb * 8, 8)
            d = pl.multiple_of(dst_first + rb * 8, 8)
            yv = coordinate(sub_row + r, height)
            value = vp[z, pl.ds(pl.multiple_of(PAD + r, 8), 8), :]
            for k in range(3):
                value = value + grads[k, z, pl.ds(r, 8), :] * (xk[z, k] + slopes[k] * yv)
            value = value * xk[z, 3]
            for stream in extra:
                value = value + rcv[stream, pl.ds(d, 8), :]
            if scale is not None:
                value = value * scale
            dst(d, value)
            return 0

        lax.fori_loop(0, CHUNK // 8, body, 0)

    def hop(stream, c):
        rows = pl.ds(pl.multiple_of(c * CHUNK, CHUNK), CHUNK)
        target = down_view if stream % 2 == 0 else up_view
        return remote(
            snd.at[stream, rows], rcv.at[stream, rows], ssem.at[stream, c], rsem.at[stream, c], dev(t, target)
        )

    def send_chunk(stream, c, plane, upper, extra=()):
        def put(d, value):
            snd[stream, pl.ds(d, 8), :] = value

        c_row = pl.multiple_of(c * CHUNK, CHUNK)
        numerator_rows(plane, (half if upper else 0) + c_row, put, c_row, extra, None)
        hop(stream, c).start()

    def relay_raw(side, c):
        plane = (down_view, up_view)[side]
        stream = 4 + side
        c_row = pl.multiple_of(c * CHUNK, CHUNK)

        def body(rb, _):
            d = pl.multiple_of(c_row + rb * 8, 8)
            r = pl.multiple_of(side * half + d, 8)
            yv = coordinate(sub_row + r, height)
            shifts = [xk[plane, k] + slopes[k] * yv for k in range(3)]
            value = vp[plane, pl.ds(pl.multiple_of(PAD + r, 8), 8), :]
            for k in range(3):
                value = value + grads[k, plane, pl.ds(r, 8), :] * shifts[k]
            before, here_v, after = [rawv[side, pl.ds(pl.multiple_of(d + k * PAD, 8), 8), :] for k in range(3)]
            other = here_v + rawg[side, pl.ds(d, 8), :] * shifts[0]
            other = other + y_gradient(before, here_v, after) * shifts[1] + x_gradient(here_v) * shifts[2]
            snd[stream, pl.ds(d, 8), :] = value * xk[plane, 3] + other * wraw[side]
            return 0

        lax.fori_loop(0, CHUNK // 8, body, 0)
        hop(stream, c).start()

    def far(c, _):
        send_chunk(0, c, far_view, False)
        send_chunk(1, c, far_view, True)
        return 0

    def near_planes(c, _):
        send_chunk(2, c, down_view, True)
        send_chunk(3, c, up_view, False)
        return 0

    def relay(c, _):
        hop(0, c).wait_recv()
        send_chunk(4, c, down_view, False, (0,))
        hop(1, c).wait_recv()
        send_chunk(5, c, up_view, True, (1,))
        return 0

    def relay_both(c, _):
        relay_raw(0, c)
        relay_raw(1, c)
        return 0

    lax.fori_loop(RAW_CHUNKS, chunks, far, 0)
    lax.fori_loop(0, chunks, near_planes, 0)
    for raw in raws:
        raw.wait_recv()
    rawv[0, PAD - 1 : PAD, :] = 2.0 * rawv[0, PAD : PAD + 1, :] - rawv[0, PAD + 1 : PAD + 2, :]
    lax.fori_loop(0, RAW_CHUNKS, relay_both, 0)
    lax.fori_loop(RAW_CHUNKS, chunks, relay, 0)

    def finish(c, _):
        c_row = pl.multiple_of(c * CHUNK, CHUNK)
        for part, streams in ((0, (3, 4)), (1, (2, 5))):
            for stream in streams:
                hop(stream, c).wait_recv()

            def put(d, value, part=part):
                out[0, 0, pl.ds(pl.multiple_of(part * half + d, 8), 8), :] = value

            numerator_rows(v, part * half + c_row, put, c_row, streams, inverse)
        return 0

    lax.fori_loop(0, chunks, finish, 0)

    def drain(c, _):
        for stream in range(2, 6):
            hop(stream, c).wait_send()
        return 0

    def drain_far(c, _):
        hop(0, c).wait_send()
        hop(1, c).wait_send()
        return 0

    lax.fori_loop(0, chunks, drain, 0)
    lax.fori_loop(RAW_CHUNKS, chunks, drain_far, 0)
    when_tile(1, send_margin.wait_send)
    when_tile(1, send_near.wait_send)
    for send_window in send_windows:
        when_tile(-1, send_window.wait_send)
    for k, passed in zip(tile_steps, passes):
        when_tile(k, passed.wait_send)
    for copy in shares + raws:
        copy.wait_send()


def on_device(tiles, views, volumes, initial_affine, slab_start, margin_rows, view_gain):
    depth, height, width = volumes.shape[2:]
    half = height // 2
    chunks = half // CHUNK
    smem = pl.BlockSpec(memory_space=pltpu.SMEM)
    vmem = pl.BlockSpec(memory_space=pltpu.VMEM)
    dma = pltpu.SemaphoreType.DMA
    return pl.pallas_call(
        functools.partial(kernel, tiles, views),
        out_shape=(jax.ShapeDtypeStruct((1, 1, height, width), F32), jax.ShapeDtypeStruct((1, 12), F32)),
        in_specs=[pl.BlockSpec(memory_space=pltpu.HBM), pl.BlockSpec(memory_space=pltpu.HBM), smem, smem, smem],
        out_specs=(vmem, vmem),
        scratch_shapes=[
            pltpu.VMEM((depth, height + 2 * PAD, width), F32),
            pltpu.VMEM((3, depth, height, width), F32),
            pltpu.VMEM((depth, SLAB + 2 * PAD, width), F32),
            pltpu.VMEM((3, depth, SLAB, width), F32),
            pltpu.VMEM((depth, SENT_ROWS + PAD, width), F32),
            pltpu.VMEM((3, depth, FIRST_ROWS, width), F32),
            pltpu.VMEM((depth, REST_ROWS, width), F32),
            pltpu.VMEM((8, 128), jnp.int32),
            pltpu.VMEM((8, 128), jnp.int32),
            pltpu.VMEM((1, 12), F32),
            pltpu.VMEM((6, 10, 8, 128), F32),
            pltpu.VMEM((2, 12, 8, 128), F32),
            pltpu.VMEM((14, 16, 128), F32),
            pltpu.VMEM((views, 16, 128), F32),
            pltpu.VMEM((5, 16, 128), F32),
            pltpu.VMEM((16, 128), F32),
            pltpu.VMEM((depth, 4, 8, width), F32),
            pltpu.VMEM((6, half, width), F32),
            pltpu.VMEM((6, half, width), F32),
            pltpu.VMEM((2, RAW_CHUNKS * CHUNK + 2 * PAD, width), F32),
            pltpu.VMEM((2, RAW_CHUNKS * CHUNK, width), F32),
            pltpu.VMEM((2, 8, width), F32),
            dma((depth + 1,)), dma((2,)), dma((2, depth)), dma((2,)),
            dma((views - 1,)), dma((views - 1,)), dma((4,)), dma((4,)),
            dma((6, chunks)), dma((6, chunks)), dma((2, 8)),
        ],
        compiler_params=pltpu.CompilerParams(
            collective_id=0, has_side_effects=True, vmem_limit_bytes=52 * 1024 * 1024
        ),
        name="refine_and_join",
    )(
        pltpu.with_memory_space_constraint(volumes, pltpu.HBM),
        pltpu.with_memory_space_constraint(initial_affine, pltpu.HBM),
        slab_start,
        margin_rows,
        view_gain,
    )


def solution(mesh):
    placed = (
        P("tile", "view", None, None, None),
        P("tile", None),
        P("tile"),
        P("tile"),
        P("tile", "view"),
    )
    return jax.shard_map(
        functools.partial(on_device, mesh.shape["tile"], mesh.shape["view"]),
        mesh=mesh,
        in_specs=placed,
        out_specs=(P("tile", "view", None, None), P("tile", None)),
        check_vma=False,
    )
```

```python
import functools

import jax
import jax.numpy as jnp
from jax import lax
from jax.experimental import pallas as pl
from jax.experimental.pallas import tpu as pltpu
from jax.sharding import PartitionSpec as P

MESH = pl.DeviceIdType.MESH
F32 = jnp.float32
SLAB = 64
FIRST_ROWS = 16
REST_ROWS = SLAB - FIRST_ROWS
SENT_ROWS = FIRST_ROWS + 8
STIFFNESS_FACTOR = 0.25
PAD = 8
CHUNK = 32
RAW_CHUNKS = 5
EARLY_ROWS = 72
PAIRS = ((0, 0), (0, 1), (0, 2), (1, 1), (1, 2), (2, 2))
MONOS = ((0, 0), (0, 1), (0, 2), (0, 3), (1, 1), (1, 2), (1, 3), (2, 2), (2, 3), (3, 3))


def iota(shape, dim):
    return lax.broadcasted_iota(jnp.int32, shape, dim)


def coordinate(index, count):
    return (index.astype(F32) + 0.5) * (2.0 / count) - 1.0


def x_gradient(a):
    width = a.shape[-1]
    left = pltpu.roll(a, 1, 1)
    right = pltpu.roll(a, width - 1, 1)
    lane = iota(a.shape, 1)
    inner = (right - left) * 0.5
    return jnp.where(lane == 0, right - a, jnp.where(lane == width - 1, a - left, inner))


def y_gradient(before, a, after):
    top, bottom = iota(a.shape, 0) == 0, iota(a.shape, 0) == 7
    upper = jnp.where(bottom, pltpu.roll(after, 7, 0), pltpu.roll(a, 7, 0))
    lower = jnp.where(top, pltpu.roll(before, 1, 0), pltpu.roll(a, 1, 0))
    return (upper - lower) * 0.5


def z_gradients(p):
    n = len(p)
    inner = [(p[z + 1] - p[z - 1]) * 0.5 for z in range(1, n - 1)]
    return [p[1] - p[0]] + inner + [p[n - 1] - p[n - 2]]


def kernel(
    tiles, views,
    vol, aff, slab, margin, gain, out, refined,
    vp, grads, wst, wgrad, wrx, wrx_grad, nrx, mown, mlow, start_affine, hacc, qacc, cols, buf1, buf2, pcol, xk, snd, rcv, rawv, rawg, wraw,
    vsem, msem, wsem, nsem, s1, r1, s2, r2, ssem, rsem, rawsem,
):
    depth, height, width = vol.shape[2:]
    lanes = width // 128
    half = height // 2
    chunks = half // CHUNK
    t = lax.axis_index("tile")
    v = lax.axis_index("view")

    def tile_at(k):
        return lax.rem(t + tiles + k, tiles)

    def view_at(k):
        return lax.rem(v + views + k, views)

    def exists(k):
        return t + k >= 0 if k < 0 else t + k < tiles

    def when_tile(k, action):
        pl.when(exists(k))(action)

    def dev(tile, view):
        return {"tile": tile, "view": view}

    def remote(src, dst, send, recv, device):
        return pltpu.make_async_remote_copy(
            src_ref=src, dst_ref=dst, send_sem=send, recv_sem=recv, device_id=device, device_id_type=MESH
        )

    loads = [pltpu.make_async_copy(vol.at[0, 0, z], vp.at[z, pl.ds(PAD, height)], vsem.at[z]) for z in range(depth)]
    loads.append(pltpu.make_async_copy(aff, start_affine, vsem.at[depth]))
    for load in loads:
        load.start()
    barrier = pltpu.get_barrier_semaphore()
    buf2[...] = jnp.zeros_like(buf2)
    tile_steps = (-2, -1, 1, 2)

    def greet(device):
        pl.semaphore_signal(barrier, inc=1, device_id=device, device_id_type=MESH)

    for k in tile_steps:
        when_tile(k, functools.partial(greet, dev(tile_at(k), v)))
    for k in range(1, views):
        greet(dev(t, view_at(k)))
    mown[...] = jnp.full((8, 128), margin[0], jnp.int32)
    hacc[...] = jnp.zeros_like(hacc)
    qacc[...] = jnp.zeros_like(qacc)
    cols[...] = jnp.zeros_like(cols)
    peers = views - 1
    for k in tile_steps:
        peers = peers + jnp.where(exists(k), 1, 0)
    pl.semaphore_wait(barrier, peers)
    send_margin = remote(mown, mlow, msem.at[0], msem.at[1], dev(tile_at(1), v))
    when_tile(1, send_margin.start)
    send_near = remote(
        vol.at[0, 0, :, pl.ds(height - REST_ROWS, REST_ROWS)], nrx, nsem.at[0], nsem.at[1], dev(tile_at(1), v)
    )
    when_tile(1, send_near.start)

    down_view, up_view, far_view = view_at(-1), view_at(1), view_at(2)
    raws = []
    for part, (first, end) in enumerate(((0, EARLY_ROWS), (EARLY_ROWS, RAW_CHUNKS * CHUNK))):
        for side, target in ((0, down_view), (1, up_view)):
            begin = first + PAD if part else first - side * PAD
            source = vol.at[0, 0, far_view, pl.ds(side * half + begin, end + PAD - begin)]
            landing = rawv.at[side, pl.ds(PAD + begin, end + PAD - begin)]
            raws.append(remote(source, landing, rawsem.at[0, 4 * part + side], rawsem.at[1, 4 * part + side], dev(t, target)))
        for side, target in ((0, down_view), (1, up_view)):
            sems = [rawsem.at[k, 4 * part + 2 + side] for k in range(2)]
            rows = pl.ds(side * half + first, end - first)
            raws.append(
                remote(grads.at[0, far_view, rows], rawg.at[side, pl.ds(first, end - first)], *sems, dev(t, target))
            )
    for raw in raws[:2]:
        raw.start()
    start = slab[0]
    aligned = lax.div(start, 8) * 8
    shift = jnp.full((SLAB + 8, width), start - aligned, jnp.int32)
    moves = [(k, lax.bitwise_and(shift, k) != 0) for k in (1, 2, 4)]
    for load in loads:
        load.wait()
    send_windows = []
    for z in range(depth):
        rows = vp[z, pl.ds(aligned + PAD, SLAB + 8), :]
        for k, moved in moves:
            rows = jnp.where(moved, pltpu.roll(rows, SLAB + 8 - k, 0), rows)
        wst[z, PAD : PAD + SLAB, :] = rows[:SLAB]
        sent = pl.ds(PAD, SENT_ROWS)
        send_windows.append(
            remote(wst.at[z, sent], wrx.at[z, sent], wsem.at[0, z], wsem.at[1, z], dev(tile_at(-1), v))
        )
        when_tile(-1, send_windows[z].start)
    for z in range(depth):
        vp[z, PAD - 1 : PAD, :] = 2.0 * vp[z, PAD : PAD + 1, :] - vp[z, PAD + 1 : PAD + 2, :]
        last = PAD + height - 1
        vp[z, last + 1 : last + 2, :] = 2.0 * vp[z, last : last + 1, :] - vp[z, last - 1 : last, :]

    def depth_gradients_of(src, dst, count):
        def body(r, _):
            r = pl.multiple_of(r * 8, 8)
            planes = [src[z, pl.ds(pl.multiple_of(PAD + r, 8), 8), :] for z in range(depth)]
            for z, g in enumerate(z_gradients(planes)):
                dst[0, z, pl.ds(r, 8), :] = g
            return 0

        lax.fori_loop(0, count // 8, body, 0)

    depth_gradients_of(vp, grads, height)

    for raw in raws[2:4]:
        raw.start()

    for z in range(depth):
        wst[z, PAD - 1 : PAD, :] = 2.0 * wst[z, PAD : PAD + 1, :] - wst[z, PAD + 1 : PAD + 2, :]
        last = PAD + SLAB - 1
        wst[z, last + 1 : last + 2, :] = 2.0 * wst[z, last : last + 1, :] - wst[z, last - 1 : last, :]

    def gradients_of(src, dst, first, end):
        def body(r, _):
            r = pl.multiple_of(r * 8, 8)
            planes = [src[z, pl.ds(PAD + r, 8), :] for z in range(depth)]
            for z in range(depth):
                before, after = src[z, pl.ds(r, 8), :], src[z, pl.ds(2 * PAD + r, 8), :]
                dst[1, z, pl.ds(r, 8), :] = y_gradient(before, planes[z], after)
                dst[2, z, pl.ds(r, 8), :] = x_gradient(planes[z])
            return 0

        lax.fori_loop(first // 8, end // 8, body, 0)

    depth_gradients_of(wst, wgrad, SLAB)
    gradients_of(wst, wgrad, 0, SLAB)

    zc = [(z + 0.5) / depth * 2.0 - 1.0 for z in range(depth)]

    def depth_sum(fields, power):
        return functools.reduce(lambda a, b: a + b, [f * (c**power) if power else f for f, c in zip(fields, zc)])

    sub = iota((8, 128), 0)
    lane8 = iota((8, 128), 1)

    def gradients_at(srcg, r, xs, mask):
        return [[srcg[k, z, pl.ds(r, 8), xs] * mask for z in range(depth)] for k in range(3)]

    def row_coordinate(r):
        return coordinate(sub + (r + height - SLAB), height)

    when_tile(-1, send_margin.wait_recv)
    low_rows = mlow[...]
    own_rows = mown[...]

    def matrix_lanes(xl, _):
        xs = pl.ds(pl.multiple_of(xl * 128, 128), 128)
        xv = coordinate(lane8 + xl * 128, width)

        def body(yb, carry):
            r = pl.multiple_of(yb * 8, 8)
            mask = jnp.where(sub + r < low_rows, 1.0, 0.0).astype(F32)
            g = gradients_at(wgrad, r, xs, mask)
            yv = row_coordinate(r)
            new = []
            for f, (a, b) in enumerate(PAIRS):
                fields = [g[a][z] * g[b][z] for z in range(depth)]
                p0, p1, p2 = (depth_sum(fields, k) for k in range(3))
                yp = yv * p0
                terms = (p2, yv * p1, p1, yv * yp, yp, p0)
                new += [c + term for c, term in zip(carry[6 * f : 6 * f + 6], terms)]
            return tuple(new)

        sums = lax.fori_loop(0, SLAB // 8, body, tuple(jnp.zeros((8, 128), F32) for _ in range(36)))
        for f in range(6):
            zz, zy, zo, yy, yo, oo = sums[6 * f : 6 * f + 6]
            xo = xv * oo
            for m, term in enumerate((zz, zy, xv * zo, zo, yy, xv * yo, yo, xv * xo, xo, oo)):
                hacc[f, m] += term
        return 0

    lax.fori_loop(0, lanes, matrix_lanes, 0)
    for f, (a, b) in enumerate(PAIRS):
        for m, (i, j) in enumerate(MONOS):
            row = jnp.sum(hacc[f, m], axis=0, keepdims=True)
            for p, q in {(4 * a + i, 4 * b + j), (4 * a + j, 4 * b + i), (4 * b + i, 4 * a + j), (4 * b + j, 4 * a + i)}:
                cols[p, q : q + 1, :] = row

    def moment(part, src, srcg, first, count, rows, near):
        def lane_block(xl, _):
            xs = pl.ds(pl.multiple_of(xl * 128, 128), 128)
            xv = coordinate(lane8 + xl * 128, width)

            def body(yb, carry):
                r = pl.multiple_of(yb * 8, 8)
                mask = jnp.where(sub + (r + first) < rows, 1.0, 0.0).astype(F32)
                g = gradients_at(srcg, pl.multiple_of(r + first, 8), xs, mask)
                window = [src[z, pl.ds(pl.multiple_of(PAD + first + r, 8), 8), xs] for z in range(depth)]
                residual = [near(z, r, xs) - window[z] for z in range(depth)]
                yv = row_coordinate(r + first)
                new = []
                for k in range(3):
                    fields = [g[k][z] * residual[z] for z in range(depth)]
                    p0, p1 = depth_sum(fields, 0), depth_sum(fields, 1)
                    new += [c + term for c, term in zip(carry[3 * k : 3 * k + 3], (p1, yv * p0, p0))]
                return tuple(new)

            sums = lax.fori_loop(0, count // 8, body, tuple(jnp.zeros((8, 128), F32) for _ in range(9)))
            for k in range(3):
                zo, yo, oo = sums[3 * k : 3 * k + 3]
                for j, term in enumerate((zo, yo, xv * oo, oo)):
                    qacc[part, 4 * k + j] += term
            return 0

        lax.fori_loop(0, lanes, lane_block, 0)
        for i in range(12):
            cols[12 + part, i : i + 1, :] = jnp.sum(qacc[part, i], axis=0, keepdims=True)

    row = iota((16, 128), 0)
    lane = iota((16, 128), 1)
    tile_index = row * 0 + t
    has_low, has_next = tile_index > 0, tile_index < tiles - 1
    block = jnp.zeros((16, 128), F32)

    def placed(block, c):
        total = jnp.sum(cols[c], axis=1, keepdims=True)
        return jnp.where((lane == c) & (has_next if c == 13 else has_low), total, block)

    for c in range(12):
        block = placed(block, c)
    when_tile(-1, send_near.wait_recv)
    moment(0, wst, wgrad, FIRST_ROWS, REST_ROWS, low_rows, lambda z, r, xs: nrx[z, pl.ds(r, 8), xs])
    for send_window in send_windows:
        when_tile(1, send_window.wait_recv)
    for z in range(depth):
        wrx[z, PAD - 1 : PAD, :] = 2.0 * wrx[z, PAD : PAD + 1, :] - wrx[z, PAD + 1 : PAD + 2, :]
    depth_gradients_of(wrx, wrx_grad, FIRST_ROWS)
    gradients_of(wrx, wrx_grad, 0, FIRST_ROWS)
    moment(1, wrx, wrx_grad, 0, FIRST_ROWS, own_rows, lambda z, r, xs: vp[z, pl.ds(PAD + height - SLAB + r, 8), xs])

    block = placed(block, 12)
    block = placed(block, 13)
    buf1[v] = block
    buf1[v, 13:14, :] = jnp.full((1, 128), gain[0, 0], F32)
    shares = [
        remote(buf1.at[v], buf1.at[v], s1.at[k - 1], r1.at[k - 1], dev(t, view_at(k))) for k in range(1, views)
    ]
    for share in shares:
        share.start()
    for raw in raws[4:]:
        raw.start()
    gradients_of(vp, grads, 0, half)
    for k, share in enumerate(shares):
        share.wait_recv()
    total = buf1[0]
    for k in range(1, views):
        total = total + buf1[k]
    buf2[2] = jnp.where(row < 12, total, 0.0)
    buf2[2, 12:13, 0:12] = start_affine[...]
    passes = [
        remote(buf2.at[2], buf2.at[2 - k], s2.at[i], r2.at[i], dev(tile_at(k), v)) for i, k in enumerate(tile_steps)
    ]
    for k, passed in zip(tile_steps, passes):
        when_tile(k, passed.start)
    gradients_of(vp, grads, half, height)
    across = coordinate(iota((8, width), 1), width)
    facing = 1.0 - 2.0 * lax.rem(v, 2).astype(F32)

    def plane_weights(z, _):
        xk[z, 3] = (0.2 + (1.0 + facing * across) * 0.5) * (gain[0, 0] * (1.5 + facing * coordinate(z, depth)))
        return 0

    lax.fori_loop(0, depth, plane_weights, 0)
    for side, plane, source in ((0, down_view, up_view), (1, up_view, down_view)):
        g = jnp.concatenate([jnp.broadcast_to(buf1[source, 13:14, :], (8, 128))] * lanes, axis=1)
        wraw[side] = (0.2 + (1.0 - facing * across) * 0.5) * (g * (1.5 - facing * coordinate(plane, depth)))

    zf = coordinate(v, depth)
    weights = jnp.zeros((8, width), F32)
    for k in range(views):
        s = 1.0 - 2.0 * (k % 2)
        g = jnp.concatenate([jnp.broadcast_to(buf1[k, 13:14, :], (8, 128))] * lanes, axis=1)
        weights = weights + g * (1.5 + s * zf) * (0.2 + (1.0 + s * across) * 0.5)
    inverse = 1.0 / weights

    for k, passed in zip(tile_steps, passes):
        when_tile(-k, passed.wait_recv)

    inside = (row < 12) & (lane < 12)
    blocks = [buf2[k] for k in range(5)]
    below2, below, here, above = [jnp.where(inside, blocks[k + 1], 0.0) for k in range(4)]
    eye = jnp.where((row == lane) & (row < 12), 1.0, 0.0).astype(F32)

    def column(a, k):
        return jnp.broadcast_to(a[:, k : k + 1], (16, 128))

    def lane_sum(a):
        return jnp.broadcast_to(jnp.sum(a, axis=1, keepdims=True), (16, 128))

    def as_row(col):
        return jnp.broadcast_to(jnp.sum(col * eye, axis=0, keepdims=True), (16, 128))

    q = [column(blocks[k + 1], 12) + column(blocks[k], 13) for k in range(4)]
    starts = [jnp.broadcast_to(blocks[k][12:13, :], (16, 128)) for k in range(5)]
    stiff = eye * (STIFFNESS_FACTOR * depth * SLAB * width * views)
    right_up = lane_sum(above * starts[4] + here * starts[2] + stiff * starts[3]) - q[3] + q[2]
    right_down = lane_sum(below * starts[2] + below2 * starts[0] + stiff * starts[1]) - q[1] + q[0]
    right_own = lane_sum(stiff * starts[2]) - q[2] + q[1]
    real = row < 12
    up = jnp.where((lane == 12) & real, right_up, above + here + stiff)
    down = jnp.where((lane == 12) & real, right_down, below + below2 + stiff)
    own = here + below + stiff + pltpu.roll(here, 12, 1) + pltpu.roll(below, 24, 1)
    own = jnp.where((lane == 36) & real, right_own, own)
    systems = [up, down, own]
    for k in range(12):
        for i in range(3):
            a = systems[i]
            col = column(a, k)
            scaled = jnp.broadcast_to(a[k : k + 1, :] / col[k : k + 1, :], (16, 128))
            systems[i] = jnp.where(row == k, scaled, a - col * scaled)
    up, down, own = systems
    first_up, first_down = as_row(column(up, 12)), as_row(column(down, 12))
    mix = pltpu.roll(first_up, 12, 1) + pltpu.roll(first_down, 24, 1) + jnp.where(lane == 36, 1.0, 0.0)
    params = lane_sum(own * mix)
    pcol[...] = params
    refined[...] = as_row(params)[0:1, 0:12]

    def entry(k, j):
        return jnp.broadcast_to(pcol[4 * k + j : 4 * k + j + 1, :], (8, 128))

    def entry_row(k, j):
        return jnp.concatenate([entry(k, j)] * lanes, axis=1)

    def tables(z, _):
        zf = coordinate(z, depth)
        for k in range(3):
            xk[z, k] = entry_row(k, 0) * zf + entry_row(k, 3) + entry_row(k, 2) * across
        return 0

    lax.fori_loop(0, depth, tables, 0)
    slopes = [entry_row(k, 1) for k in range(3)]
    sub_row = iota((8, width), 0)

    def numerator_rows(z, first, dst, dst_first, extra, scale):
        def body(rb, _):
            r = pl.multiple_of(first + rb * 8, 8)
            d = pl.multiple_of(dst_first + rb * 8, 8)
            yv = coordinate(sub_row + r, height)
            value = vp[z, pl.ds(pl.multiple_of(PAD + r, 8), 8), :]
            for k in range(3):
                value = value + grads[k, z, pl.ds(r, 8), :] * (xk[z, k] + slopes[k] * yv)
            value = value * xk[z, 3]
            for stream in extra:
                value = value + rcv[stream, pl.ds(d, 8), :]
            if scale is not None:
                value = value * scale
            dst(d, value)
            return 0

        lax.fori_loop(0, CHUNK // 8, body, 0)

    def hop(stream, c):
        rows = pl.ds(pl.multiple_of(c * CHUNK, CHUNK), CHUNK)
        target = down_view if stream % 2 == 0 else up_view
        return remote(
            snd.at[stream, rows], rcv.at[stream, rows], ssem.at[stream, c], rsem.at[stream, c], dev(t, target)
        )

    def send_chunk(stream, c, plane, upper, extra=()):
        def put(d, value):
            snd[stream, pl.ds(d, 8), :] = value

        c_row = pl.multiple_of(c * CHUNK, CHUNK)
        numerator_rows(plane, (half if upper else 0) + c_row, put, c_row, extra, None)
        hop(stream, c).start()

    def relay_raw(side, c):
        plane = (down_view, up_view)[side]
        stream = 4 + side
        c_row = pl.multiple_of(c * CHUNK, CHUNK)

        def body(rb, _):
            d = pl.multiple_of(c_row + rb * 8, 8)
            r = pl.multiple_of(side * half + d, 8)
            yv = coordinate(sub_row + r, height)
            shifts = [xk[plane, k] + slopes[k] * yv for k in range(3)]
            value = vp[plane, pl.ds(pl.multiple_of(PAD + r, 8), 8), :]
            for k in range(3):
                value = value + grads[k, plane, pl.ds(r, 8), :] * shifts[k]
            before, here_v, after = [rawv[side, pl.ds(pl.multiple_of(d + k * PAD, 8), 8), :] for k in range(3)]
            other = here_v + rawg[side, pl.ds(d, 8), :] * shifts[0]
            other = other + y_gradient(before, here_v, after) * shifts[1] + x_gradient(here_v) * shifts[2]
            snd[stream, pl.ds(d, 8), :] = value * xk[plane, 3] + other * wraw[side]
            return 0

        lax.fori_loop(0, CHUNK // 8, body, 0)
        hop(stream, c).start()

    def far(c, _):
        send_chunk(0, c, far_view, False)
        send_chunk(1, c, far_view, True)
        return 0

    def near_planes(c, _):
        send_chunk(2, c, down_view, True)
        send_chunk(3, c, up_view, False)
        return 0

    def relay(c, _):
        hop(0, c).wait_recv()
        send_chunk(4, c, down_view, False, (0,))
        hop(1, c).wait_recv()
        send_chunk(5, c, up_view, True, (1,))
        return 0

    def relay_both(c, _):
        relay_raw(0, c)
        relay_raw(1, c)
        return 0

    lax.fori_loop(RAW_CHUNKS, chunks, far, 0)
    lax.fori_loop(0, chunks, near_planes, 0)
    for raw in raws:
        raw.wait_recv()
    rawv[0, PAD - 1 : PAD, :] = 2.0 * rawv[0, PAD : PAD + 1, :] - rawv[0, PAD + 1 : PAD + 2, :]
    lax.fori_loop(0, RAW_CHUNKS, relay_both, 0)
    lax.fori_loop(RAW_CHUNKS, chunks, relay, 0)

    def finish(c, _):
        c_row = pl.multiple_of(c * CHUNK, CHUNK)
        for part, streams in ((0, (3, 4)), (1, (2, 5))):
            for stream in streams:
                hop(stream, c).wait_recv()

            def put(d, value, part=part):
                out[0, 0, pl.ds(pl.multiple_of(part * half + d, 8), 8), :] = value

            numerator_rows(v, part * half + c_row, put, c_row, streams, inverse)
        return 0

    lax.fori_loop(0, chunks, finish, 0)

    def drain(c, _):
        for stream in range(2, 6):
            hop(stream, c).wait_send()
        return 0

    def drain_far(c, _):
        hop(0, c).wait_send()
        hop(1, c).wait_send()
        return 0

    lax.fori_loop(0, chunks, drain, 0)
    lax.fori_loop(RAW_CHUNKS, chunks, drain_far, 0)
    when_tile(1, send_margin.wait_send)
    when_tile(1, send_near.wait_send)
    for send_window in send_windows:
        when_tile(-1, send_window.wait_send)
    for k, passed in zip(tile_steps, passes):
        when_tile(k, passed.wait_send)
    for copy in shares + raws:
        copy.wait_send()


def on_device(tiles, views, volumes, initial_affine, slab_start, margin_rows, view_gain):
    depth, height, width = volumes.shape[2:]
    half = height // 2
    chunks = half // CHUNK
    smem = pl.BlockSpec(memory_space=pltpu.SMEM)
    vmem = pl.BlockSpec(memory_space=pltpu.VMEM)
    dma = pltpu.SemaphoreType.DMA
    return pl.pallas_call(
        functools.partial(kernel, tiles, views),
        out_shape=(jax.ShapeDtypeStruct((1, 1, height, width), F32), jax.ShapeDtypeStruct((1, 12), F32)),
        in_specs=[pl.BlockSpec(memory_space=pltpu.HBM), pl.BlockSpec(memory_space=pltpu.HBM), smem, smem, smem],
        out_specs=(vmem, vmem),
        scratch_shapes=[
            pltpu.VMEM((depth, height + 2 * PAD, width), F32),
            pltpu.VMEM((3, depth, height, width), F32),
            pltpu.VMEM((depth, SLAB + 2 * PAD, width), F32),
            pltpu.VMEM((3, depth, SLAB, width), F32),
            pltpu.VMEM((depth, SENT_ROWS + PAD, width), F32),
            pltpu.VMEM((3, depth, FIRST_ROWS, width), F32),
            pltpu.VMEM((depth, REST_ROWS, width), F32),
            pltpu.VMEM((8, 128), jnp.int32),
            pltpu.VMEM((8, 128), jnp.int32),
            pltpu.VMEM((1, 12), F32),
            pltpu.VMEM((6, 10, 8, 128), F32),
            pltpu.VMEM((2, 12, 8, 128), F32),
            pltpu.VMEM((14, 16, 128), F32),
            pltpu.VMEM((views, 16, 128), F32),
            pltpu.VMEM((5, 16, 128), F32),
            pltpu.VMEM((16, 128), F32),
            pltpu.VMEM((depth, 4, 8, width), F32),
            pltpu.VMEM((6, half, width), F32),
            pltpu.VMEM((6, half, width), F32),
            pltpu.VMEM((2, RAW_CHUNKS * CHUNK + 2 * PAD, width), F32),
            pltpu.VMEM((2, RAW_CHUNKS * CHUNK, width), F32),
            pltpu.VMEM((2, 8, width), F32),
            dma((depth + 1,)), dma((2,)), dma((2, depth)), dma((2,)),
            dma((views - 1,)), dma((views - 1,)), dma((4,)), dma((4,)),
            dma((6, chunks)), dma((6, chunks)), dma((2, 8)),
        ],
        compiler_params=pltpu.CompilerParams(
            collective_id=0, has_side_effects=True, vmem_limit_bytes=52 * 1024 * 1024
        ),
        name="refine_and_join",
    )(
        pltpu.with_memory_space_constraint(volumes, pltpu.HBM),
        pltpu.with_memory_space_constraint(initial_affine, pltpu.HBM),
        slab_start,
        margin_rows,
        view_gain,
    )


def solution(mesh):
    placed = (
        P("tile", "view", None, None, None),
        P("tile", None),
        P("tile"),
        P("tile"),
        P("tile", "view"),
    )
    return jax.shard_map(
        functools.partial(on_device, mesh.shape["tile"], mesh.shape["view"]),
        mesh=mesh,
        in_specs=placed,
        out_specs=(P("tile", "view", None, None), P("tile", None)),
        check_vma=False,
    )
```
